32 devices in a mesh: groups: 2 (over y), row: 4 (over z), col: 4 (over x, core).
Axes of the slice: x: 2, y: 2, z: 4, core: 2. Of those that a mesh axis runs over, the one named last changes fastest.
Arguments:
- right_side: float32 [128, 8192], P('groups', ('row', 'col')), parts along dimension 0, may hold values from -6 to 6
- prior: float32 [8192], P(('row', 'col')), may hold values from 0.5 to 2
- blocks: bfloat16 [1024, 128, 128], P(('row', 'col')), may hold values from -0.125 to 0.125
- block_row: int32 [1024], P(('row', 'col')), may hold values from 0 to 63, as said below
- block_col: int32 [1024], P(('row', 'col')), may hold values from 0 to 63, as said below
Outputs:
- solution_field: float32 [128, 8192], P('groups', ('row', 'col')), parts along dimension 0
- residual: float32 [128, 8192], P('groups', ('row', 'col')), parts along dimension 0
The draws below stay inside these ranges and needn't reach their ends.
There are 2 independent parts, one for each index of `groups`. The reference program is written for one: setup_inputs(seed, part) draws one part's arguments, and reference() takes and returns one part's arrays. A program takes and returns all parts, laid end to end along the dimension named above; an argument that names none is the same for every part. Nothing has to cross between parts.
Inputs may be any that keep to these rules, and one draw needn't show every extreme that they name: `block_row`: stored blocks k*64 to (k+1)*64 - 1 belong to device k of row+col, k = r*4+c; their block rows lie in r*16 to (r+1)*16 - 1. `block_col`: the block columns b of device (r, c) satisfy (b // 4) % 4 == c.
All inputs are finite; a program needn't handle non-finite values.
Results may differ from the reference program's by a relative error of at most 0.0069.
Values may be sent and summed in bfloat16 or wider, within the bound.
No kernel may reach another device: no remote copies, remote signals or barrier semaphores. Data moves between devices by JAX's collectives and lax.ppermute only.
A program may use at most 64 MiB of HBM per device.

```python
import math
import jax
import jax.numpy as jnp
from jax import lax

BLOCK = 128
FRAMES = 64
CB = 4
KB = 64
ITERS = 2
GRID_ROWS = 4
GRID_COLS = 4
ROWBLK = 16
NBLK = 64
NPIX = 8192
NNZ = 1024


def draw_block_row(key, part):
    device = jnp.arange(NNZ, dtype=jnp.int32) // KB
    position = jnp.arange(NNZ, dtype=jnp.int32) % KB
    grid_row = device // GRID_COLS
    offset_row = jax.random.randint(jax.random.fold_in(key, 11), (NNZ,), 0, ROWBLK, dtype=jnp.int32)
    offset_row = jnp.where(position == 0, 0, offset_row)
    offset_row = jnp.where(position == KB - 1, ROWBLK - 1, offset_row)
    return (grid_row * ROWBLK + offset_row).astype(jnp.int32)


def draw_block_col(key, part):
    key_stretch, key_inner = jax.random.split(jax.random.fold_in(key, 23))
    device = jnp.arange(NNZ, dtype=jnp.int32) // KB
    position = jnp.arange(NNZ, dtype=jnp.int32) % KB
    grid_col = device % GRID_COLS
    stretch_row = jax.random.randint(key_stretch, (NNZ,), 0, GRID_ROWS, dtype=jnp.int32)
    inner = jax.random.randint(key_inner, (NNZ,), 0, CB, dtype=jnp.int32)
    stretch_row = jnp.where(position == 0, 0, stretch_row)
    inner = jnp.where(position == 0, 0, inner)
    stretch_row = jnp.where(position == KB - 1, GRID_ROWS - 1, stretch_row)
    inner = jnp.where(position == KB - 1, CB - 1, inner)
    return ((stretch_row * GRID_COLS + grid_col) * CB + inner).astype(jnp.int32)


def block_scale(own_key, shape, cuts, low, high):
    factor_of = 1.0
    for axis_at, shards_of in cuts:
        heights = jax.random.uniform(jax.random.fold_in(jax.random.fold_in(own_key, 6), axis_at), (shards_of,), jnp.float32, low / len(cuts), high / len(cuts))
        factor_of = factor_of * jnp.repeat(jnp.exp(heights), shape[axis_at] // shards_of).reshape((-1,) + (1,) * (len(shape) - 1 - axis_at))
    return factor_of


def bell_draw(own_key, shape, scale, bound, pieces=(), kind=jnp.bfloat16):
    values = scale * jax.random.normal(own_key, shape, jnp.float32)
    if pieces:
        values = values * block_scale(own_key, shape, pieces, -0.22, 0.18)
    return jnp.clip(values, -bound, bound).astype(kind)


def setup_inputs(seed: int = 0, part: int = 0) -> dict:
    arg_keys = jax.random.split(jax.random.key(seed), 6)
    part_splits = jax.random.split(jax.random.fold_in(arg_keys[5], part), 6)
    return {
        "right_side": bell_draw(part_splits[0], (FRAMES, NPIX), 1.0, 6.0, ((1, 16),), jnp.float32),
        "prior": jnp.clip(jnp.exp(math.log(2.0) - 1.3862944 * jax.random.uniform(arg_keys[1], (NPIX,), jnp.float32) ** block_scale(arg_keys[1], (NPIX,), ((0, 16),), -0.2, 0.2)), 0.5, 2.0),
        "blocks": bell_draw(arg_keys[2], (NNZ, BLOCK, BLOCK), (KB // CB * BLOCK) ** -0.5, 0.125, ((0, 16),)),
        "block_row": draw_block_row(jax.random.fold_in(arg_keys[5], 71), part),
        "block_col": draw_block_col(jax.random.fold_in(arg_keys[5], 71), part),
    }


def spd_solve(matrix, rhs):
    factor = jnp.linalg.cholesky(matrix)
    half_solved = lax.linalg.triangular_solve(factor, rhs, left_side=True, lower=True)
    return lax.linalg.triangular_solve(factor, half_solved, left_side=True, lower=True, transpose_a=True)

def pair_gram(left, right):
    return lax.dot_general(left.astype(jnp.float32), right.astype(jnp.float32), (((1,), (1,)), ((), ())), precision=lax.Precision.HIGHEST, preferred_element_type=jnp.float32)

def apply_left(coeffs, panel):
    return jnp.dot(coeffs.astype(jnp.float32), panel.astype(jnp.float32), precision=lax.Precision.HIGHEST, preferred_element_type=jnp.float32)

def operator(grouped, prior, direction):
    search = direction.astype(jnp.bfloat16).astype(jnp.float32)
    panel_view = search.reshape(FRAMES, NBLK, BLOCK)

    def forward_step(total, stacked):
        tile_set, row_ids, col_ids = stacked
        picked = jnp.take(panel_view, col_ids, axis=1)
        contrib = jnp.einsum('fkj,kij->kfi', picked, tile_set.astype(jnp.float32), precision=lax.Precision.HIGHEST)
        return (total.at[row_ids].add(contrib), None)
    total, _ = lax.scan(forward_step, jnp.zeros((NBLK, FRAMES, BLOCK), jnp.float32), grouped)
    footprint = total.transpose(1, 0, 2).reshape(FRAMES, NPIX).astype(jnp.bfloat16).astype(jnp.float32)
    foot_view = footprint.reshape(FRAMES, NBLK, BLOCK)

    def backward_step(total, stacked):
        tile_set, row_ids, col_ids = stacked
        picked = jnp.take(foot_view, row_ids, axis=1)
        contrib = jnp.einsum('fki,kij->kfj', picked, tile_set.astype(jnp.float32), precision=lax.Precision.HIGHEST)
        return (total.at[col_ids].add(contrib), None)
    total, _ = lax.scan(backward_step, jnp.zeros((NBLK, FRAMES, BLOCK), jnp.float32), grouped)
    return total.transpose(1, 0, 2).reshape(FRAMES, NPIX) + prior[None, :] * direction

def reference(right_side, prior, blocks, block_row, block_col):
    devices = GRID_ROWS * GRID_COLS
    grouped = (blocks.reshape(devices, KB, BLOCK, BLOCK), block_row.reshape(devices, KB).astype(jnp.int32), block_col.reshape(devices, KB).astype(jnp.int32))
    solution = jnp.zeros_like(right_side)
    residual = right_side
    direction = right_side
    gram = pair_gram(residual, residual)
    for iteration in range(ITERS):
        image = operator(grouped, prior, direction)
        curvature = pair_gram(direction, image)
        step_alpha = spd_solve(curvature, gram)
        solution = solution + apply_left(step_alpha.T, direction)
        residual = residual - apply_left(step_alpha.T, image)
        if iteration + 1 < ITERS:
            new_gram = pair_gram(residual, residual)
            step_beta = spd_solve(gram, new_gram)
            direction = residual + apply_left(step_beta.T, direction)
            gram = new_gram
    return (solution, residual)
```

```python
import jax
import jax.numpy as jnp
from jax import lax
from jax.experimental import pallas as pl
from jax.experimental.pallas import tpu as pltpu
from jax.sharding import PartitionSpec as P

BLOCK = 128
FP32 = lax.Precision.HIGHEST
VMEM = pl.BlockSpec(memory_space=pltpu.VMEM)
SMEM = pl.BlockSpec(memory_space=pltpu.SMEM)
PARAMS = pltpu.CompilerParams(vmem_limit_bytes=48 * 1024 * 1024)


def nt_dot(a, b, precision=None):
    return lax.dot_general(
        a, b, (((1,), (1,)), ((), ())), precision=precision, preferred_element_type=jnp.float32
    )


def tn_dot(a, b):
    return lax.dot_general(
        a, b, (((0,), (0,)), ((), ())), precision=FP32, preferred_element_type=jnp.float32
    )


def nn_dot(a, b):
    return lax.dot_general(
        a, b, (((1,), (0,)), ((), ())), precision=FP32, preferred_element_type=jnp.float32
    )


def call(kernel, outs, ins, scratch=()):
    return pl.pallas_call(
        kernel,
        out_shape=outs,
        in_specs=[SMEM if x.dtype == jnp.int32 else VMEM for x in ins],
        out_specs=jax.tree.map(lambda _: VMEM, outs),
        scratch_shapes=list(scratch),
        compiler_params=PARAMS,
    )(*ins)


def store_split(out_ref, at, value):
    high = value.astype(jnp.bfloat16)
    low = (value - high.astype(jnp.float32)).astype(jnp.bfloat16)
    for dest in range(out_ref.shape[0]):
        out_ref[dest, at] = high
        out_ref[dest, at + 1] = low


def load_split(in_ref, at):
    total = None
    for source in range(in_ref.shape[0]):
        part = in_ref[source, at].astype(jnp.float32) + in_ref[source, at + 1].astype(jnp.float32)
        total = part if total is None else total + part
    return total


def load_sum(in_ref, at):
    total = in_ref[0, at].astype(jnp.float32)
    for source in range(1, in_ref.shape[0]):
        total += in_ref[source, at].astype(jnp.float32)
    return total


def lanes(j):
    return slice(j * BLOCK, (j + 1) * BLOCK)


def cast_kernel(v_ref, out_ref):
    for j in range(out_ref.shape[0]):
        out_ref[j] = v_ref[:, lanes(j)].astype(jnp.bfloat16)


def forward_kernel(row_span, stretch, brow, bcol, search, blocks, v_ref, prior, out_ref, acc):
    acc[...] = jnp.zeros_like(acc)
    for k in range(blocks.shape[0]):
        at_row = lax.rem(brow[k], row_span)
        at_col = lax.div(bcol[k], row_span) * stretch + lax.rem(bcol[k], stretch)
        acc[at_row] += nt_dot(search[at_col], blocks[k])
    for dest in range(out_ref.shape[0]):
        for j in range(stretch):
            out_ref[dest, j] = acc[dest * stretch + j].astype(jnp.bfloat16)
    value = v_ref[...]
    both = jnp.concatenate([value, value * prior[...]], axis=0)
    store_split(out_ref, stretch, nt_dot(value, both, FP32))


def foot_kernel(in_ref, foot_ref, gram_ref):
    stretch = foot_ref.shape[0]
    for j in range(stretch):
        foot_ref[j] = load_sum(in_ref, j).astype(jnp.bfloat16)
    gram_ref[...] = load_split(in_ref, stretch)


def backward_kernel(row_span, stretch, brow, bcol, foot, blocks, gram, out_ref, acc):
    acc[...] = jnp.zeros_like(acc)
    for k in range(blocks.shape[0]):
        at_row = lax.rem(brow[k], row_span)
        at_col = lax.div(bcol[k], row_span) * stretch + lax.rem(bcol[k], stretch)
        acc[at_col] += jnp.dot(foot[at_row], blocks[k], preferred_element_type=jnp.float32)
    for dest in range(out_ref.shape[0]):
        for j in range(stretch):
            out_ref[dest, j] = acc[dest * stretch + j].astype(jnp.bfloat16)
    whole = jnp.concatenate([foot[b] for b in range(row_span)], axis=1)
    padded = jnp.concatenate([jnp.zeros_like(whole), whole], axis=0)
    store_split(out_ref, stretch, gram[...] + nt_dot(whole, padded))


def frame_scale(gram):
    n = gram.shape[0]
    same = lax.broadcasted_iota(jnp.int32, (n, n), 0) == lax.broadcasted_iota(jnp.int32, (n, n), 1)
    norm = jnp.where(same, gram[:, :n], 0.0)
    energy = jnp.where(same, gram[:, n:], 0.0)
    column = jnp.sum(energy, axis=1, keepdims=True) / jnp.sum(norm, axis=1, keepdims=True)
    row = jnp.sum(energy, axis=0, keepdims=True) / jnp.sum(norm, axis=0, keepdims=True)
    return column, row


def image_kernel(in_ref, v_ref, prior, image_ref, next_ref, cast_ref, gram_ref):
    stretch = cast_ref.shape[0]
    gram = load_split(in_ref, stretch)
    gram_ref[...] = gram
    scale, _ = frame_scale(gram)
    for j in range(stretch):
        value = v_ref[:, lanes(j)]
        image = load_sum(in_ref, j) + prior[:, lanes(j)] * value
        following = image - scale * value
        image_ref[:, lanes(j)] = image
        next_ref[:, lanes(j)] = following
        cast_ref[j] = following.astype(jnp.bfloat16)


def eliminate(work, n):
    at = lax.broadcasted_iota(jnp.int32, (n, 1), 0)
    for k in range(n):
        pivot_row = work[k : k + 1, :] / work[k : k + 1, k : k + 1]
        column = jnp.where(at == k, 0.0, work[:, k : k + 1])
        work = jnp.where(at == k, pivot_row, work - column * pivot_row)
    return work[:, n:]


def inverse_kernel(gram, out_ref):
    n = gram.shape[0]
    eye = lax.broadcasted_iota(jnp.int32, (n, n), 0) == lax.broadcasted_iota(jnp.int32, (n, n), 1)
    out_ref[...] = eliminate(
        jnp.concatenate([gram[:, n:], jnp.where(eye, 1.0, 0.0)], axis=1), n
    )


def final_kernel(in_ref, v_ref, image_ref, next_ref, prior, gram_ref, inverse_ref, x_ref, r_ref):
    n = gram_ref.shape[0]
    stretch = in_ref.shape[1] - 2
    gram = gram_ref[...]
    norm, energy = gram[:, :n], gram[:, n:]
    scale, scale_row = frame_scale(gram)
    second = load_split(in_ref, stretch)
    next_norm, next_energy = second[:, :n], second[:, n:]
    next_rhs = energy - scale * norm
    cross = next_norm + next_rhs * scale_row
    inverse = inverse_ref[...]
    alpha = nn_dot(inverse, norm)
    conj = nn_dot(inverse, cross.T)
    schur = next_energy - nn_dot(cross, conj)
    rhs = next_rhs - nn_dot(cross, alpha)
    gamma = eliminate(jnp.concatenate([schur, rhs], axis=1), n)
    first = alpha - nn_dot(conj, gamma)
    coeffs = jnp.concatenate([first, gamma], axis=0)
    for j in range(stretch):
        value = v_ref[:, lanes(j)]
        following = next_ref[:, lanes(j)]
        second_image = load_sum(in_ref, j) + prior[:, lanes(j)] * following
        x_ref[:, lanes(j)] = tn_dot(coeffs, jnp.concatenate([value, following], axis=0))
        r_ref[:, lanes(j)] = value - tn_dot(
            coeffs, jnp.concatenate([image_ref[:, lanes(j)], second_image], axis=0)
        )


def gather(x, axis):
    return lax.all_gather(x, axis, axis=0, tiled=True)


def exchange(x, axis):
    return lax.all_to_all(x, axis, split_axis=0, concat_axis=0, tiled=True)


def shards(right_side, prior, blocks, block_row, block_col):
    frames, pix = right_side.shape
    stretch = pix // BLOCK
    rows, cols = lax.axis_size("row"), lax.axis_size("col")
    row_span, col_span = stretch * cols, stretch * rows
    prior = prior.reshape(1, pix)
    f32, bf16 = jnp.float32, jnp.bfloat16

    def shape(dims, dtype):
        return jax.ShapeDtypeStruct(dims, dtype)

    panel = shape((stretch, frames, BLOCK), bf16)
    gram_type = shape((frames, 2 * frames), f32)
    own = shape((frames, pix), f32)

    def apply_operator(own_value, own_cast):
        search = gather(own_cast, "row")
        partial = call(
            lambda *refs: forward_kernel(row_span, stretch, *refs),
            shape((cols, stretch + 2, frames, BLOCK), bf16),
            (block_row, block_col, search, blocks, own_value, prior),
            [pltpu.VMEM((row_span, frames, BLOCK), f32)],
        )
        foot, gram = call(foot_kernel, (panel, gram_type), (exchange(partial, "col"),))
        foot = gather(foot, "col")
        partial = call(
            lambda *refs: backward_kernel(row_span, stretch, *refs),
            shape((rows, stretch + 2, frames, BLOCK), bf16),
            (block_row, block_col, foot, blocks, gram),
            [pltpu.VMEM((col_span, frames, BLOCK), f32)],
        )
        return exchange(partial, "row")

    cast = call(cast_kernel, panel, (right_side,))
    received = apply_operator(right_side, cast)
    image, following, cast, gram = call(
        image_kernel, (own, own, panel, gram_type), (received, right_side, prior)
    )
    inverse = call(inverse_kernel, shape((frames, frames), f32), (gram,))
    received = apply_operator(following, cast)
    return call(
        final_kernel,
        (own, own),
        (received, right_side, image, following, prior, gram, inverse),
    )


def solution(mesh):
    return jax.shard_map(
        shards,
        mesh=mesh,
        in_specs=(
            P("groups", ("row", "col")),
            P(("row", "col")),
            P(("row", "col"), None, None),
            P(("row", "col")),
            P(("row", "col")),
        ),
        out_specs=(P("groups", ("row", "col")), P("groups", ("row", "col"))),
        check_vma=False,
    )
```

```python
import jax
import jax.numpy as jnp
from jax import lax
from jax.experimental import pallas as pl
from jax.experimental.pallas import tpu as pltpu
from jax.sharding import PartitionSpec as P

BLOCK = 128
FP32 = lax.Precision.HIGHEST
VMEM = pl.BlockSpec(memory_space=pltpu.VMEM)
SMEM = pl.BlockSpec(memory_space=pltpu.SMEM)
PARAMS = pltpu.CompilerParams(vmem_limit_bytes=48 * 1024 * 1024)


def nt_dot(a, b, precision=None):
    return lax.dot_general(
        a, b, (((1,), (1,)), ((), ())), precision=precision, preferred_element_type=jnp.float32
    )


def tn_dot(a, b):
    return lax.dot_general(
        a, b, (((0,), (0,)), ((), ())), precision=FP32, preferred_element_type=jnp.float32
    )


def nn_dot(a, b):
    return lax.dot_general(
        a, b, (((1,), (0,)), ((), ())), precision=FP32, preferred_element_type=jnp.float32
    )


def call(kernel, outs, ins, scratch=()):
    flat_ins, ins_tree = jax.tree.flatten(tuple(ins))
    flat_outs, outs_tree = jax.tree.flatten(outs if isinstance(outs, tuple) else (outs,))

    def body(*refs):
        middle, last = len(flat_ins), len(flat_ins) + len(flat_outs)
        kernel(
            *jax.tree.unflatten(ins_tree, refs[:middle]),
            *jax.tree.unflatten(outs_tree, refs[middle:last]),
            *refs[last:],
        )

    results = pl.pallas_call(
        body,
        out_shape=flat_outs,
        in_specs=[SMEM if x.dtype == jnp.int32 else VMEM for x in flat_ins],
        out_specs=[VMEM for _ in flat_outs],
        scratch_shapes=list(scratch),
        compiler_params=PARAMS,
    )(*flat_ins)
    results = jax.tree.unflatten(outs_tree, results)
    return results if isinstance(outs, tuple) else results[0]


def store_split(out_refs, at, value):
    high = value.astype(jnp.bfloat16)
    low = (value - high.astype(jnp.float32)).astype(jnp.bfloat16)
    for out_ref in out_refs:
        out_ref[at] = high
        out_ref[at + 1] = low


def load_sum(in_refs, at):
    total = in_refs[0][at].astype(jnp.float32)
    for in_ref in in_refs[1:]:
        total += in_ref[at].astype(jnp.float32)
    return total


def load_split(in_refs, at):
    return load_sum(in_refs, at) + load_sum(in_refs, at + 1)


def fill_panel(panel, in_refs, axis):
    count, stretch = len(in_refs), in_refs[0].shape[0]
    me = lax.axis_index(axis)
    for shift, in_ref in enumerate(in_refs):
        source = lax.rem(me - shift + count, count)
        for j in range(stretch):
            panel[source * stretch + j] = in_ref[j]


def spread(out_refs, acc, axis, stretch):
    count = len(out_refs)
    me = lax.axis_index(axis)
    for shift, out_ref in enumerate(out_refs):
        dest = lax.rem(me + shift, count)
        for j in range(stretch):
            out_ref[j] = acc[dest * stretch + j].astype(jnp.bfloat16)


def lanes(j):
    return slice(j * BLOCK, (j + 1) * BLOCK)


def cast_kernel(v_ref, out_ref):
    for j in range(out_ref.shape[0]):
        out_ref[j] = v_ref[:, lanes(j)].astype(jnp.bfloat16)


def forward_kernel(row_span, stretch, brow, bcol, search, blocks, v_ref, prior, out_refs, acc, panel):
    acc[...] = jnp.zeros_like(acc)
    fill_panel(panel, search, "row")
    for k in range(blocks.shape[0]):
        at_row = lax.rem(brow[k], row_span)
        at_col = lax.div(bcol[k], row_span) * stretch + lax.rem(bcol[k], stretch)
        acc[at_row] += nt_dot(panel[at_col], blocks[k])
    spread(out_refs, acc, "col", stretch)
    value = v_ref[...]
    both = jnp.concatenate([value, value * prior[...]], axis=0)
    store_split(out_refs, stretch, nt_dot(value, both, FP32))


def foot_kernel(in_ref, foot_ref, gram_ref):
    stretch = foot_ref.shape[0]
    for j in range(stretch):
        foot_ref[j] = load_sum(in_ref, j).astype(jnp.bfloat16)
    gram_ref[...] = load_split(in_ref, stretch)


def backward_kernel(row_span, stretch, brow, bcol, foot, blocks, gram, out_refs, acc, panel):
    acc[...] = jnp.zeros_like(acc)
    fill_panel(panel, foot, "col")
    for k in range(blocks.shape[0]):
        at_row = lax.rem(brow[k], row_span)
        at_col = lax.div(bcol[k], row_span) * stretch + lax.rem(bcol[k], stretch)
        acc[at_col] += jnp.dot(panel[at_row], blocks[k], preferred_element_type=jnp.float32)
    spread(out_refs, acc, "row", stretch)
    whole = jnp.concatenate([panel[b] for b in range(row_span)], axis=1)
    padded = jnp.concatenate([jnp.zeros_like(whole), whole], axis=0)
    store_split(out_refs, stretch, gram[...] + nt_dot(whole, padded))


def frame_scale(gram):
    n = gram.shape[0]
    same = lax.broadcasted_iota(jnp.int32, (n, n), 0) == lax.broadcasted_iota(jnp.int32, (n, n), 1)
    norm = jnp.where(same, gram[:, :n], 0.0)
    energy = jnp.where(same, gram[:, n:], 0.0)
    column = jnp.sum(energy, axis=1, keepdims=True) / jnp.sum(norm, axis=1, keepdims=True)
    row = jnp.sum(energy, axis=0, keepdims=True) / jnp.sum(norm, axis=0, keepdims=True)
    return 1.25 * column, 1.25 * row


def image_kernel(in_ref, v_ref, prior, image_ref, next_ref, cast_ref, gram_ref):
    stretch = cast_ref.shape[0]
    gram = load_split(in_ref, stretch)
    gram_ref[...] = gram
    scale, _ = frame_scale(gram)
    for j in range(stretch):
        value = v_ref[:, lanes(j)]
        image = load_sum(in_ref, j) + prior[:, lanes(j)] * value
        following = image - scale * value
        image_ref[:, lanes(j)] = image
        next_ref[:, lanes(j)] = following
        cast_ref[j] = following.astype(jnp.bfloat16)


def eliminate(work, n):
    at = lax.broadcasted_iota(jnp.int32, (n, 1), 0)
    for k in range(n):
        pivot_row = work[k : k + 1, :] / work[k : k + 1, k : k + 1]
        column = jnp.where(at == k, 0.0, work[:, k : k + 1])
        work = jnp.where(at == k, pivot_row, work - column * pivot_row)
    return work[:, n:]


def inverse_kernel(gram, out_ref):
    n = gram.shape[0]
    eye = lax.broadcasted_iota(jnp.int32, (n, n), 0) == lax.broadcasted_iota(jnp.int32, (n, n), 1)
    out_ref[...] = eliminate(
        jnp.concatenate([gram[:, n:], jnp.where(eye, 1.0, 0.0)], axis=1), n
    )


def final_kernel(in_ref, v_ref, image_ref, next_ref, prior, gram_ref, inverse_ref, x_ref, r_ref):
    n = gram_ref.shape[0]
    stretch = in_ref[0].shape[0] - 2
    gram = gram_ref[...]
    norm, energy = gram[:, :n], gram[:, n:]
    scale, scale_row = frame_scale(gram)
    second = load_split(in_ref, stretch)
    next_norm, next_energy = second[:, :n], second[:, n:]
    next_rhs = energy - scale * norm
    cross = next_norm + next_rhs * scale_row
    inverse = inverse_ref[...]
    alpha = nn_dot(inverse, norm)
    conj = nn_dot(inverse, cross.T)
    schur = next_energy - nn_dot(cross, conj)
    rhs = next_rhs - nn_dot(cross, alpha)
    gamma = eliminate(jnp.concatenate([schur, rhs], axis=1), n)
    first = alpha - nn_dot(conj, gamma)
    coeffs = jnp.concatenate([first, gamma], axis=0)
    for j in range(stretch):
        value = v_ref[:, lanes(j)]
        following = next_ref[:, lanes(j)]
        second_image = load_sum(in_ref, j) + prior[:, lanes(j)] * following
        x_ref[:, lanes(j)] = tn_dot(coeffs, jnp.concatenate([value, following], axis=0))
        r_ref[:, lanes(j)] = value - tn_dot(
            coeffs, jnp.concatenate([image_ref[:, lanes(j)], second_image], axis=0)
        )


def shifted(x, axis, shift):
    count = lax.axis_size(axis)
    return lax.ppermute(x, axis, [(i, (i + shift) % count) for i in range(count)])


def gather(x, axis):
    return tuple([x] + [shifted(x, axis, s) for s in range(1, lax.axis_size(axis))])


def exchange(parts, axis):
    return tuple([parts[0]] + [shifted(x, axis, s) for s, x in enumerate(parts) if s])


def shards(right_side, prior, blocks, block_row, block_col):
    frames, pix = right_side.shape
    stretch = pix // BLOCK
    rows, cols = lax.axis_size("row"), lax.axis_size("col")
    row_span, col_span = stretch * cols, stretch * rows
    prior = prior.reshape(1, pix)
    f32, bf16 = jnp.float32, jnp.bfloat16

    def shape(dims, dtype):
        return jax.ShapeDtypeStruct(dims, dtype)

    panel = shape((stretch, frames, BLOCK), bf16)
    gram_type = shape((frames, 2 * frames), f32)
    own = shape((frames, pix), f32)

    def apply_operator(own_value, own_cast):
        search = gather(own_cast, "row")
        (partial,) = call(
            lambda *refs: forward_kernel(row_span, stretch, *refs),
            ((shape((stretch + 2, frames, BLOCK), bf16),) * cols,),
            (block_row, block_col, search, blocks, own_value, prior),
            [pltpu.VMEM((row_span, frames, BLOCK), f32), pltpu.VMEM((col_span, frames, BLOCK), bf16)],
        )
        foot, gram = call(foot_kernel, (panel, gram_type), (exchange(partial, "col"),))
        foot = gather(foot, "col")
        (partial,) = call(
            lambda *refs: backward_kernel(row_span, stretch, *refs),
            ((shape((stretch + 2, frames, BLOCK), bf16),) * rows,),
            (block_row, block_col, foot, blocks, gram),
            [pltpu.VMEM((col_span, frames, BLOCK), f32), pltpu.VMEM((row_span, frames, BLOCK), bf16)],
        )
        return exchange(partial, "row")

    cast = call(cast_kernel, panel, (right_side,))
    received = apply_operator(right_side, cast)
    image, following, cast, gram = call(
        image_kernel, (own, own, panel, gram_type), (received, right_side, prior)
    )
    inverse = call(inverse_kernel, shape((frames, frames), f32), (gram,))
    received = apply_operator(following, cast)
    return call(
        final_kernel,
        (own, own),
        (received, right_side, image, following, prior, gram, inverse),
    )


def solution(mesh):
    return jax.shard_map(
        shards,
        mesh=mesh,
        in_specs=(
            P("groups", ("row", "col")),
            P(("row", "col")),
            P(("row", "col"), None, None),
            P(("row", "col")),
            P(("row", "col")),
        ),
        out_specs=(P("groups", ("row", "col")), P("groups", ("row", "col"))),
        check_vma=False,
    )
```

```python
import jax
import jax.numpy as jnp
from jax import lax
from jax.experimental import pallas as pl
from jax.experimental.pallas import tpu as pltpu
from jax.sharding import PartitionSpec as P

BLOCK = 128
FP32 = lax.Precision.HIGHEST
VMEM = pl.BlockSpec(memory_space=pltpu.VMEM)
SMEM = pl.BlockSpec(memory_space=pltpu.SMEM)
PARAMS = pltpu.CompilerParams(vmem_limit_bytes=48 * 1024 * 1024)


def nt_dot(a, b, precision=None):
    return lax.dot_general(
        a, b, (((1,), (1,)), ((), ())), precision=precision, preferred_element_type=jnp.float32
    )


def tn_dot(a, b):
    return lax.dot_general(
        a, b, (((0,), (0,)), ((), ())), precision=FP32, preferred_element_type=jnp.float32
    )


def nn_dot(a, b):
    return lax.dot_general(
        a, b, (((1,), (0,)), ((), ())), precision=FP32, preferred_element_type=jnp.float32
    )


def call(kernel, outs, ins, scratch=()):
    flat_ins, ins_tree = jax.tree.flatten(tuple(ins))
    flat_outs, outs_tree = jax.tree.flatten(outs if isinstance(outs, tuple) else (outs,))

    def body(*refs):
        middle, last = len(flat_ins), len(flat_ins) + len(flat_outs)
        kernel(
            *jax.tree.unflatten(ins_tree, refs[:middle]),
            *jax.tree.unflatten(outs_tree, refs[middle:last]),
            *refs[last:],
        )

    results = pl.pallas_call(
        body,
        out_shape=flat_outs,
        in_specs=[SMEM if x.dtype == jnp.int32 else VMEM for x in flat_ins],
        out_specs=[VMEM for _ in flat_outs],
        scratch_shapes=list(scratch),
        compiler_params=PARAMS,
    )(*flat_ins)
    results = jax.tree.unflatten(outs_tree, results)
    return results if isinstance(outs, tuple) else results[0]


def store_split(out_refs, at, value):
    high = value.astype(jnp.bfloat16)
    low = (value - high.astype(jnp.float32)).astype(jnp.bfloat16)
    for out_ref in out_refs:
        out_ref[at] = high
        out_ref[at + 1] = low


def load_sum(in_refs, at):
    total = in_refs[0][at].astype(jnp.float32)
    for in_ref in in_refs[1:]:
        total += in_ref[at].astype(jnp.float32)
    return total


def load_split(in_refs, at):
    return load_sum(in_refs, at) + load_sum(in_refs, at + 1)


def fill_panel(panel, in_refs, axis):
    stretch = in_refs[0].shape[0]
    me = lax.axis_index(axis)
    for flip, in_ref in enumerate(in_refs):
        source = lax.bitwise_xor(me, flip)
        for j in range(stretch):
            panel[source * stretch + j] = in_ref[j]


def spread(out_refs, acc, axis, stretch):
    me = lax.axis_index(axis)
    for flip, out_ref in enumerate(out_refs):
        dest = lax.bitwise_xor(me, flip)
        for j in range(stretch):
            out_ref[j] = acc[dest * stretch + j].astype(jnp.bfloat16)


def lanes(j):
    return slice(j * BLOCK, (j + 1) * BLOCK)


def cast_kernel(v_ref, out_ref):
    for j in range(out_ref.shape[0]):
        out_ref[j] = v_ref[:, lanes(j)].astype(jnp.bfloat16)


def forward_kernel(row_span, stretch, brow, bcol, search, blocks, v_ref, prior, out_refs, acc, panel):
    acc[...] = jnp.zeros_like(acc)
    fill_panel(panel, search, "row")
    for k in range(blocks.shape[0]):
        at_row = lax.rem(brow[k], row_span)
        at_col = lax.div(bcol[k], row_span) * stretch + lax.rem(bcol[k], stretch)
        acc[at_row] += nt_dot(panel[at_col], blocks[k])
    spread(out_refs, acc, "col", stretch)
    value = v_ref[...]
    both = jnp.concatenate([value, value * prior[...]], axis=0)
    store_split(out_refs, stretch, nt_dot(value, both, FP32))


def foot_kernel(in_ref, foot_ref, gram_ref):
    stretch = foot_ref.shape[0]
    for j in range(stretch):
        foot_ref[j] = load_sum(in_ref, j).astype(jnp.bfloat16)
    gram_ref[...] = load_split(in_ref, stretch)


def backward_kernel(row_span, stretch, brow, bcol, foot, blocks, gram, out_refs, acc, panel):
    acc[...] = jnp.zeros_like(acc)
    fill_panel(panel, foot, "col")
    for k in range(blocks.shape[0]):
        at_row = lax.rem(brow[k], row_span)
        at_col = lax.div(bcol[k], row_span) * stretch + lax.rem(bcol[k], stretch)
        acc[at_col] += jnp.dot(panel[at_row], blocks[k], preferred_element_type=jnp.float32)
    spread(out_refs, acc, "row", stretch)
    whole = jnp.concatenate([panel[b] for b in range(row_span)], axis=1)
    padded = jnp.concatenate([jnp.zeros_like(whole), whole], axis=0)
    store_split(out_refs, stretch, gram[...] + nt_dot(whole, padded))


def frame_scale(gram):
    n = gram.shape[0]
    same = lax.broadcasted_iota(jnp.int32, (n, n), 0) == lax.broadcasted_iota(jnp.int32, (n, n), 1)
    norm = jnp.where(same, gram[:, :n], 0.0)
    energy = jnp.where(same, gram[:, n:], 0.0)
    column = jnp.sum(energy, axis=1, keepdims=True) / jnp.sum(norm, axis=1, keepdims=True)
    row = jnp.sum(energy, axis=0, keepdims=True) / jnp.sum(norm, axis=0, keepdims=True)
    return 1.25 * column, 1.25 * row


def image_kernel(in_ref, v_ref, prior, image_ref, next_ref, cast_ref, gram_ref):
    stretch = cast_ref.shape[0]
    gram = load_split(in_ref, stretch)
    gram_ref[...] = gram
    scale, _ = frame_scale(gram)
    for j in range(stretch):
        value = v_ref[:, lanes(j)]
        image = load_sum(in_ref, j) + prior[:, lanes(j)] * value
        following = image - scale * value
        image_ref[:, lanes(j)] = image
        next_ref[:, lanes(j)] = following
        cast_ref[j] = following.astype(jnp.bfloat16)


def eliminate(work, n):
    at = lax.broadcasted_iota(jnp.int32, (n, 1), 0)
    for k in range(n):
        pivot_row = work[k : k + 1, :] / work[k : k + 1, k : k + 1]
        column = jnp.where(at == k, 0.0, work[:, k : k + 1])
        work = jnp.where(at == k, pivot_row, work - column * pivot_row)
    return work[:, n:]


def inverse_kernel(gram, out_ref):
    n = gram.shape[0]
    eye = lax.broadcasted_iota(jnp.int32, (n, n), 0) == lax.broadcasted_iota(jnp.int32, (n, n), 1)
    out_ref[...] = eliminate(
        jnp.concatenate([gram[:, n:], jnp.where(eye, 1.0, 0.0)], axis=1), n
    )


def final_kernel(in_ref, v_ref, image_ref, next_ref, prior, gram_ref, inverse_ref, x_ref, r_ref):
    n = gram_ref.shape[0]
    stretch = in_ref[0].shape[0] - 2
    gram = gram_ref[...]
    norm, energy = gram[:, :n], gram[:, n:]
    scale, scale_row = frame_scale(gram)
    second = load_split(in_ref, stretch)
    next_norm, next_energy = second[:, :n], second[:, n:]
    next_rhs = energy - scale * norm
    cross = next_norm + next_rhs * scale_row
    inverse = inverse_ref[...]
    alpha = nn_dot(inverse, norm)
    conj = nn_dot(inverse, cross.T)
    schur = next_energy - nn_dot(cross, conj)
    rhs = next_rhs - nn_dot(cross, alpha)
    gamma = eliminate(jnp.concatenate([schur, rhs], axis=1), n)
    first = alpha - nn_dot(conj, gamma)
    coeffs = jnp.concatenate([first, gamma], axis=0)
    for j in range(stretch):
        value = v_ref[:, lanes(j)]
        following = next_ref[:, lanes(j)]
        second_image = load_sum(in_ref, j) + prior[:, lanes(j)] * following
        x_ref[:, lanes(j)] = tn_dot(coeffs, jnp.concatenate([value, following], axis=0))
        r_ref[:, lanes(j)] = value - tn_dot(
            coeffs, jnp.concatenate([image_ref[:, lanes(j)], second_image], axis=0)
        )


def swap(x, axis, flip):
    return lax.ppermute(x, axis, [(i, i ^ flip) for i in range(lax.axis_size(axis))])


def gather(x, axis):
    return tuple([x] + [swap(x, axis, s) for s in range(1, lax.axis_size(axis))])


def exchange(parts, axis):
    return tuple([parts[0]] + [swap(x, axis, s) for s, x in enumerate(parts) if s])


def shards(right_side, prior, blocks, block_row, block_col):
    frames, pix = right_side.shape
    stretch = pix // BLOCK
    rows, cols = lax.axis_size("row"), lax.axis_size("col")
    row_span, col_span = stretch * cols, stretch * rows
    prior = prior.reshape(1, pix)
    f32, bf16 = jnp.float32, jnp.bfloat16

    def shape(dims, dtype):
        return jax.ShapeDtypeStruct(dims, dtype)

    panel = shape((stretch, frames, BLOCK), bf16)
    gram_type = shape((frames, 2 * frames), f32)
    own = shape((frames, pix), f32)

    def apply_operator(own_value, own_cast):
        search = gather(own_cast, "row")
        (partial,) = call(
            lambda *refs: forward_kernel(row_span, stretch, *refs),
            ((shape((stretch + 2, frames, BLOCK), bf16),) * cols,),
            (block_row, block_col, search, blocks, own_value, prior),
            [pltpu.VMEM((row_span, frames, BLOCK), f32), pltpu.VMEM((col_span, frames, BLOCK), bf16)],
        )
        foot, gram = call(foot_kernel, (panel, gram_type), (exchange(partial, "col"),))
        foot = gather(foot, "col")
        (partial,) = call(
            lambda *refs: backward_kernel(row_span, stretch, *refs),
            ((shape((stretch + 2, frames, BLOCK), bf16),) * rows,),
            (block_row, block_col, foot, blocks, gram),
            [pltpu.VMEM((col_span, frames, BLOCK), f32), pltpu.VMEM((row_span, frames, BLOCK), bf16)],
        )
        return exchange(partial, "row")

    cast = call(cast_kernel, panel, (right_side,))
    received = apply_operator(right_side, cast)
    image, following, cast, gram = call(
        image_kernel, (own, own, panel, gram_type), (received, right_side, prior)
    )
    inverse = call(inverse_kernel, shape((frames, frames), f32), (gram,))
    received = apply_operator(following, cast)
    return call(
        final_kernel,
        (own, own),
        (received, right_side, image, following, prior, gram, inverse),
    )


def solution(mesh):
    return jax.shard_map(
        shards,
        mesh=mesh,
        in_specs=(
            P("groups", ("row", "col")),
            P(("row", "col")),
            P(("row", "col"), None, None),
            P(("row", "col")),
            P(("row", "col")),
        ),
        out_specs=(P("groups", ("row", "col")), P("groups", ("row", "col"))),
        check_vma=False,
    )
```

```python
import jax
import jax.numpy as jnp
from jax import lax
from jax.experimental import pallas as pl
from jax.experimental.pallas import tpu as pltpu
from jax.sharding import PartitionSpec as P

BLOCK = 128
TILE = 8
PANEL = 4
DIAG = 16
F32, BF16 = jnp.float32, jnp.bfloat16
FP32 = lax.Precision.HIGHEST
VMEM = pl.BlockSpec(memory_space=pltpu.VMEM)
SMEM = pl.BlockSpec(memory_space=pltpu.SMEM)
ANY = pl.BlockSpec(memory_space=pl.ANY)


def nt_dot(a, b, precision=None):
    return lax.dot_general(
        a, b, (((1,), (1,)), ((), ())), precision=precision, preferred_element_type=F32
    )


def tn_dot(a, b):
    return lax.dot_general(
        a, b, (((0,), (0,)), ((), ())), precision=FP32, preferred_element_type=F32
    )


def nn_dot(a, b):
    return lax.dot_general(
        a, b, (((1,), (0,)), ((), ())), precision=FP32, preferred_element_type=F32
    )


def call(kernel, outs, ins, scratch=(), specs=None, cost=None):
    flat_ins, ins_tree = jax.tree.flatten(tuple(ins))
    flat_outs, outs_tree = jax.tree.flatten(tuple(outs))

    def body(*refs):
        middle, last = len(flat_ins), len(flat_ins) + len(flat_outs)
        kernel(
            *jax.tree.unflatten(ins_tree, refs[:middle]),
            *jax.tree.unflatten(outs_tree, refs[middle:last]),
            *refs[last:],
        )

    def space(x):
        return SMEM if x.dtype == jnp.int32 else VMEM

    results = pl.pallas_call(
        body,
        out_shape=flat_outs,
        in_specs=specs or [space(x) for x in flat_ins],
        out_specs=[space(x) for x in flat_outs],
        scratch_shapes=list(scratch),
        compiler_params=pltpu.CompilerParams(vmem_limit_bytes=48 * 1024 * 1024),
        cost_estimate=cost,
    )(*flat_ins)
    return jax.tree.unflatten(outs_tree, results)


def lanes(j):
    return slice(j * BLOCK, (j + 1) * BLOCK)


def rows(j, count):
    return slice(j * count, (j + 1) * count)


def split(value):
    high = value.astype(BF16)
    return high, (value - high.astype(F32)).astype(BF16)


def sum_rows(refs, at):
    total = refs[0][at, :].astype(F32)
    for ref in refs[1:]:
        total += ref[at, :].astype(F32)
    return total


def eye(n):
    return lax.broadcasted_iota(jnp.int32, (n, n), 0) == lax.broadcasted_iota(jnp.int32, (n, n), 1)


def cast_kernel(v_ref, out_ref):
    frames = v_ref.shape[0]
    for j in range(v_ref.shape[1] // BLOCK):
        out_ref[rows(j, frames), :] = v_ref[:, lanes(j)].astype(BF16)


def stage_kernel(row_span, stretch, brow, bcol, blocks, index_ref, out_ref, sem):
    copy = pltpu.make_async_copy(blocks, out_ref, sem)
    copy.start()
    for k in range(brow.shape[0]):
        index_ref[0, k] = lax.rem(brow[k], row_span)
        index_ref[1, k] = lax.div(bcol[k], row_span) * stretch + lax.rem(bcol[k], stretch)
    copy.wait()


def gram_kernel(v_ref, prior, out_ref):
    value = v_ref[...]
    out_ref[...] = nt_dot(value, jnp.concatenate([value, value * prior[...]], axis=0), FP32)


def fill(panel, ref, at, stretch):
    frames = panel.shape[1]
    for j in range(stretch):
        panel[at * stretch + j] = ref[rows(j, frames), :]


def whole_of(panel):
    return jnp.concatenate([panel[b] for b in range(panel.shape[0])], axis=1)


def forward_kernel(stretch, cols, index, search, blocks, gram, half, keep_ref, send_ref, acc, panel):
    frames = panel.shape[1]
    me = lax.axis_index("row")
    for shift, ref in enumerate(search):
        fill(panel, ref, lax.rem(me - shift + len(search), len(search)), stretch)
    acc[...] = jnp.zeros_like(acc)
    for k in range(blocks.shape[0]):
        acc[index[0, k]] += nt_dot(panel[index[1, k]], blocks[k])
    core = lax.rem(lax.axis_index("col"), 2)
    for x in range(cols // 2):
        for j in range(stretch):
            at = rows(x * stretch + j, frames)
            keep_ref[at, :] = acc[(2 * x + core) * stretch + j]
            send_ref[at, :] = acc[(2 * x + 1 - core) * stretch + j]
    at = rows(cols // 2 * stretch, frames)
    value = gram[...]
    if half:
        whole = whole_of(panel)
        inner = nt_dot(whole, jnp.concatenate([whole, jnp.zeros_like(whole)], axis=0))
        lane = lax.broadcasted_iota(jnp.int32, value.shape, 1)
        value = jnp.where(lane < frames, inner, value)
        send_ref[at.stop :, :] = half[0][...]
        keep_ref[at.stop :, :] = half[0][...]
    keep_ref[at, :] = value
    send_ref[at, :] = value


def pair_kernel(frames, keep, received, out_ref, first_refs):
    core = lax.rem(lax.axis_index("col"), 2)
    split_at = frames // 2
    data = out_ref.shape[0] - frames
    for j in range(data // frames):
        at = rows(j, frames)
        out_ref[at, :] = (keep[at, :] + received[at, :]).astype(BF16)
    at = pl.ds(pl.multiple_of(data + core * split_at, split_at), split_at)
    out_ref[data : data + split_at, :], out_ref[data + split_at :, :] = split(
        keep[at, :] + received[at, :]
    )
    if first_refs:
        at = pl.ds(pl.multiple_of(core * split_at, split_at), split_at)
        first_refs[0][at, :] = keep[data + frames :, :]
        at = pl.ds(pl.multiple_of((1 - core) * split_at, split_at), split_at)
        first_refs[0][at, :] = received[data + frames :, :]


def chips_kernel(frames, parts, out_ref):
    split_at = frames // 2
    data = out_ref.shape[0] - frames
    for j in range(data // frames):
        at = rows(j, frames)
        out_ref[at, :] = sum_rows(parts, at).astype(BF16)
    high, low = slice(data, data + split_at), slice(data + split_at, data + frames)
    out_ref[high, :], out_ref[low, :] = split(sum_rows(parts, high) + sum_rows(parts, low))


def backward_kernel(
    stretch, cols, last, index, own, received, blocks, out_refs, norm_refs, acc, panel, gram
):
    frames = panel.shape[1]
    split_at = frames // 2
    core = lax.rem(lax.axis_index("col"), 2)
    data = cols // 2 * stretch * frames
    for ref, side in ((own, core), (received, 1 - core)):
        for x in range(cols // 2):
            for j in range(stretch):
                panel[(2 * x + side) * stretch + j] = ref[rows(x * stretch + j, frames), :]
        at = pl.ds(pl.multiple_of(side * split_at, split_at), split_at)
        gram[at, :] = ref[data : data + split_at, :].astype(F32) + ref[data + split_at :, :].astype(
            F32
        )
    acc[...] = jnp.zeros_like(acc)
    for k in range(blocks.shape[0]):
        acc[index[1, k]] += jnp.dot(panel[index[0, k]], blocks[k], preferred_element_type=F32)
    me = lax.axis_index("row")
    for shift, out_ref in enumerate(out_refs):
        dest = lax.rem(me + shift, len(out_refs))
        for j in range(stretch):
            out_ref[rows(j, frames), :] = acc[dest * stretch + j].astype(BF16)
    whole = whole_of(panel)
    total = gram[...] + nt_dot(whole, jnp.concatenate([jnp.zeros_like(whole), whole], axis=0))
    at = stretch * frames
    if last:
        high, low = split(total[:, frames:])
        block = jnp.concatenate([high, low], axis=1)
        for out_ref in out_refs:
            out_ref[at:, :] = block
        norm_refs[0][...] = total[:, :frames]
    else:
        gram[...] = total
        high, low = split(gram[pl.ds(pl.multiple_of(core * split_at, split_at), split_at), :])
        lane = lax.broadcasted_iota(jnp.int32, total.shape, 1)
        row = lax.broadcasted_iota(jnp.int32, total.shape, 0)
        on_diagonal = jnp.logical_or(lane == row, lane == row + frames)
        diagonal = jnp.sum(jnp.where(on_diagonal, total, 0.0), axis=0, keepdims=True)
        row = lax.broadcasted_iota(jnp.int32, (DIAG, 2 * frames), 0)
        tile = jnp.where(row == 0, diagonal, 0.0).astype(BF16)
        for out_ref in out_refs:
            out_ref[at : at + split_at, :] = high
            out_ref[at + split_at : at + frames, :] = low
            out_ref[at + frames :, :] = tile


def frame_shift(diagonal, frames):
    row = 1.25 * diagonal[:, frames:] / diagonal[:, :frames]
    return jnp.sum(jnp.where(eye(frames), row, 0.0), axis=1, keepdims=True), row


def image_kernel(parts, v_ref, prior, image_ref, next_ref, cast_ref, half_ref, diag_ref):
    frames = v_ref.shape[0]
    split_at = frames // 2
    data = cast_ref.shape[0]
    diagonal = sum_rows(parts, slice(data + frames, data + frames + DIAG))
    diag_ref[...] = diagonal
    shift, _ = frame_shift(diagonal[0:1, :], frames)
    for j in range(data // frames):
        value = v_ref[:, lanes(j)]
        image = sum_rows(parts, rows(j, frames)) + prior[:, lanes(j)] * value
        following = image - shift * value
        image_ref[:, lanes(j)] = image
        next_ref[:, lanes(j)] = following
        cast_ref[rows(j, frames), :] = following.astype(BF16)
    half_ref[...] = sum_rows(parts, slice(data, data + split_at)) + sum_rows(
        parts, slice(data + split_at, data + frames)
    )


def eliminate(matrix, right, n):
    width = matrix.shape[1] + right.shape[1]
    work = jnp.concatenate([matrix, right], axis=1)
    work = [work[rows(i, TILE), :] for i in range(n // TILE)]
    at = lax.broadcasted_iota(jnp.int32, (TILE, width), 0)

    def step(tiles, column, k, pivot):
        i, s = divmod(k, TILE)
        row = tiles[i][s : s + 1, :] * pivot
        done = [t - c * row for t, c in zip(tiles, column)]
        done[i] = jnp.where(at == s, row, done[i])
        return done

    for start in range(0, n, PANEL):
        columns = [
            [jnp.broadcast_to(t[:, k : k + 1], (TILE, width)) for t in work]
            for k in range(start, start + PANEL)
        ]
        for u in range(PANEL):
            k = start + u
            i, s = divmod(k, TILE)
            pivot = 1.0 / columns[u][i][s : s + 1, :]
            for later in range(u + 1, PANEL):
                columns[later] = step(columns[later], columns[u], k, pivot)
            work = step(work, columns[u], k, pivot)
    return jnp.concatenate(work, axis=0)[:, n:]


def inverse_kernel(first, out_ref):
    n = first.shape[0]
    out_ref[...] = eliminate(first[:, n:], jnp.where(eye(n), 1.0, 0.0), n)


def final_kernel(
    parts, v_ref, image_ref, next_ref, prior, first, inverse_ref, norm_ref, diag_ref, x_ref, r_ref
):
    n = first.shape[0]
    data = parts[0].shape[0] - n
    norm, energy = first[:, :n], first[:, n:]
    shift, shift_row = frame_shift(diag_ref[0:1, :], n)
    second = sum_rows(parts, slice(data, data + n))
    next_energy = second[:, :n] + second[:, n:]
    next_rhs = energy - shift * norm
    cross = norm_ref[...] + next_rhs * shift_row
    inverse = inverse_ref[...]
    alpha = nn_dot(inverse, norm)
    conj = nn_dot(inverse, cross.T)
    schur = next_energy - nn_dot(cross, conj)
    rhs = next_rhs - nn_dot(cross, alpha)
    gamma = eliminate(schur, rhs, n)
    coeffs = jnp.concatenate([alpha - nn_dot(conj, gamma), gamma], axis=0)
    for j in range(data // n):
        value = v_ref[:, lanes(j)]
        following = next_ref[:, lanes(j)]
        second_image = sum_rows(parts, rows(j, n)) + prior[:, lanes(j)] * following
        x_ref[:, lanes(j)] = tn_dot(coeffs, jnp.concatenate([value, following], axis=0))
        r_ref[:, lanes(j)] = value - tn_dot(
            coeffs, jnp.concatenate([image_ref[:, lanes(j)], second_image], axis=0)
        )


def shifted(x, axis, shift):
    count = lax.axis_size(axis)
    return lax.ppermute(x, axis, [(i, (i + shift) % count) for i in range(count)])


def swapped(x, axis, flip):
    return lax.ppermute(x, axis, [(i, i ^ flip) for i in range(lax.axis_size(axis))])


def gather(x, axis):
    return tuple([x] + [shifted(x, axis, s) for s in range(1, lax.axis_size(axis))])


def exchange(parts, axis):
    return tuple([parts[0]] + [shifted(x, axis, s) for s, x in enumerate(parts) if s])


def shards(right_side, prior, blocks, block_row, block_col):
    frames, pix = right_side.shape
    stretch = pix // BLOCK
    n_rows, n_cols = lax.axis_size("row"), lax.axis_size("col")
    row_span, col_span = stretch * n_cols, stretch * n_rows
    prior = prior.reshape(1, pix)
    stored = blocks.shape[0]
    half_cols = n_cols // 2 * stretch * frames

    def shape(dims, dtype=F32):
        return jax.ShapeDtypeStruct(dims, dtype)

    own = shape((frames, pix))
    gram_type = shape((frames, 2 * frames))
    cast_type = shape((stretch * frames, BLOCK), BF16)
    aside = pl.CostEstimate(flops=2 * 10**9, bytes_accessed=8 * 10**6, transcendentals=0)

    def forward(search, gram, half):
        size = half_cols + frames + (frames // 2 if half else 0)
        keep, send = call(
            lambda *refs: forward_kernel(stretch, n_cols, *refs),
            (shape((size, BLOCK)),) * 2,
            (index, search, staged, gram, half),
            [
                pltpu.VMEM((row_span, frames, BLOCK), F32),
                pltpu.VMEM((col_span, frames, BLOCK), BF16),
            ],
        )
        received = swapped(send, "col", 1)
        pair, first = call(
            lambda *refs: pair_kernel(frames, *refs),
            (shape((half_cols + frames, BLOCK), BF16), (gram_type,) if half else ()),
            (keep, received),
        )
        parts = tuple([pair] + [swapped(pair, "col", flip) for flip in range(2, n_cols, 2)])
        (foot,) = call(
            lambda *refs: chips_kernel(frames, *refs),
            (shape((half_cols + frames, BLOCK), BF16),),
            (parts,),
        )
        return foot, swapped(foot, "col", 1), first

    def backward(own_foot, other_foot, last):
        size = stretch * frames + frames + (0 if last else DIAG)
        parts, norm = call(
            lambda *refs: backward_kernel(stretch, n_cols, last, *refs),
            ((shape((size, BLOCK), BF16),) * n_rows, (shape((frames, frames)),) if last else ()),
            (index, own_foot, other_foot, staged),
            [
                pltpu.VMEM((col_span, frames, BLOCK), F32),
                pltpu.VMEM((row_span, frames, BLOCK), BF16),
                pltpu.VMEM((frames, 2 * frames), F32),
            ],
        )
        return exchange(parts, "row"), norm

    (cast,) = call(cast_kernel, (cast_type,), (right_side,))
    search = gather(cast, "row")
    index, staged = call(
        lambda *refs: stage_kernel(row_span, stretch, *refs),
        (shape((2, stored), jnp.int32), shape(blocks.shape, BF16)),
        (block_row, block_col, blocks),
        [pltpu.SemaphoreType.DMA],
        specs=[SMEM, SMEM, ANY],
        cost=aside,
    )
    (gram,) = call(gram_kernel, (gram_type,), (right_side, prior), cost=aside)
    own_foot, other_foot, _ = forward(search, gram, ())
    parts, _ = backward(own_foot, other_foot, False)
    image, following, cast, half, diagonal = call(
        image_kernel,
        (own, own, cast_type, shape((frames // 2, 2 * frames)), shape((DIAG, 2 * frames))),
        (parts, right_side, prior),
    )
    search = gather(cast, "row")
    (gram,) = call(gram_kernel, (gram_type,), (following, prior), cost=aside)
    own_foot, other_foot, (first,) = forward(search, gram, (half,))
    (inverse,) = call(inverse_kernel, (shape((frames, frames)),), (first,), cost=aside)
    parts, (norm,) = backward(own_foot, other_foot, True)
    return tuple(
        call(
            final_kernel,
            (own, own),
            (parts, right_side, image, following, prior, first, inverse, norm, diagonal),
        )
    )


def solution(mesh):
    return jax.shard_map(
        shards,
        mesh=mesh,
        in_specs=(
            P("groups", ("row", "col")),
            P(("row", "col")),
            P(("row", "col"), None, None),
            P(("row", "col")),
            P(("row", "col")),
        ),
        out_specs=(P("groups", ("row", "col")), P("groups", ("row", "col"))),
        check_vma=False,
    )
```

```python
import jax
import jax.numpy as jnp
from jax import lax
from jax.experimental import pallas as pl
from jax.experimental.pallas import tpu as pltpu
from jax.sharding import PartitionSpec as P

BLOCK = 128
TILE = 8
AHEAD = 4
DIAG = 16
F32, BF16 = jnp.float32, jnp.bfloat16
FP32 = lax.Precision.HIGHEST
VMEM = pl.BlockSpec(memory_space=pltpu.VMEM)
SMEM = pl.BlockSpec(memory_space=pltpu.SMEM)
ANY = pl.BlockSpec(memory_space=pl.ANY)


def nt_dot(a, b, precision=None):
    return lax.dot_general(
        a, b, (((1,), (1,)), ((), ())), precision=precision, preferred_element_type=F32
    )


def tn_dot(a, b):
    return lax.dot_general(
        a, b, (((0,), (0,)), ((), ())), precision=FP32, preferred_element_type=F32
    )


def nn_dot(a, b):
    return lax.dot_general(
        a, b, (((1,), (0,)), ((), ())), precision=FP32, preferred_element_type=F32
    )


def call(kernel, outs, ins, scratch=(), specs=None, cost=None):
    flat_ins, ins_tree = jax.tree.flatten(tuple(ins))
    flat_outs, outs_tree = jax.tree.flatten(tuple(outs))

    def body(*refs):
        middle, last = len(flat_ins), len(flat_ins) + len(flat_outs)
        kernel(
            *jax.tree.unflatten(ins_tree, refs[:middle]),
            *jax.tree.unflatten(outs_tree, refs[middle:last]),
            *refs[last:],
        )

    def space(x):
        return SMEM if x.dtype == jnp.int32 else VMEM

    results = pl.pallas_call(
        body,
        out_shape=flat_outs,
        in_specs=specs or [space(x) for x in flat_ins],
        out_specs=[space(x) for x in flat_outs],
        scratch_shapes=list(scratch),
        compiler_params=pltpu.CompilerParams(vmem_limit_bytes=48 * 1024 * 1024),
        cost_estimate=cost,
    )(*flat_ins)
    return jax.tree.unflatten(outs_tree, results)


def lanes(j):
    return slice(j * BLOCK, (j + 1) * BLOCK)


def rows(j, count):
    return slice(j * count, (j + 1) * count)


def split(value):
    high = value.astype(BF16)
    return high, (value - high.astype(F32)).astype(BF16)


def sum_rows(refs, at):
    total = refs[0][at, :].astype(F32)
    for ref in refs[1:]:
        total += ref[at, :].astype(F32)
    return total


def eye(n):
    return lax.broadcasted_iota(jnp.int32, (n, n), 0) == lax.broadcasted_iota(jnp.int32, (n, n), 1)


def cast_kernel(v_ref, out_ref):
    frames = v_ref.shape[0]
    for j in range(v_ref.shape[1] // BLOCK):
        out_ref[rows(j, frames), :] = v_ref[:, lanes(j)].astype(BF16)


def stage_kernel(row_span, stretch, brow, bcol, blocks, index_ref, out_ref, sem):
    copy = pltpu.make_async_copy(blocks, out_ref, sem)
    copy.start()
    for k in range(brow.shape[0]):
        index_ref[0, k] = lax.rem(brow[k], row_span)
        index_ref[1, k] = lax.div(bcol[k], row_span) * stretch + lax.rem(bcol[k], stretch)
    copy.wait()


def turn_kernel(blocks, out_ref):
    for k in range(blocks.shape[0]):
        out_ref[k] = blocks[k].T


def gram_kernel(v_ref, prior, out_ref):
    value = v_ref[...]
    out_ref[...] = nt_dot(value, jnp.concatenate([value, value * prior[...]], axis=0), FP32)


def fill(panel, ref, at, stretch):
    frames = panel.shape[1]
    for j in range(stretch):
        panel[at * stretch + j] = ref[rows(j, frames), :]


def whole_of(panel):
    return jnp.concatenate([panel[b] for b in range(panel.shape[0])], axis=1)


def forward_kernel(stretch, cols, index, search, blocks, gram, half, keep_ref, send_ref, acc, panel):
    frames = panel.shape[1]
    me = lax.axis_index("row")
    for flip, ref in enumerate(search):
        fill(panel, ref, lax.bitwise_xor(me, flip), stretch)
    acc[...] = jnp.zeros_like(acc)
    for k in range(blocks.shape[0]):
        if half:
            part = jnp.dot(panel[index[1, k]], blocks[k], preferred_element_type=F32)
        else:
            part = nt_dot(panel[index[1, k]], blocks[k])
        acc[index[0, k]] += part
    core = lax.rem(lax.axis_index("col"), 2)
    for x in range(cols // 2):
        for j in range(stretch):
            at = rows(x * stretch + j, frames)
            keep_ref[at, :] = acc[(2 * x + core) * stretch + j]
            send_ref[at, :] = acc[(2 * x + 1 - core) * stretch + j]
    at = rows(cols // 2 * stretch, frames)
    value = gram[...]
    if half:
        whole = whole_of(panel)
        inner = nt_dot(whole, jnp.concatenate([whole, jnp.zeros_like(whole)], axis=0))
        lane = lax.broadcasted_iota(jnp.int32, value.shape, 1)
        value = jnp.where(lane < frames, inner, value)
        send_ref[at.stop :, :] = half[0][...]
        keep_ref[at.stop :, :] = half[0][...]
    keep_ref[at, :] = value
    send_ref[at, :] = value


def pair_kernel(frames, keep, received, out_ref, first_refs):
    core = lax.rem(lax.axis_index("col"), 2)
    split_at = frames // 2
    data = out_ref.shape[0] - frames
    for j in range(data // frames):
        at = rows(j, frames)
        out_ref[at, :] = (keep[at, :] + received[at, :]).astype(BF16)
    at = pl.ds(pl.multiple_of(data + core * split_at, split_at), split_at)
    out_ref[data : data + split_at, :], out_ref[data + split_at :, :] = split(
        keep[at, :] + received[at, :]
    )
    if first_refs:
        at = pl.ds(pl.multiple_of(core * split_at, split_at), split_at)
        first_refs[0][at, :] = keep[data + frames :, :]
        at = pl.ds(pl.multiple_of((1 - core) * split_at, split_at), split_at)
        first_refs[0][at, :] = received[data + frames :, :]


def chips_kernel(frames, parts, out_ref):
    split_at = frames // 2
    data = out_ref.shape[0] - frames
    for j in range(data // frames):
        at = rows(j, frames)
        out_ref[at, :] = sum_rows(parts, at).astype(BF16)
    high, low = slice(data, data + split_at), slice(data + split_at, data + frames)
    out_ref[high, :], out_ref[low, :] = split(sum_rows(parts, high) + sum_rows(parts, low))


def backward_kernel(
    stretch, cols, last, index, own, received, blocks,
    far_refs, near_ref, keep_refs, keep_ref, norm_refs, acc, panel, gram,
):
    frames = panel.shape[1]
    split_at = frames // 2
    core = lax.rem(lax.axis_index("col"), 2)
    data = cols // 2 * stretch * frames
    for ref, side in ((own, core), (received, 1 - core)):
        for x in range(cols // 2):
            for j in range(stretch):
                panel[(2 * x + side) * stretch + j] = ref[rows(x * stretch + j, frames), :]
        at = pl.ds(pl.multiple_of(side * split_at, split_at), split_at)
        gram[at, :] = ref[data : data + split_at, :].astype(F32) + ref[data + split_at :, :].astype(
            F32
        )
    acc[...] = jnp.zeros_like(acc)
    for k in range(blocks.shape[0]):
        acc[index[1, k]] += jnp.dot(panel[index[0, k]], blocks[k], preferred_element_type=F32)
    me = lax.axis_index("row")
    for far, (far_ref, kept_ref) in enumerate(zip(far_refs, keep_refs)):
        shard = lax.bitwise_xor(me, 2 * (far + 1))
        other = lax.bitwise_xor(shard, 1)
        for j in range(stretch):
            kept_ref[rows(j, frames), :] = acc[shard * stretch + j]
            far_ref[rows(j, frames), :] = acc[other * stretch + j].astype(BF16)
    other = lax.bitwise_xor(me, 1)
    for j in range(stretch):
        keep_ref[rows(j, frames), :] = acc[me * stretch + j]
        near_ref[rows(j, frames), :] = acc[other * stretch + j].astype(BF16)
    whole = whole_of(panel)
    total = gram[...] + nt_dot(whole, jnp.concatenate([jnp.zeros_like(whole), whole], axis=0))
    at = stretch * frames
    out_ref = far_refs[0]
    if last:
        high, low = split(total[:, frames:])
        out_ref[at:, :] = jnp.concatenate([high, low], axis=1)
        norm_refs[0][...] = total[:, :frames]
    else:
        gram[...] = total
        out_ref[at : at + split_at, :], out_ref[at + split_at : at + frames, :] = split(
            gram[pl.ds(pl.multiple_of(core * split_at, split_at), split_at), :]
        )
        lane = lax.broadcasted_iota(jnp.int32, total.shape, 1)
        row = lax.broadcasted_iota(jnp.int32, total.shape, 0)
        on_diagonal = jnp.logical_or(lane == row, lane == row + frames)
        diagonal = jnp.sum(jnp.where(on_diagonal, total, 0.0), axis=0, keepdims=True)
        row = lax.broadcasted_iota(jnp.int32, (DIAG, 2 * frames), 0)
        out_ref[at + frames :, :] = jnp.where(row == 0, diagonal, 0.0).astype(BF16)


def rows_kernel(last, frames, sent, received, kept, out_refs, gram_ref, diag_ref):
    split_at = frames // 2
    data = kept[0].shape[0]
    for out_ref, kept_ref, received_ref in zip(out_refs, kept, received):
        for j in range(data // frames):
            at = rows(j, frames)
            out_ref[at, :] = (kept_ref[at, :] + received_ref[at, :].astype(F32)).astype(BF16)
    pair = (sent, received[0])
    if last:
        both = sum_rows(pair, slice(data, data + frames))
        value = both[:, :frames] + both[:, frames:]
        block = jnp.concatenate(split(value), axis=1)
        gram_ref[...] = value
    else:
        high, low = slice(data, data + split_at), slice(data + split_at, data + frames)
        value = sum_rows(pair, high) + sum_rows(pair, low)
        gram_ref[...] = value
        block = jnp.concatenate(split(value), axis=0)
        tile = sum_rows(pair, slice(data + frames, data + frames + DIAG)).astype(BF16)
        diag_ref[0][...] = tile
    for out_ref in out_refs:
        out_ref[data : data + frames, :] = block
        if not last:
            out_ref[data + frames :, :] = tile


def own_sum(keep, near, far, j, frames):
    at = rows(j, frames)
    return keep[at, :] + sum_rows((near, *far), at)


def frame_shift(diagonal, frames):
    row = 1.25 * diagonal[:, frames:] / diagonal[:, :frames]
    return jnp.sum(jnp.where(eye(frames), row, 0.0), axis=1, keepdims=True), row


def image_kernel(
    keep, near, far, gram, tile, v_ref, prior, image_ref, next_ref, cast_ref, half_ref, diag_ref
):
    frames = v_ref.shape[0]
    split_at = frames // 2
    data = cast_ref.shape[0]
    diagonal = tile[...].astype(F32) + sum_rows(far, slice(data + frames, data + frames + DIAG))
    diag_ref[...] = diagonal
    shift, _ = frame_shift(diagonal[0:1, :], frames)
    for j in range(data // frames):
        value = v_ref[:, lanes(j)]
        image = own_sum(keep, near, far, j, frames) + prior[:, lanes(j)] * value
        following = image - shift * value
        image_ref[:, lanes(j)] = image
        next_ref[:, lanes(j)] = following
        cast_ref[rows(j, frames), :] = following.astype(BF16)
    half_ref[...] = (
        gram[...]
        + sum_rows(far, slice(data, data + split_at))
        + sum_rows(far, slice(data + split_at, data + frames))
    )


def eliminate(matrix, right, n):
    width = matrix.shape[1] + right.shape[1]
    work = jnp.concatenate([matrix, right], axis=1)
    work = [work[rows(i, TILE), :] for i in range(n // TILE)]
    at = lax.broadcasted_iota(jnp.int32, (TILE, width), 0)

    def column(k):
        return [jnp.broadcast_to(t[:, k : k + 1], (TILE, width)) for t in work]

    def step(tiles, spread, k, pivot):
        i, s = divmod(k, TILE)
        row = tiles[i][s : s + 1, :] * pivot
        done = [t - c * row for t, c in zip(tiles, spread)]
        done[i] = jnp.where(at == s, row, done[i])
        return done

    ahead = [column(k) for k in range(AHEAD)]
    for k in range(n):
        i, s = divmod(k, TILE)
        spread = ahead.pop(0)
        pivot = 1.0 / spread[i][s : s + 1, :]
        ahead = [step(later, spread, k, pivot) for later in ahead]
        work = step(work, spread, k, pivot)
        if k + AHEAD < n:
            ahead.append(column(k + AHEAD))
    return jnp.concatenate(work, axis=0)[:, n:]


def middle_kernel(first, norm_ref, diag_ref, out_ref):
    n = first.shape[0]
    norm, energy = first[:, :n], first[:, n:]
    shift, shift_row = frame_shift(diag_ref[0:1, :], n)
    inverse = eliminate(energy, jnp.where(eye(n), 1.0, 0.0), n)
    next_rhs = energy - shift * norm
    cross = norm_ref[...] + next_rhs * shift_row
    alpha = nn_dot(inverse, norm)
    conj = nn_dot(inverse, cross.T)
    out_ref[0] = alpha
    out_ref[1] = conj
    out_ref[2] = nn_dot(cross, conj)
    out_ref[3] = next_rhs - nn_dot(cross, alpha)


def final_kernel(
    keep, near, far, gram, v_ref, image_ref, next_ref, prior, middle, x_ref, r_ref
):
    n = v_ref.shape[0]
    data = keep.shape[0]
    second = sum_rows(far, slice(data, data + n))
    schur = gram[...] + second[:, :n] + second[:, n:] - middle[2]
    gamma = eliminate(schur, middle[3], n)
    coeffs = jnp.concatenate([middle[0] - nn_dot(middle[1], gamma), gamma], axis=0)
    for j in range(data // n):
        value = v_ref[:, lanes(j)]
        following = next_ref[:, lanes(j)]
        second_image = own_sum(keep, near, far, j, n) + prior[:, lanes(j)] * following
        x_ref[:, lanes(j)] = tn_dot(coeffs, jnp.concatenate([value, following], axis=0))
        r_ref[:, lanes(j)] = value - tn_dot(
            coeffs, jnp.concatenate([image_ref[:, lanes(j)], second_image], axis=0)
        )


def swapped(x, axis, flip):
    return lax.ppermute(x, axis, [(i, i ^ flip) for i in range(lax.axis_size(axis))])


def gather(x, axis):
    even = [x] + [swapped(x, axis, flip) for flip in range(2, lax.axis_size(axis), 2)]
    return tuple(part for own in even for part in (own, swapped(own, axis, 1)))


def shards(right_side, prior, blocks, block_row, block_col):
    frames, pix = right_side.shape
    stretch = pix // BLOCK
    n_rows, n_cols = lax.axis_size("row"), lax.axis_size("col")
    row_span, col_span = stretch * n_cols, stretch * n_rows
    prior = prior.reshape(1, pix)
    stored = blocks.shape[0]
    half_cols = n_cols // 2 * stretch * frames

    def shape(dims, dtype=F32):
        return jax.ShapeDtypeStruct(dims, dtype)

    own = shape((frames, pix))
    gram_type = shape((frames, 2 * frames))
    cast_type = shape((stretch * frames, BLOCK), BF16)
    aside = pl.CostEstimate(flops=2 * 10**9, bytes_accessed=8 * 10**6, transcendentals=0)

    def forward(search, gram, half):
        size = half_cols + frames + (frames // 2 if half else 0)
        keep, send = call(
            lambda *refs: forward_kernel(stretch, n_cols, *refs),
            (shape((size, BLOCK)),) * 2,
            (index, search, turned if half else staged, gram, half),
            [
                pltpu.VMEM((row_span, frames, BLOCK), F32),
                pltpu.VMEM((col_span, frames, BLOCK), BF16),
            ],
        )
        received = swapped(send, "col", 1)
        pair, first = call(
            lambda *refs: pair_kernel(frames, *refs),
            (shape((half_cols + frames, BLOCK), BF16), (gram_type,) if half else ()),
            (keep, received),
        )
        parts = tuple([pair] + [swapped(pair, "col", flip) for flip in range(2, n_cols, 2)])
        (foot,) = call(
            lambda *refs: chips_kernel(frames, *refs),
            (shape((half_cols + frames, BLOCK), BF16),),
            (parts,),
        )
        return foot, swapped(foot, "col", 1), first

    def backward(own_foot, other_foot, last):
        size = stretch * frames
        extra = frames + (0 if last else DIAG)
        pairs = n_rows // 2 - 1
        far, near, kept, keep, norm = call(
            lambda *refs: backward_kernel(stretch, n_cols, last, *refs),
            (
                tuple(shape((size + (0 if p else extra), BLOCK), BF16) for p in range(pairs)),
                shape((size, BLOCK), BF16),
                (shape((size, BLOCK)),) * pairs,
                shape((size, BLOCK)),
                (shape((frames, frames)),) if last else (),
            ),
            (index, own_foot, other_foot, staged),
            [
                pltpu.VMEM((col_span, frames, BLOCK), F32),
                pltpu.VMEM((row_span, frames, BLOCK), BF16),
                pltpu.VMEM((frames, 2 * frames), F32),
            ],
        )
        received = tuple(swapped(x, "row", 1) for x in far)
        near = swapped(near, "row", 1)
        sums, gram, tile = call(
            lambda *refs: rows_kernel(last, frames, *refs),
            (
                (shape((size + extra, BLOCK), BF16),) * pairs,
                shape((frames, frames) if last else (frames // 2, 2 * frames)),
                () if last else (shape((DIAG, 2 * frames), BF16),),
            ),
            (far[0], received, kept),
        )
        far = tuple(swapped(x, "row", 2 * (p + 1)) for p, x in enumerate(sums))
        return (keep, near, far, gram, *tile), norm

    (cast,) = call(cast_kernel, (cast_type,), (right_side,))
    search = gather(cast, "row")
    index, staged = call(
        lambda *refs: stage_kernel(row_span, stretch, *refs),
        (shape((2, stored), jnp.int32), shape(blocks.shape, BF16)),
        (block_row, block_col, blocks),
        [pltpu.SemaphoreType.DMA],
        specs=[SMEM, SMEM, ANY],
        cost=aside,
    )
    (gram,) = call(gram_kernel, (gram_type,), (right_side, prior), cost=aside)
    own_foot, other_foot, _ = forward(search, gram, ())
    (turned,) = call(turn_kernel, (shape(blocks.shape, BF16),), (staged,), cost=aside)
    parts, _ = backward(own_foot, other_foot, False)
    image, following, cast, half, diagonal = call(
        image_kernel,
        (own, own, cast_type, shape((frames // 2, 2 * frames)), shape((DIAG, 2 * frames))),
        (*parts, right_side, prior),
    )
    search = gather(cast, "row")
    (gram,) = call(gram_kernel, (gram_type,), (following, prior), cost=aside)
    own_foot, other_foot, (first,) = forward(search, gram, (half,))
    parts, (norm,) = backward(own_foot, other_foot, True)
    (middle,) = call(
        middle_kernel, (shape((4, frames, frames)),), (first, norm, diagonal), cost=aside
    )
    return tuple(
        call(
            final_kernel,
            (own, own),
            (*parts, right_side, image, following, prior, middle),
        )
    )


def solution(mesh):
    return jax.shard_map(
        shards,
        mesh=mesh,
        in_specs=(
            P("groups", ("row", "col")),
            P(("row", "col")),
            P(("row", "col"), None, None),
            P(("row", "col")),
            P(("row", "col")),
        ),
        out_specs=(P("groups", ("row", "col")), P("groups", ("row", "col"))),
        check_vma=False,
    )
```

```python
import jax
import jax.numpy as jnp
from jax import lax
from jax.experimental import pallas as pl
from jax.experimental.pallas import tpu as pltpu
from jax.sharding import PartitionSpec as P

BLOCK = 128
TILE = 8
AHEAD = 4
DIAG = 16
F32, BF16 = jnp.float32, jnp.bfloat16
FP32 = lax.Precision.HIGHEST
VMEM = pl.BlockSpec(memory_space=pltpu.VMEM)
SMEM = pl.BlockSpec(memory_space=pltpu.SMEM)
ANY = pl.BlockSpec(memory_space=pl.ANY)


def nt_dot(a, b, precision=None):
    return lax.dot_general(
        a, b, (((1,), (1,)), ((), ())), precision=precision, preferred_element_type=F32
    )


def tn_dot(a, b):
    return lax.dot_general(
        a, b, (((0,), (0,)), ((), ())), precision=FP32, preferred_element_type=F32
    )


def nn_dot(a, b):
    return lax.dot_general(
        a, b, (((1,), (0,)), ((), ())), precision=FP32, preferred_element_type=F32
    )


def call(kernel, outs, ins, scratch=(), specs=None, cost=None):
    flat_ins, ins_tree = jax.tree.flatten(tuple(ins))
    flat_outs, outs_tree = jax.tree.flatten(tuple(outs))

    def body(*refs):
        middle, last = len(flat_ins), len(flat_ins) + len(flat_outs)
        kernel(
            *jax.tree.unflatten(ins_tree, refs[:middle]),
            *jax.tree.unflatten(outs_tree, refs[middle:last]),
            *refs[last:],
        )

    def space(x):
        return SMEM if x.dtype == jnp.int32 else VMEM

    results = pl.pallas_call(
        body,
        out_shape=flat_outs,
        in_specs=specs or [space(x) for x in flat_ins],
        out_specs=[space(x) for x in flat_outs],
        scratch_shapes=list(scratch),
        compiler_params=pltpu.CompilerParams(vmem_limit_bytes=48 * 1024 * 1024),
        cost_estimate=cost,
    )(*flat_ins)
    return jax.tree.unflatten(outs_tree, results)


def lanes(j):
    return slice(j * BLOCK, (j + 1) * BLOCK)


def rows(j, count):
    return slice(j * count, (j + 1) * count)


def split(value):
    high = value.astype(BF16)
    return high, (value - high.astype(F32)).astype(BF16)


def sum_rows(refs, at):
    total = refs[0][at, :].astype(F32)
    for ref in refs[1:]:
        total += ref[at, :].astype(F32)
    return total


def eye(n):
    return lax.broadcasted_iota(jnp.int32, (n, n), 0) == lax.broadcasted_iota(jnp.int32, (n, n), 1)


def cast_kernel(v_ref, out_ref):
    frames = v_ref.shape[0]
    for j in range(v_ref.shape[1] // BLOCK):
        out_ref[rows(j, frames), :] = v_ref[:, lanes(j)].astype(BF16)


def stage_kernel(row_span, stretch, brow, bcol, blocks, index_ref, out_ref, sem):
    copy = pltpu.make_async_copy(blocks, out_ref, sem)
    copy.start()
    for k in range(brow.shape[0]):
        index_ref[0, k] = lax.rem(brow[k], row_span)
        index_ref[1, k] = lax.div(bcol[k], row_span) * stretch + lax.rem(bcol[k], stretch)
    copy.wait()


def turn_kernel(blocks, out_ref):
    for k in range(blocks.shape[0]):
        out_ref[k] = blocks[k].T


def as_row(column):
    n = column.shape[0]
    return jnp.sum(jnp.where(eye(n), column, 0.0), axis=0, keepdims=True)


def as_tile(row):
    at = lax.broadcasted_iota(jnp.int32, (DIAG, row.shape[1]), 0)
    return jnp.where(at == 0, row, 0.0)


def split_tile(row):
    high, low = split(row)
    at = lax.broadcasted_iota(jnp.int32, (DIAG, row.shape[1]), 0)
    return jnp.where(at == 0, high.astype(F32), jnp.where(at == 1, low.astype(F32), 0.0)).astype(BF16)


def tile_row(tile):
    return tile[0:1, :] + tile[1:2, :]


def energy_kernel(v_ref, prior, out_ref):
    value = v_ref[...]
    plain = jnp.sum(value * value, axis=1, keepdims=True)
    weighted = jnp.sum(value * value * prior[...], axis=1, keepdims=True)
    out_ref[...] = as_tile(jnp.concatenate([as_row(plain), as_row(weighted)], axis=1))


def grams_kernel(v_ref, next_ref, prior, out_ref):
    n = v_ref.shape[0]
    for at, ref in ((slice(0, n), v_ref), (slice(n, 2 * n), next_ref)):
        value = ref[...]
        both = jnp.concatenate([value, value * prior[...]], axis=0)
        out_ref[at, :] = nt_dot(value, both, FP32)


def add_kernel(parts, out_ref):
    total = parts[0][...]
    for part in parts[1:]:
        total += part[...]
    out_ref[...] = total


def fill(panel, ref, at, stretch):
    frames = panel.shape[1]
    for j in range(stretch):
        panel[at * stretch + j] = ref[rows(j, frames), :]


def fill_foot(panel, own, received, stretch, cols):
    core = lax.rem(lax.axis_index("col"), 2)
    frames = panel.shape[1]
    for ref, side in ((own, core), (received, 1 - core)):
        for x in range(cols // 2):
            for j in range(stretch):
                panel[(2 * x + side) * stretch + j] = ref[rows(x * stretch + j, frames), :]


def foot_gram(own, received, data, frames):
    whole = jnp.concatenate(
        [ref[rows(j, frames), :] for ref in (own, received) for j in range(data // frames)], axis=1
    )
    return whole, jnp.concatenate([jnp.zeros_like(whole), whole], axis=0)


def first_grams_kernel(data, parts, own, received, out_ref):
    n = parts[0].shape[0] // 2
    total = parts[0][...]
    for part in parts[1:]:
        total += part[...]
    out_ref[...] = total
    out_ref[:n, :] += nt_dot(*foot_gram(own, received, data, n))


def second_gram_kernel(data, own, received, out_ref):
    n = out_ref.shape[0]
    whole, padded = foot_gram(own, received, data, n)
    gram = nt_dot(whole, whole)
    out_ref[...] = jnp.concatenate(split(gram), axis=1)


def second_pair_kernel(own, received, gram_ref, out_ref):
    n = own.shape[0]
    both = own[...].astype(F32) + received[...].astype(F32)
    value = both[:, :n] + both[:, n:]
    gram_ref[...] = value
    out_ref[...] = jnp.concatenate(split(value), axis=1)


def forward_kernel(stretch, cols, index, search, blocks, tile, keep_ref, send_ref, acc, panel):
    frames = panel.shape[1]
    me = lax.axis_index("row")
    for flip, ref in enumerate(search):
        fill(panel, ref, lax.bitwise_xor(me, flip), stretch)
    acc[...] = jnp.zeros_like(acc)
    for k in range(blocks.shape[0]):
        acc[index[0, k]] += jnp.dot(panel[index[1, k]], blocks[k], preferred_element_type=F32)
    core = lax.rem(lax.axis_index("col"), 2)
    for x in range(cols // 2):
        for j in range(stretch):
            at = rows(x * stretch + j, frames)
            keep_ref[at, :] = acc[(2 * x + core) * stretch + j]
            send_ref[at, :] = acc[(2 * x + 1 - core) * stretch + j]
    if tile:
        at = cols // 2 * stretch * frames
        keep_ref[at:, :] = tile[0][...]
        send_ref[at:, :] = tile[0][...]


def pair_kernel(data, frames, keep, received, out_ref):
    for j in range(data // frames):
        at = rows(j, frames)
        out_ref[at, :] = (keep[at, :] + received[at, :]).astype(BF16)
    if out_ref.shape[0] > data:
        out_ref[data:, :] = split_tile(keep[data : data + 1, :] + received[data : data + 1, :])


def chips_kernel(data, frames, parts, out_ref):
    for j in range(data // frames):
        at = rows(j, frames)
        out_ref[at, :] = sum_rows(parts, at).astype(BF16)
    if out_ref.shape[0] > data:
        out_ref[data:, :] = split_tile(tile_row(sum_rows(parts, slice(data, data + DIAG))))


def backward_kernel(
    stretch, cols, last, index, own, received, blocks,
    far_refs, near_ref, keep_refs, keep_ref, acc, panel,
):
    frames = panel.shape[1]
    data = cols // 2 * stretch * frames
    fill_foot(panel, own, received, stretch, cols)
    acc[...] = jnp.zeros_like(acc)
    for k in range(blocks.shape[0]):
        acc[index[1, k]] += jnp.dot(panel[index[0, k]], blocks[k], preferred_element_type=F32)
    me = lax.axis_index("row")
    for far, (far_ref, kept_ref) in enumerate(zip(far_refs, keep_refs)):
        shard = lax.bitwise_xor(me, 2 * (far + 1))
        other = lax.bitwise_xor(shard, 1)
        for j in range(stretch):
            kept_ref[rows(j, frames), :] = acc[shard * stretch + j]
            far_ref[rows(j, frames), :] = acc[other * stretch + j].astype(BF16)
    other = lax.bitwise_xor(me, 1)
    for j in range(stretch):
        keep_ref[rows(j, frames), :] = acc[me * stretch + j]
        near_ref[rows(j, frames), :] = acc[other * stretch + j].astype(BF16)
    if not last:
        squares = jnp.zeros((frames, BLOCK), F32)
        for b in range(panel.shape[0]):
            part = panel[b].astype(F32)
            squares += part * part
        energy = as_row(jnp.sum(squares, axis=1, keepdims=True))
        row = tile_row(own[data:, :].astype(F32))
        row += jnp.concatenate([jnp.zeros_like(energy), energy], axis=1)
        far_refs[0][stretch * frames :, :] = split_tile(row)


def rows_kernel(data, frames, sent, received, kept, out_refs):
    for out_ref, kept_ref, received_ref in zip(out_refs, kept, received):
        for j in range(data // frames):
            at = rows(j, frames)
            out_ref[at, :] = (kept_ref[at, :] + received_ref[at, :].astype(F32)).astype(BF16)
    if out_refs[0].shape[0] > data:
        tile = split_tile(tile_row(sum_rows((sent, received[0]), slice(data, data + DIAG))))
        for out_ref in out_refs:
            out_ref[data:, :] = tile


def own_sum(keep, near, far, j, frames):
    at = rows(j, frames)
    return keep[at, :] + sum_rows((near, *far), at)


def frame_shift(diagonal, frames):
    row = 1.25 * diagonal[:, frames:] / diagonal[:, :frames]
    return jnp.sum(jnp.where(eye(frames), row, 0.0), axis=1, keepdims=True), row


def image_kernel(
    keep, near, far, sent, v_ref, prior, image_ref, next_ref, cast_ref, diag_ref
):
    frames = v_ref.shape[0]
    data = cast_ref.shape[0]
    diagonal = tile_row(sum_rows((sent, *far), slice(data, data + DIAG)))
    diag_ref[...] = as_tile(diagonal)
    shift, _ = frame_shift(diagonal, frames)
    for j in range(data // frames):
        value = v_ref[:, lanes(j)]
        image = own_sum(keep, near, far, j, frames) + prior[:, lanes(j)] * value
        following = image - shift * value
        image_ref[:, lanes(j)] = image
        next_ref[:, lanes(j)] = following
        cast_ref[rows(j, frames), :] = following.astype(BF16)


def eliminate(matrix, right, n):
    width = matrix.shape[1] + right.shape[1]
    work = jnp.concatenate([matrix, right], axis=1)
    work = [work[rows(i, TILE), :] for i in range(n // TILE)]
    at = lax.broadcasted_iota(jnp.int32, (TILE, width), 0)

    def column(k):
        return [jnp.broadcast_to(t[:, k : k + 1], (TILE, width)) for t in work]

    def step(tiles, spread, k, pivot):
        i, s = divmod(k, TILE)
        row = tiles[i][s : s + 1, :] * pivot
        done = [t - c * row for t, c in zip(tiles, spread)]
        done[i] = jnp.where(at == s, row, done[i])
        return done

    ahead = [column(k) for k in range(AHEAD)]
    for k in range(n):
        i, s = divmod(k, TILE)
        spread = ahead.pop(0)
        pivot = 1.0 / spread[i][s : s + 1, :]
        ahead = [step(later, spread, k, pivot) for later in ahead]
        work = step(work, spread, k, pivot)
        if k + AHEAD < n:
            ahead.append(column(k + AHEAD))
    return jnp.concatenate(work, axis=0)[:, n:]


def middle_kernel(grams, diag_ref, out_ref):
    n = grams.shape[0] // 2
    norm, energy = grams[:n, :n], grams[:n, n:]
    shift, shift_row = frame_shift(diag_ref[0:1, :], n)
    inverse = eliminate(energy, jnp.where(eye(n), 1.0, 0.0), n)
    next_rhs = energy - shift * norm
    cross = grams[n:, :n] + next_rhs * shift_row
    alpha = nn_dot(inverse, norm)
    conj = nn_dot(inverse, cross.T)
    out_ref[0] = alpha
    out_ref[1] = conj
    out_ref[2] = grams[n:, n:] - nn_dot(cross, conj)
    out_ref[3] = next_rhs - nn_dot(cross, alpha)


def solve_kernel(gram, parts, middle, out_ref):
    n = gram.shape[0]
    schur = gram[...] + middle[2]
    for part in parts:
        both = part[...].astype(F32)
        schur += both[:, :n] + both[:, n:]
    gamma = eliminate(schur, middle[3], n)
    out_ref[:n, :] = middle[0] - nn_dot(middle[1], gamma)
    out_ref[n:, :] = gamma


def final_kernel(keep, near, far, v_ref, image_ref, next_ref, prior, coeffs_ref, x_ref, r_ref):
    n = v_ref.shape[0]
    coeffs = coeffs_ref[...]
    for j in range(keep.shape[0] // n):
        value = v_ref[:, lanes(j)]
        following = next_ref[:, lanes(j)]
        second_image = own_sum(keep, near, far, j, n) + prior[:, lanes(j)] * following
        x_ref[:, lanes(j)] = tn_dot(coeffs, jnp.concatenate([value, following], axis=0))
        r_ref[:, lanes(j)] = value - tn_dot(
            coeffs, jnp.concatenate([image_ref[:, lanes(j)], second_image], axis=0)
        )


def swapped(x, axis, flip):
    return lax.ppermute(x, axis, [(i, i ^ flip) for i in range(lax.axis_size(axis))])


def others(x, axis):
    return (x, *(swapped(x, axis, flip) for flip in range(2, lax.axis_size(axis), 2)))


def gather(x, axis):
    return tuple(part for own in others(x, axis) for part in (own, swapped(own, axis, 1)))


def shards(right_side, prior, blocks, block_row, block_col):
    frames, pix = right_side.shape
    stretch = pix // BLOCK
    n_rows, n_cols = lax.axis_size("row"), lax.axis_size("col")
    row_span, col_span = stretch * n_cols, stretch * n_rows
    prior = prior.reshape(1, pix)
    stored = blocks.shape[0]
    half_cols = n_cols // 2 * stretch * frames

    def shape(dims, dtype=F32):
        return jax.ShapeDtypeStruct(dims, dtype)

    own = shape((frames, pix))
    cast_type = shape((stretch * frames, BLOCK), BF16)
    aside = pl.CostEstimate(flops=2 * 10**9, bytes_accessed=8 * 10**6, transcendentals=0)
    pairs = n_rows // 2 - 1

    def forward(search, tile):
        size = half_cols + (DIAG if tile else 0)
        keep, send = call(
            lambda *refs: forward_kernel(stretch, n_cols, *refs),
            (shape((size, BLOCK)),) * 2,
            (index, search, turned, tile),
            [
                pltpu.VMEM((row_span, frames, BLOCK), F32),
                pltpu.VMEM((col_span, frames, BLOCK), BF16),
            ],
        )
        received = swapped(send, "col", 1)
        (pair,) = call(
            lambda *refs: pair_kernel(half_cols, frames, *refs),
            (shape((size, BLOCK), BF16),),
            (keep, received),
        )
        (foot,) = call(
            lambda *refs: chips_kernel(half_cols, frames, *refs),
            (shape((size, BLOCK), BF16),),
            (others(pair, "col"),),
        )
        return foot, swapped(foot, "col", 1)

    def backward(foot, last):
        size = stretch * frames
        extra = 0 if last else DIAG
        far, near, kept, keep = call(
            lambda *refs: backward_kernel(stretch, n_cols, last, *refs),
            (
                tuple(shape((size + (0 if p else extra), BLOCK), BF16) for p in range(pairs)),
                shape((size, BLOCK), BF16),
                (shape((size, BLOCK)),) * pairs,
                shape((size, BLOCK)),
            ),
            (index, *foot, staged),
            [
                pltpu.VMEM((col_span, frames, BLOCK), F32),
                pltpu.VMEM((row_span, frames, BLOCK), BF16),
            ],
        )
        received = tuple(swapped(x, "row", 1) for x in far)
        near = swapped(near, "row", 1)
        (sums,) = call(
            lambda *refs: rows_kernel(size, frames, *refs),
            ((shape((size + extra, BLOCK), BF16),) * pairs,),
            (far[0], received, kept),
        )
        far = tuple(swapped(x, "row", 2 * (p + 1)) for p, x in enumerate(sums))
        return keep, near, far, sums[0]

    def add(parts):
        return call(add_kernel, (shape(parts[0].shape),), (parts,))[0]

    (cast,) = call(cast_kernel, (cast_type,), (right_side,))
    search = gather(cast, "row")
    index, staged = call(
        lambda *refs: stage_kernel(row_span, stretch, *refs),
        (shape((2, stored), jnp.int32), shape(blocks.shape, BF16)),
        (block_row, block_col, blocks),
        [pltpu.SemaphoreType.DMA],
        specs=[SMEM, SMEM, ANY],
        cost=aside,
    )
    (turned,) = call(turn_kernel, (shape(blocks.shape, BF16),), (staged,), cost=aside)
    (tile,) = call(energy_kernel, (shape((DIAG, 2 * frames)),), (right_side, prior), cost=aside)
    foot = forward(search, (tile,))
    keep, near, far, sent = backward(foot, False)
    image, following, cast, diagonal = call(
        image_kernel,
        (own, own, cast_type, shape((DIAG, 2 * frames))),
        (keep, near, far, sent, right_side, prior),
    )
    search = gather(cast, "row")
    (grams,) = call(
        grams_kernel, (shape((2 * frames,) * 2),), (right_side, following, prior), cost=aside
    )
    grams = add((grams, swapped(grams, "col", 1)))
    (grams,) = call(
        lambda *refs: first_grams_kernel(half_cols, *refs),
        (shape(grams.shape),),
        (others(grams, "col"), *foot),
        cost=aside,
    )
    foot = forward(search, ())
    grams = add((grams, swapped(grams, "row", 1)))
    grams = add(others(grams, "row"))
    (second,) = call(
        lambda *refs: second_gram_kernel(half_cols, *refs),
        (shape((frames, 2 * frames), BF16),),
        foot,
    )
    gram, second = call(
        second_pair_kernel,
        (shape((frames, frames)), shape((frames, 2 * frames), BF16)),
        (second, swapped(second, "row", 1)),
    )
    second = others(second, "row")[1:]
    keep, near, far, _ = backward(foot, True)
    (middle,) = call(middle_kernel, (shape((4, frames, frames)),), (grams, diagonal), cost=aside)
    (coeffs,) = call(
        solve_kernel, (shape((2 * frames, frames)),), (gram, second, middle), cost=aside
    )
    return tuple(
        call(
            final_kernel,
            (own, own),
            (keep, near, far, right_side, image, following, prior, coeffs),
        )
    )


def solution(mesh):
    return jax.shard_map(
        shards,
        mesh=mesh,
        in_specs=(
            P("groups", ("row", "col")),
            P(("row", "col")),
            P(("row", "col"), None, None),
            P(("row", "col")),
            P(("row", "col")),
        ),
        out_specs=(P("groups", ("row", "col")), P("groups", ("row", "col"))),
        check_vma=False,
    )
```

```python
import jax
import jax.numpy as jnp
from jax import lax
from jax.experimental import pallas as pl
from jax.experimental.pallas import tpu as pltpu
from jax.sharding import PartitionSpec as P

BLOCK = 128
TILE = 8
AHEAD = 4
DIAG = 16
F32, BF16 = jnp.float32, jnp.bfloat16
FP32 = lax.Precision.HIGHEST
VMEM = pl.BlockSpec(memory_space=pltpu.VMEM)
SMEM = pl.BlockSpec(memory_space=pltpu.SMEM)


def nt_dot(a, b, precision=None):
    return lax.dot_general(
        a, b, (((1,), (1,)), ((), ())), precision=precision, preferred_element_type=F32
    )


def tn_dot(a, b):
    return lax.dot_general(
        a, b, (((0,), (0,)), ((), ())), precision=FP32, preferred_element_type=F32
    )


def nn_dot(a, b):
    return lax.dot_general(
        a, b, (((1,), (0,)), ((), ())), precision=FP32, preferred_element_type=F32
    )


def call(kernel, outs, ins, scratch=(), cost=None):
    flat_ins, ins_tree = jax.tree.flatten(tuple(ins))
    flat_outs, outs_tree = jax.tree.flatten(tuple(outs))

    def body(*refs):
        middle, last = len(flat_ins), len(flat_ins) + len(flat_outs)
        kernel(
            *jax.tree.unflatten(ins_tree, refs[:middle]),
            *jax.tree.unflatten(outs_tree, refs[middle:last]),
            *refs[last:],
        )

    def space(x):
        return SMEM if x.dtype == jnp.int32 else VMEM

    results = pl.pallas_call(
        body,
        out_shape=flat_outs,
        in_specs=[space(x) for x in flat_ins],
        out_specs=[space(x) for x in flat_outs],
        scratch_shapes=list(scratch),
        compiler_params=pltpu.CompilerParams(vmem_limit_bytes=48 * 1024 * 1024),
        cost_estimate=cost,
    )(*flat_ins)
    return jax.tree.unflatten(outs_tree, results)


def lanes(j):
    return slice(j * BLOCK, (j + 1) * BLOCK)


def rows(j, count):
    return slice(j * count, (j + 1) * count)


def split(value):
    high = value.astype(BF16)
    return high, (value - high.astype(F32)).astype(BF16)


def sum_rows(refs, at):
    total = refs[0][at, :].astype(F32)
    for ref in refs[1:]:
        total += ref[at, :].astype(F32)
    return total


def eye(n):
    return lax.broadcasted_iota(jnp.int32, (n, n), 0) == lax.broadcasted_iota(jnp.int32, (n, n), 1)


def cast_kernel(v_ref, out_ref):
    frames = v_ref.shape[0]
    for j in range(v_ref.shape[1] // BLOCK):
        out_ref[rows(j, frames), :] = v_ref[:, lanes(j)].astype(BF16)


def turn_kernel(row_span, stretch, brow, bcol, blocks, index_ref, out_ref):
    for k in range(blocks.shape[0]):
        index_ref[0, k] = lax.rem(brow[k], row_span)
        index_ref[1, k] = lax.div(bcol[k], row_span) * stretch + lax.rem(bcol[k], stretch)
        out_ref[k] = blocks[k].T


def gram_kernel(v_ref, prior, out_ref):
    value = v_ref[...]
    out_ref[...] = nt_dot(value, jnp.concatenate([value, value * prior[...]], axis=0), FP32)


def fill(panel, ref, at, stretch):
    frames = panel.shape[1]
    for j in range(stretch):
        panel[at * stretch + j] = ref[rows(j, frames), :]


def whole_of(panel):
    return jnp.concatenate([panel[b] for b in range(panel.shape[0])], axis=1)


def forward_kernel(stretch, cols, index, search, blocks, gram, half, keep_ref, send_ref, acc, panel):
    frames = panel.shape[1]
    me = lax.axis_index("row")
    for flip, ref in enumerate(search):
        fill(panel, ref, lax.bitwise_xor(me, flip), stretch)
    acc[...] = jnp.zeros_like(acc)
    for k in range(blocks.shape[0]):
        acc[index[0, k]] += jnp.dot(panel[index[1, k]], blocks[k], preferred_element_type=F32)
    core = lax.rem(lax.axis_index("col"), 2)
    for x in range(cols // 2):
        for j in range(stretch):
            at = rows(x * stretch + j, frames)
            keep_ref[at, :] = acc[(2 * x + core) * stretch + j]
            send_ref[at, :] = acc[(2 * x + 1 - core) * stretch + j]
    at = rows(cols // 2 * stretch, frames)
    value = gram[...]
    if half:
        whole = whole_of(panel)
        inner = nt_dot(whole, jnp.concatenate([whole, jnp.zeros_like(whole)], axis=0))
        lane = lax.broadcasted_iota(jnp.int32, value.shape, 1)
        value = jnp.where(lane < frames, inner, value)
        send_ref[at.stop :, :] = half[0][...]
        keep_ref[at.stop :, :] = half[0][...]
    keep_ref[at, :] = value
    send_ref[at, :] = value


def pair_kernel(frames, keep, received, out_ref, first_refs):
    core = lax.rem(lax.axis_index("col"), 2)
    split_at = frames // 2
    data = out_ref.shape[0] - frames
    for j in range(data // frames):
        at = rows(j, frames)
        out_ref[at, :] = (keep[at, :] + received[at, :]).astype(BF16)
    at = pl.ds(pl.multiple_of(data + core * split_at, split_at), split_at)
    out_ref[data : data + split_at, :], out_ref[data + split_at :, :] = split(
        keep[at, :] + received[at, :]
    )
    if first_refs:
        at = pl.ds(pl.multiple_of(core * split_at, split_at), split_at)
        first_refs[0][at, :] = keep[data + frames :, :]
        at = pl.ds(pl.multiple_of((1 - core) * split_at, split_at), split_at)
        first_refs[0][at, :] = received[data + frames :, :]


def chips_kernel(frames, parts, before, out_ref):
    split_at = frames // 2
    data = out_ref.shape[0] - frames
    for j in range(data // frames):
        at = rows(j, frames)
        out_ref[at, :] = sum_rows(parts, at).astype(BF16)
    high, low = slice(data, data + split_at), slice(data + split_at, data + frames)
    out_ref[high, :], out_ref[low, :] = split(sum_rows(parts, high) + sum_rows(parts, low))


def backward_kernel(
    stretch, cols, last, index, own, received, blocks,
    far_refs, near_ref, keep_refs, keep_ref, norm_refs, acc, panel, gram,
):
    frames = panel.shape[1]
    split_at = frames // 2
    core = lax.rem(lax.axis_index("col"), 2)
    data = cols // 2 * stretch * frames
    for ref, side in ((own, core), (received, 1 - core)):
        for x in range(cols // 2):
            for j in range(stretch):
                panel[(2 * x + side) * stretch + j] = ref[rows(x * stretch + j, frames), :]
    fill_gram(gram, own, received, data, frames)
    acc[...] = jnp.zeros_like(acc)
    for k in range(blocks.shape[0]):
        acc[index[1, k]] += jnp.dot(panel[index[0, k]], blocks[k], preferred_element_type=F32)
    me = lax.axis_index("row")
    for far, (far_ref, kept_ref) in enumerate(zip(far_refs, keep_refs)):
        shard = lax.bitwise_xor(me, 2 * (far + 1))
        other = lax.bitwise_xor(shard, 1)
        for j in range(stretch):
            kept_ref[rows(j, frames), :] = acc[shard * stretch + j]
            far_ref[rows(j, frames), :] = acc[other * stretch + j].astype(BF16)
    other = lax.bitwise_xor(me, 1)
    for j in range(stretch):
        keep_ref[rows(j, frames), :] = acc[me * stretch + j]
        near_ref[rows(j, frames), :] = acc[other * stretch + j].astype(BF16)
    if last:
        norm_refs[0][...] = gram[:, :frames]
        return
    whole = whole_of(panel)
    total = gram[...] + nt_dot(whole, jnp.concatenate([jnp.zeros_like(whole), whole], axis=0))
    at = stretch * frames
    out_ref = far_refs[0]
    gram[...] = total
    out_ref[at : at + split_at, :], out_ref[at + split_at : at + frames, :] = split(
        gram[pl.ds(pl.multiple_of(core * split_at, split_at), split_at), :]
    )
    lane = lax.broadcasted_iota(jnp.int32, total.shape, 1)
    row = lax.broadcasted_iota(jnp.int32, total.shape, 0)
    on_diagonal = jnp.logical_or(lane == row, lane == row + frames)
    diagonal = jnp.sum(jnp.where(on_diagonal, total, 0.0), axis=0, keepdims=True)
    row = lax.broadcasted_iota(jnp.int32, (DIAG, 2 * frames), 0)
    out_ref[at + frames :, :] = jnp.where(row == 0, diagonal, 0.0).astype(BF16)


def rows_kernel(frames, sent, received, kept, before, out_refs, gram_refs):
    split_at = frames // 2
    data = kept[0].shape[0]
    for out_ref, kept_ref, received_ref in zip(out_refs, kept, received):
        for j in range(data // frames):
            at = rows(j, frames)
            out_ref[at, :] = (kept_ref[at, :] + received_ref[at, :].astype(F32)).astype(BF16)
    if gram_refs:
        pair = (sent, received[0])
        high, low = slice(data, data + split_at), slice(data + split_at, data + frames)
        value = sum_rows(pair, high) + sum_rows(pair, low)
        block = jnp.concatenate(split(value), axis=0)
        tile = sum_rows(pair, slice(data + frames, data + frames + DIAG)).astype(BF16)
        gram_refs[0][...] = value
        gram_refs[1][...] = tile
        for out_ref in out_refs:
            out_ref[data : data + frames, :] = block
            out_ref[data + frames :, :] = tile


def fill_gram(gram, own, received, data, frames):
    split_at = frames // 2
    core = lax.rem(lax.axis_index("col"), 2)
    for ref, side in ((own, core), (received, 1 - core)):
        at = pl.ds(pl.multiple_of(side * split_at, split_at), split_at)
        gram[at, :] = ref[data : data + split_at, :].astype(F32) + ref[data + split_at :, :].astype(
            F32
        )


def second_gram_kernel(data, own, received, out_ref, gram):
    frames = out_ref.shape[0]
    fill_gram(gram, own, received, data, frames)
    whole = jnp.concatenate(
        [ref[rows(j, frames), :] for ref in (own, received) for j in range(data // frames)], axis=1
    )
    value = gram[:, frames:] + nt_dot(whole, whole)
    out_ref[...] = jnp.concatenate(split(value), axis=1)


def second_pair_kernel(own, received, gram_ref, out_ref):
    n = own.shape[0]
    both = own[...].astype(F32) + received[...].astype(F32)
    value = both[:, :n] + both[:, n:]
    gram_ref[...] = value
    out_ref[...] = jnp.concatenate(split(value), axis=1)


def own_sum(keep, near, far, j, frames):
    at = rows(j, frames)
    return keep[at, :] + sum_rows((near, *far), at)


def frame_shift(diagonal, frames):
    row = 1.25 * diagonal[:, frames:] / diagonal[:, :frames]
    return jnp.sum(jnp.where(eye(frames), row, 0.0), axis=1, keepdims=True), row


def image_kernel(
    keep, near, far, gram, tile, v_ref, prior, image_ref, next_ref, cast_ref, half_ref, diag_ref
):
    frames = v_ref.shape[0]
    split_at = frames // 2
    data = cast_ref.shape[0]
    diagonal = tile[...].astype(F32) + sum_rows(far, slice(data + frames, data + frames + DIAG))
    diag_ref[...] = diagonal
    shift, _ = frame_shift(diagonal[0:1, :], frames)
    for j in range(data // frames):
        value = v_ref[:, lanes(j)]
        image = own_sum(keep, near, far, j, frames) + prior[:, lanes(j)] * value
        following = image - shift * value
        image_ref[:, lanes(j)] = image
        next_ref[:, lanes(j)] = following
        cast_ref[rows(j, frames), :] = following.astype(BF16)
    half_ref[...] = (
        gram[...]
        + sum_rows(far, slice(data, data + split_at))
        + sum_rows(far, slice(data + split_at, data + frames))
    )


def eliminate(matrix, right, n):
    width = matrix.shape[1] + right.shape[1]
    work = jnp.concatenate([matrix, right], axis=1)
    work = [work[rows(i, TILE), :] for i in range(n // TILE)]
    at = lax.broadcasted_iota(jnp.int32, (TILE, width), 0)

    def column(k):
        return [jnp.broadcast_to(t[:, k : k + 1], (TILE, width)) for t in work]

    def step(tiles, spread, k, pivot):
        i, s = divmod(k, TILE)
        row = tiles[i][s : s + 1, :] * pivot
        done = [t - c * row for t, c in zip(tiles, spread)]
        done[i] = jnp.where(at == s, row, done[i])
        return done

    ahead = [column(k) for k in range(AHEAD)]
    for k in range(n):
        i, s = divmod(k, TILE)
        spread = ahead.pop(0)
        pivot = 1.0 / spread[i][s : s + 1, :]
        ahead = [step(later, spread, k, pivot) for later in ahead]
        work = step(work, spread, k, pivot)
        if k + AHEAD < n:
            ahead.append(column(k + AHEAD))
    return jnp.concatenate(work, axis=0)[:, n:]


def inverse_kernel(first, out_ref):
    n = first.shape[0]
    out_ref[...] = eliminate(first[:, n:], jnp.where(eye(n), 1.0, 0.0), n)


def middle_kernel(first, inverse_ref, norm_ref, diag_ref, out_ref):
    n = first.shape[0]
    norm, energy = first[:, :n], first[:, n:]
    shift, shift_row = frame_shift(diag_ref[0:1, :], n)
    inverse = inverse_ref[...]
    next_rhs = energy - shift * norm
    cross = norm_ref[...] + next_rhs * shift_row
    alpha = nn_dot(inverse, norm)
    conj = nn_dot(inverse, cross.T)
    out_ref[0] = alpha
    out_ref[1] = conj
    out_ref[2] = nn_dot(cross, conj)
    out_ref[3] = next_rhs - nn_dot(cross, alpha)


def solve_kernel(gram, parts, middle, out_ref):
    n = gram.shape[0]
    schur = gram[...] - middle[2]
    for part in parts:
        both = part[...].astype(F32)
        schur += both[:, :n] + both[:, n:]
    gamma = eliminate(schur, middle[3], n)
    out_ref[:n, :] = middle[0] - nn_dot(middle[1], gamma)
    out_ref[n:, :] = gamma


def final_kernel(keep, near, far, v_ref, image_ref, next_ref, prior, coeffs_ref, x_ref, r_ref):
    n = v_ref.shape[0]
    coeffs = coeffs_ref[...]
    for j in range(keep.shape[0] // n):
        value = v_ref[:, lanes(j)]
        following = next_ref[:, lanes(j)]
        second_image = own_sum(keep, near, far, j, n) + prior[:, lanes(j)] * following
        x_ref[:, lanes(j)] = tn_dot(coeffs, jnp.concatenate([value, following], axis=0))
        r_ref[:, lanes(j)] = value - tn_dot(
            coeffs, jnp.concatenate([image_ref[:, lanes(j)], second_image], axis=0)
        )


def swapped(x, axis, flip):
    return lax.ppermute(x, axis, [(i, i ^ flip) for i in range(lax.axis_size(axis))])


def others(x, axis):
    return (x, *(swapped(x, axis, flip) for flip in range(2, lax.axis_size(axis), 2)))


def gather(x, axis):
    return tuple(part for own in others(x, axis) for part in (own, swapped(own, axis, 1)))


def shards(right_side, prior, blocks, block_row, block_col):
    frames, pix = right_side.shape
    stretch = pix // BLOCK
    n_rows, n_cols = lax.axis_size("row"), lax.axis_size("col")
    row_span, col_span = stretch * n_cols, stretch * n_rows
    prior = prior.reshape(1, pix)
    stored = blocks.shape[0]
    half_cols = n_cols // 2 * stretch * frames

    def shape(dims, dtype=F32):
        return jax.ShapeDtypeStruct(dims, dtype)

    own = shape((frames, pix))
    gram_type = shape((frames, 2 * frames))
    cast_type = shape((stretch * frames, BLOCK), BF16)
    aside = pl.CostEstimate(flops=2 * 10**9, bytes_accessed=8 * 10**6, transcendentals=0)

    pairs = n_rows // 2 - 1

    def forward(search, gram, half):
        size = half_cols + frames + (frames // 2 if half else 0)
        keep, send = call(
            lambda *refs: forward_kernel(stretch, n_cols, *refs),
            (shape((size, BLOCK)),) * 2,
            (index, search, turned, gram, half),
            [
                pltpu.VMEM((row_span, frames, BLOCK), F32),
                pltpu.VMEM((col_span, frames, BLOCK), BF16),
            ],
        )
        received = swapped(send, "col", 1)
        pair, first = call(
            lambda *refs: pair_kernel(frames, *refs),
            (shape((half_cols + frames, BLOCK), BF16), (gram_type,) if half else ()),
            (keep, received),
        )
        inverse = call(inverse_kernel, (shape((frames, frames)),), first, cost=aside) if half else ()
        (foot,) = call(
            lambda *refs: chips_kernel(frames, *refs),
            (shape((half_cols + frames, BLOCK), BF16),),
            (others(pair, "col"), inverse),
        )
        return (foot, swapped(foot, "col", 1)), (*first, *inverse)

    def backward(foot, last):
        size = stretch * frames
        extra = 0 if last else frames + DIAG
        far, near, kept, keep, norm = call(
            lambda *refs: backward_kernel(stretch, n_cols, last, *refs),
            (
                tuple(shape((size + (0 if p else extra), BLOCK), BF16) for p in range(pairs)),
                shape((size, BLOCK), BF16),
                (shape((size, BLOCK)),) * pairs,
                shape((size, BLOCK)),
                (shape((frames, frames)),) if last else (),
            ),
            (index, *foot, blocks),
            [
                pltpu.VMEM((col_span, frames, BLOCK), F32),
                pltpu.VMEM((row_span, frames, BLOCK), BF16),
                pltpu.VMEM((frames, 2 * frames), F32),
            ],
        )
        received = tuple(swapped(x, "row", 1) for x in far)
        near = swapped(near, "row", 1)
        middle = ()
        if last:
            middle = call(
                middle_kernel,
                (shape((4, frames, frames)),),
                (first, inverse, *norm, diagonal),
                cost=aside,
            )
        sums, gram = call(
            lambda *refs: rows_kernel(frames, *refs),
            (
                (shape((size + extra, BLOCK), BF16),) * pairs,
                ()
                if last
                else (shape((frames // 2, 2 * frames)), shape((DIAG, 2 * frames), BF16)),
            ),
            (far[0], received, kept, middle),
        )
        far = tuple(swapped(x, "row", 2 * (p + 1)) for p, x in enumerate(sums))
        return (keep, near, far, *gram), middle

    (cast,) = call(cast_kernel, (cast_type,), (right_side,))
    search = gather(cast, "row")
    index, turned = call(
        lambda *refs: turn_kernel(row_span, stretch, *refs),
        (shape((2, stored), jnp.int32), shape(blocks.shape, BF16)),
        (block_row, block_col, blocks),
        cost=aside,
    )
    (gram,) = call(gram_kernel, (gram_type,), (right_side, prior), cost=aside)
    foot, _ = forward(search, gram, ())
    parts, _ = backward(foot, False)
    image, following, cast, half, diagonal = call(
        image_kernel,
        (own, own, cast_type, shape((frames // 2, 2 * frames)), shape((DIAG, 2 * frames))),
        (*parts, right_side, prior),
    )
    search = gather(cast, "row")
    (gram,) = call(gram_kernel, (gram_type,), (following, prior), cost=aside)
    foot, (first, inverse) = forward(search, gram, (half,))
    (second,) = call(
        lambda *refs: second_gram_kernel(half_cols, *refs),
        (shape((frames, 2 * frames), BF16),),
        foot,
        [pltpu.VMEM((frames, 2 * frames), F32)],
    )
    gram, second = call(
        second_pair_kernel,
        (shape((frames, frames)), shape((frames, 2 * frames), BF16)),
        (second, swapped(second, "row", 1)),
    )
    second = others(second, "row")[1:]
    parts, middle = backward(foot, True)
    (coeffs,) = call(
        solve_kernel, (shape((2 * frames, frames)),), (gram, second, *middle), cost=aside
    )
    return tuple(
        call(
            final_kernel,
            (own, own),
            (*parts, right_side, image, following, prior, coeffs),
        )
    )


def solution(mesh):
    return jax.shard_map(
        shards,
        mesh=mesh,
        in_specs=(
            P("groups", ("row", "col")),
            P(("row", "col")),
            P(("row", "col"), None, None),
            P(("row", "col")),
            P(("row", "col")),
        ),
        out_specs=(P("groups", ("row", "col")), P("groups", ("row", "col"))),
        check_vma=False,
    )
```

```python
import jax
import jax.numpy as jnp
from jax import lax
from jax.experimental import pallas as pl
from jax.experimental.pallas import tpu as pltpu
from jax.sharding import PartitionSpec as P

BLOCK = 128
TILE = 8
AHEAD = 4
DIAG = 16
F32, BF16 = jnp.float32, jnp.bfloat16
FP32 = lax.Precision.HIGHEST
VMEM = pl.BlockSpec(memory_space=pltpu.VMEM)
SMEM = pl.BlockSpec(memory_space=pltpu.SMEM)


def nt_dot(a, b, precision=None):
    return lax.dot_general(
        a, b, (((1,), (1,)), ((), ())), precision=precision, preferred_element_type=F32
    )


def tn_dot(a, b):
    return lax.dot_general(
        a, b, (((0,), (0,)), ((), ())), precision=FP32, preferred_element_type=F32
    )


def nn_dot(a, b):
    return lax.dot_general(
        a, b, (((1,), (0,)), ((), ())), precision=FP32, preferred_element_type=F32
    )


def call(kernel, outs, ins, scratch=(), cost=None):
    flat_ins, ins_tree = jax.tree.flatten(tuple(ins))
    flat_outs, outs_tree = jax.tree.flatten(tuple(outs))

    def body(*refs):
        middle, last = len(flat_ins), len(flat_ins) + len(flat_outs)
        kernel(
            *jax.tree.unflatten(ins_tree, refs[:middle]),
            *jax.tree.unflatten(outs_tree, refs[middle:last]),
            *refs[last:],
        )

    def space(x):
        return SMEM if x.dtype == jnp.int32 else VMEM

    results = pl.pallas_call(
        body,
        out_shape=flat_outs,
        in_specs=[space(x) for x in flat_ins],
        out_specs=[space(x) for x in flat_outs],
        scratch_shapes=list(scratch),
        compiler_params=pltpu.CompilerParams(vmem_limit_bytes=48 * 1024 * 1024),
        cost_estimate=cost,
    )(*flat_ins)
    return jax.tree.unflatten(outs_tree, results)


def lanes(j):
    return slice(j * BLOCK, (j + 1) * BLOCK)


def rows(j, count):
    return slice(j * count, (j + 1) * count)


def split(value):
    high = value.astype(BF16)
    return high, (value - high.astype(F32)).astype(BF16)


def sum_rows(refs, at):
    total = refs[0][at, :].astype(F32)
    for ref in refs[1:]:
        total += ref[at, :].astype(F32)
    return total


def eye(n):
    return lax.broadcasted_iota(jnp.int32, (n, n), 0) == lax.broadcasted_iota(jnp.int32, (n, n), 1)


def cast_kernel(v_ref, out_ref):
    frames = v_ref.shape[0]
    for j in range(v_ref.shape[1] // BLOCK):
        out_ref[rows(j, frames), :] = v_ref[:, lanes(j)].astype(BF16)


def turn_kernel(row_span, stretch, brow, bcol, blocks, index_ref, out_ref):
    for k in range(blocks.shape[0]):
        index_ref[0, k] = lax.rem(brow[k], row_span)
        index_ref[1, k] = lax.div(bcol[k], row_span) * stretch + lax.rem(bcol[k], stretch)
        out_ref[k] = blocks[k].T


def gram_kernel(v_ref, prior, out_ref):
    value = v_ref[...]
    out_ref[...] = nt_dot(value, jnp.concatenate([value, value * prior[...]], axis=0), FP32)


def fill(panel, ref, at, stretch):
    frames = panel.shape[1]
    for j in range(stretch):
        panel[at * stretch + j] = ref[rows(j, frames), :]


def whole_of(panel):
    return jnp.concatenate([panel[b] for b in range(panel.shape[0])], axis=1)


def forward_kernel(stretch, cols, index, search, blocks, gram, half, keep_ref, send_ref, acc, panel):
    frames = panel.shape[1]
    me = lax.axis_index("row")
    for flip, ref in enumerate(search):
        fill(panel, ref, lax.bitwise_xor(me, flip), stretch)
    acc[...] = jnp.zeros_like(acc)
    for k in range(blocks.shape[0]):
        acc[index[0, k]] += jnp.dot(panel[index[1, k]], blocks[k], preferred_element_type=F32)
    core = lax.rem(lax.axis_index("col"), 2)
    for x in range(cols // 2):
        for j in range(stretch):
            at = rows(x * stretch + j, frames)
            keep_ref[at, :] = acc[(2 * x + core) * stretch + j]
            send_ref[at, :] = acc[(2 * x + 1 - core) * stretch + j]
    at = rows(cols // 2 * stretch, frames)
    value = gram[...]
    if half:
        whole = whole_of(panel)
        inner = nt_dot(whole, jnp.concatenate([whole, jnp.zeros_like(whole)], axis=0))
        lane = lax.broadcasted_iota(jnp.int32, value.shape, 1)
        value = jnp.where(lane < frames, inner, value)
        send_ref[at.stop :, :] = half[0][...]
        keep_ref[at.stop :, :] = half[0][...]
    keep_ref[at, :] = value
    send_ref[at, :] = value


def pair_kernel(frames, keep, received, out_ref, first_refs):
    core = lax.rem(lax.axis_index("col"), 2)
    split_at = frames // 2
    data = out_ref.shape[0] - frames
    for j in range(data // frames):
        at = rows(j, frames)
        out_ref[at, :] = (keep[at, :] + received[at, :]).astype(BF16)
    at = pl.ds(pl.multiple_of(data + core * split_at, split_at), split_at)
    out_ref[data : data + split_at, :], out_ref[data + split_at :, :] = split(
        keep[at, :] + received[at, :]
    )
    if first_refs:
        at = pl.ds(pl.multiple_of(core * split_at, split_at), split_at)
        first_refs[0][at, :] = keep[data + frames :, :]
        at = pl.ds(pl.multiple_of((1 - core) * split_at, split_at), split_at)
        first_refs[0][at, :] = received[data + frames :, :]


def chips_kernel(frames, parts, before, out_ref):
    split_at = frames // 2
    data = out_ref.shape[0] - frames
    for j in range(data // frames):
        at = rows(j, frames)
        out_ref[at, :] = sum_rows(parts, at).astype(BF16)
    high, low = slice(data, data + split_at), slice(data + split_at, data + frames)
    out_ref[high, :], out_ref[low, :] = split(sum_rows(parts, high) + sum_rows(parts, low))


def backward_kernel(
    stretch, cols, last, index, own, received, blocks,
    far_refs, keep_ref, last_refs, acc, panel, gram,
):
    frames = panel.shape[1]
    split_at = frames // 2
    core = lax.rem(lax.axis_index("col"), 2)
    data = cols // 2 * stretch * frames
    for ref, side in ((own, core), (received, 1 - core)):
        for x in range(cols // 2):
            for j in range(stretch):
                panel[(2 * x + side) * stretch + j] = ref[rows(x * stretch + j, frames), :]
    fill_gram(gram, own, received, data, frames)
    acc[...] = jnp.zeros_like(acc)
    for k in range(blocks.shape[0]):
        acc[index[1, k]] += jnp.dot(panel[index[0, k]], blocks[k], preferred_element_type=F32)
    me = lax.axis_index("row")
    for j in range(stretch):
        keep_ref[rows(j, frames), :] = acc[me * stretch + j]
    if last:
        for at, far_ref in enumerate(far_refs):
            shard = lax.bitwise_xor(me, len(far_refs) - at)
            for j in range(stretch):
                far_ref[rows(j, frames), :] = acc[shard * stretch + j].astype(BF16)
        last_refs[0][...] = gram[:, :frames]
        return
    near_ref, keep_refs = last_refs
    for far, (far_ref, kept_ref) in enumerate(zip(far_refs, keep_refs)):
        shard = lax.bitwise_xor(me, 2 * (far + 1))
        other = lax.bitwise_xor(shard, 1)
        for j in range(stretch):
            kept_ref[rows(j, frames), :] = acc[shard * stretch + j]
            far_ref[rows(j, frames), :] = acc[other * stretch + j].astype(BF16)
    other = lax.bitwise_xor(me, 1)
    for j in range(stretch):
        near_ref[rows(j, frames), :] = acc[other * stretch + j].astype(BF16)
    whole = whole_of(panel)
    total = gram[...] + nt_dot(whole, jnp.concatenate([jnp.zeros_like(whole), whole], axis=0))
    at = stretch * frames
    out_ref = far_refs[0]
    gram[...] = total
    out_ref[at : at + split_at, :], out_ref[at + split_at : at + frames, :] = split(
        gram[pl.ds(pl.multiple_of(core * split_at, split_at), split_at), :]
    )
    lane = lax.broadcasted_iota(jnp.int32, total.shape, 1)
    row = lax.broadcasted_iota(jnp.int32, total.shape, 0)
    on_diagonal = jnp.logical_or(lane == row, lane == row + frames)
    diagonal = jnp.sum(jnp.where(on_diagonal, total, 0.0), axis=0, keepdims=True)
    row = lax.broadcasted_iota(jnp.int32, (DIAG, 2 * frames), 0)
    out_ref[at + frames :, :] = jnp.where(row == 0, diagonal, 0.0).astype(BF16)


def rows_kernel(frames, sent, received, kept, out_refs, gram_ref, tile_ref):
    split_at = frames // 2
    data = kept[0].shape[0]
    for out_ref, kept_ref, received_ref in zip(out_refs, kept, received):
        for j in range(data // frames):
            at = rows(j, frames)
            out_ref[at, :] = (kept_ref[at, :] + received_ref[at, :].astype(F32)).astype(BF16)
    pair = (sent, received[0])
    high, low = slice(data, data + split_at), slice(data + split_at, data + frames)
    value = sum_rows(pair, high) + sum_rows(pair, low)
    block = jnp.concatenate(split(value), axis=0)
    tile = sum_rows(pair, slice(data + frames, data + frames + DIAG)).astype(BF16)
    gram_ref[...] = value
    tile_ref[...] = tile
    for out_ref in out_refs:
        out_ref[data : data + frames, :] = block
        out_ref[data + frames :, :] = tile


def fill_gram(gram, own, received, data, frames):
    split_at = frames // 2
    core = lax.rem(lax.axis_index("col"), 2)
    for ref, side in ((own, core), (received, 1 - core)):
        at = pl.ds(pl.multiple_of(side * split_at, split_at), split_at)
        gram[at, :] = ref[data : data + split_at, :].astype(F32) + ref[data + split_at :, :].astype(
            F32
        )


def second_gram_kernel(data, own, received, out_ref, gram):
    frames = out_ref.shape[0]
    fill_gram(gram, own, received, data, frames)
    whole = jnp.concatenate(
        [ref[rows(j, frames), :] for ref in (own, received) for j in range(data // frames)], axis=1
    )
    value = gram[:, frames:] + nt_dot(whole, whole)
    out_ref[...] = jnp.concatenate(split(value), axis=1)


def second_pair_kernel(own, received, gram_ref, out_ref):
    n = own.shape[0]
    both = own[...].astype(F32) + received[...].astype(F32)
    value = both[:, :n] + both[:, n:]
    gram_ref[...] = value
    out_ref[...] = jnp.concatenate(split(value), axis=1)


def own_sum(keep, parts, j, frames):
    at = rows(j, frames)
    return keep[at, :] + sum_rows(parts, at)


def frame_shift(diagonal, frames):
    row = 1.25 * diagonal[:, frames:] / diagonal[:, :frames]
    return jnp.sum(jnp.where(eye(frames), row, 0.0), axis=1, keepdims=True), row


def image_kernel(
    keep, near, far, gram, tile, v_ref, prior, image_ref, next_ref, cast_ref, half_ref, diag_ref
):
    frames = v_ref.shape[0]
    split_at = frames // 2
    data = cast_ref.shape[0]
    diagonal = tile[...].astype(F32) + sum_rows(far, slice(data + frames, data + frames + DIAG))
    diag_ref[...] = diagonal
    shift, _ = frame_shift(diagonal[0:1, :], frames)
    for j in range(data // frames):
        value = v_ref[:, lanes(j)]
        image = own_sum(keep, (near, *far), j, frames) + prior[:, lanes(j)] * value
        following = image - shift * value
        image_ref[:, lanes(j)] = image
        next_ref[:, lanes(j)] = following
        cast_ref[rows(j, frames), :] = following.astype(BF16)
    half_ref[...] = (
        gram[...]
        + sum_rows(far, slice(data, data + split_at))
        + sum_rows(far, slice(data + split_at, data + frames))
    )


def eliminate(matrix, right, n):
    width = matrix.shape[1] + right.shape[1]
    work = jnp.concatenate([matrix, right], axis=1)
    work = [work[rows(i, TILE), :] for i in range(n // TILE)]
    at = lax.broadcasted_iota(jnp.int32, (TILE, width), 0)

    def column(k):
        return [jnp.broadcast_to(t[:, k : k + 1], (TILE, width)) for t in work]

    def step(tiles, spread, k, pivot):
        i, s = divmod(k, TILE)
        row = tiles[i][s : s + 1, :] * pivot
        done = [t - c * row for t, c in zip(tiles, spread)]
        done[i] = jnp.where(at == s, row, done[i])
        return done

    ahead = [column(k) for k in range(AHEAD)]
    for k in range(n):
        i, s = divmod(k, TILE)
        spread = ahead.pop(0)
        pivot = 1.0 / spread[i][s : s + 1, :]
        ahead = [step(later, spread, k, pivot) for later in ahead]
        work = step(work, spread, k, pivot)
        if k + AHEAD < n:
            ahead.append(column(k + AHEAD))
    return jnp.concatenate(work, axis=0)[:, n:]


def inverse_kernel(first, out_ref):
    n = first.shape[0]
    out_ref[...] = eliminate(first[:, n:], jnp.where(eye(n), 1.0, 0.0), n)


def middle_kernel(first, inverse_ref, norm_ref, diag_ref, out_ref):
    n = first.shape[0]
    norm, energy = first[:, :n], first[:, n:]
    shift, shift_row = frame_shift(diag_ref[0:1, :], n)
    inverse = inverse_ref[...]
    next_rhs = energy - shift * norm
    cross = norm_ref[...] + next_rhs * shift_row
    alpha = nn_dot(inverse, norm)
    conj = nn_dot(inverse, cross.T)
    out_ref[0] = alpha
    out_ref[1] = conj
    out_ref[2] = nn_dot(cross, conj)
    out_ref[3] = next_rhs - nn_dot(cross, alpha)


def solve_kernel(gram, parts, middle, out_ref):
    n = gram.shape[0]
    schur = gram[...] - middle[2]
    for part in parts:
        both = part[...].astype(F32)
        schur += both[:, :n] + both[:, n:]
    gamma = eliminate(schur, middle[3], n)
    out_ref[:n, :] = middle[0] - nn_dot(middle[1], gamma)
    out_ref[n:, :] = gamma


def final_kernel(keep, parts, v_ref, image_ref, next_ref, prior, coeffs_ref, x_ref, r_ref):
    n = v_ref.shape[0]
    coeffs = coeffs_ref[...]
    for j in range(keep.shape[0] // n):
        value = v_ref[:, lanes(j)]
        following = next_ref[:, lanes(j)]
        second_image = own_sum(keep, parts, j, n) + prior[:, lanes(j)] * following
        x_ref[:, lanes(j)] = tn_dot(coeffs, jnp.concatenate([value, following], axis=0))
        r_ref[:, lanes(j)] = value - tn_dot(
            coeffs, jnp.concatenate([image_ref[:, lanes(j)], second_image], axis=0)
        )


def swapped(x, axis, flip):
    return lax.ppermute(x, axis, [(i, i ^ flip) for i in range(lax.axis_size(axis))])


def others(x, axis):
    return (x, *(swapped(x, axis, flip) for flip in range(2, lax.axis_size(axis), 2)))


def gather(x, axis):
    return tuple(part for own in others(x, axis) for part in (own, swapped(own, axis, 1)))


def shards(right_side, prior, blocks, block_row, block_col):
    frames, pix = right_side.shape
    stretch = pix // BLOCK
    n_rows, n_cols = lax.axis_size("row"), lax.axis_size("col")
    row_span, col_span = stretch * n_cols, stretch * n_rows
    prior = prior.reshape(1, pix)
    stored = blocks.shape[0]
    half_cols = n_cols // 2 * stretch * frames

    def shape(dims, dtype=F32):
        return jax.ShapeDtypeStruct(dims, dtype)

    own = shape((frames, pix))
    gram_type = shape((frames, 2 * frames))
    cast_type = shape((stretch * frames, BLOCK), BF16)
    aside = pl.CostEstimate(flops=2 * 10**9, bytes_accessed=8 * 10**6, transcendentals=0)

    pairs = n_rows // 2 - 1

    def forward(search, gram, half):
        size = half_cols + frames + (frames // 2 if half else 0)
        keep, send = call(
            lambda *refs: forward_kernel(stretch, n_cols, *refs),
            (shape((size, BLOCK)),) * 2,
            (index, search, turned, gram, half),
            [
                pltpu.VMEM((row_span, frames, BLOCK), F32),
                pltpu.VMEM((col_span, frames, BLOCK), BF16),
            ],
        )
        received = swapped(send, "col", 1)
        pair, first = call(
            lambda *refs: pair_kernel(frames, *refs),
            (shape((half_cols + frames, BLOCK), BF16), (gram_type,) if half else ()),
            (keep, received),
        )
        inverse = call(inverse_kernel, (shape((frames, frames)),), first, cost=aside) if half else ()
        (foot,) = call(
            lambda *refs: chips_kernel(frames, *refs),
            (shape((half_cols + frames, BLOCK), BF16),),
            (others(pair, "col"), inverse),
        )
        return (foot, swapped(foot, "col", 1)), (*first, *inverse)

    size = stretch * frames
    small = frames + DIAG

    def backward(foot, outs):
        return call(
            lambda *refs: backward_kernel(stretch, n_cols, len(outs[2]) == 1, *refs),
            outs,
            (index, *foot, blocks),
            [
                pltpu.VMEM((col_span, frames, BLOCK), F32),
                pltpu.VMEM((row_span, frames, BLOCK), BF16),
                pltpu.VMEM((frames, 2 * frames), F32),
            ],
        )

    (cast,) = call(cast_kernel, (cast_type,), (right_side,))
    search = gather(cast, "row")
    index, turned = call(
        lambda *refs: turn_kernel(row_span, stretch, *refs),
        (shape((2, stored), jnp.int32), shape(blocks.shape, BF16)),
        (block_row, block_col, blocks),
        cost=aside,
    )
    (gram,) = call(gram_kernel, (gram_type,), (right_side, prior), cost=aside)
    foot, _ = forward(search, gram, ())
    far, keep, (near, kept) = backward(
        foot,
        (
            tuple(shape((size + (0 if p else small), BLOCK), BF16) for p in range(pairs)),
            shape((size, BLOCK)),
            (shape((size, BLOCK), BF16), (shape((size, BLOCK)),) * pairs),
        ),
    )
    received = tuple(swapped(x, "row", 1) for x in far)
    near = swapped(near, "row", 1)
    sums, gram, tile = call(
        lambda *refs: rows_kernel(frames, *refs),
        (
            (shape((size + small, BLOCK), BF16),) * pairs,
            shape((frames // 2, 2 * frames)),
            shape((DIAG, 2 * frames), BF16),
        ),
        (far[0], received, kept),
    )
    far = tuple(swapped(x, "row", 2 * (p + 1)) for p, x in enumerate(sums))
    image, following, cast, half, diagonal = call(
        image_kernel,
        (own, own, cast_type, shape((frames // 2, 2 * frames)), shape((DIAG, 2 * frames))),
        (keep, near, far, gram, tile, right_side, prior),
    )
    search = gather(cast, "row")
    (gram,) = call(gram_kernel, (gram_type,), (following, prior), cost=aside)
    foot, (first, inverse) = forward(search, gram, (half,))
    (second,) = call(
        lambda *refs: second_gram_kernel(half_cols, *refs),
        (shape((frames, 2 * frames), BF16),),
        foot,
        [pltpu.VMEM((frames, 2 * frames), F32)],
    )
    gram, second = call(
        second_pair_kernel,
        (shape((frames, frames)), shape((frames, 2 * frames), BF16)),
        (second, swapped(second, "row", 1)),
    )
    second = others(second, "row")[1:]
    parts, keep, (norm,) = backward(
        foot,
        (
            (shape((size, BLOCK), BF16),) * (n_rows - 1),
            shape((size, BLOCK)),
            (shape((frames, frames)),),
        ),
    )
    parts = tuple(swapped(x, "row", n_rows - 1 - at) for at, x in enumerate(parts))
    (middle,) = call(
        middle_kernel,
        (shape((4, frames, frames)),),
        (first, inverse, norm, diagonal),
        cost=aside,
    )
    (coeffs,) = call(
        solve_kernel, (shape((2 * frames, frames)),), (gram, second, middle), cost=aside
    )
    return tuple(
        call(
            final_kernel,
            (own, own),
            (keep, parts, right_side, image, following, prior, coeffs),
        )
    )


def solution(mesh):
    return jax.shard_map(
        shards,
        mesh=mesh,
        in_specs=(
            P("groups", ("row", "col")),
            P(("row", "col")),
            P(("row", "col"), None, None),
            P(("row", "col")),
            P(("row", "col")),
        ),
        out_specs=(P("groups", ("row", "col")), P("groups", ("row", "col"))),
        check_vma=False,
    )
```

```python
import jax
import jax.numpy as jnp
from jax import lax
from jax.experimental import pallas as pl
from jax.experimental.pallas import tpu as pltpu
from jax.sharding import PartitionSpec as P

BLOCK = 128
TILE = 8
AHEAD = 4
DIAG = 16
F32, BF16 = jnp.float32, jnp.bfloat16
FP32 = lax.Precision.HIGHEST
VMEM = pl.BlockSpec(memory_space=pltpu.VMEM)
SMEM = pl.BlockSpec(memory_space=pltpu.SMEM)


def nt_dot(a, b, precision=None):
    return lax.dot_general(
        a, b, (((1,), (1,)), ((), ())), precision=precision, preferred_element_type=F32
    )


def tn_dot(a, b):
    return lax.dot_general(
        a, b, (((0,), (0,)), ((), ())), precision=FP32, preferred_element_type=F32
    )


def nn_dot(a, b):
    return lax.dot_general(
        a, b, (((1,), (0,)), ((), ())), precision=FP32, preferred_element_type=F32
    )


def call(kernel, outs, ins, scratch=(), cost=None):
    flat_ins, ins_tree = jax.tree.flatten(tuple(ins))
    flat_outs, outs_tree = jax.tree.flatten(tuple(outs))

    def body(*refs):
        middle, last = len(flat_ins), len(flat_ins) + len(flat_outs)
        kernel(
            *jax.tree.unflatten(ins_tree, refs[:middle]),
            *jax.tree.unflatten(outs_tree, refs[middle:last]),
            *refs[last:],
        )

    def space(x):
        return SMEM if x.dtype == jnp.int32 else VMEM

    results = pl.pallas_call(
        body,
        out_shape=flat_outs,
        in_specs=[space(x) for x in flat_ins],
        out_specs=[space(x) for x in flat_outs],
        scratch_shapes=list(scratch),
        compiler_params=pltpu.CompilerParams(vmem_limit_bytes=48 * 1024 * 1024),
        cost_estimate=cost,
    )(*flat_ins)
    return jax.tree.unflatten(outs_tree, results)


def lanes(j):
    return slice(j * BLOCK, (j + 1) * BLOCK)


def rows(j, count):
    return slice(j * count, (j + 1) * count)


def split(value):
    high = value.astype(BF16)
    return high, (value - high.astype(F32)).astype(BF16)


def sum_rows(refs, at):
    total = refs[0][at, :].astype(F32)
    for ref in refs[1:]:
        total += ref[at, :].astype(F32)
    return total


def eye(n):
    return lax.broadcasted_iota(jnp.int32, (n, n), 0) == lax.broadcasted_iota(jnp.int32, (n, n), 1)


def cast_kernel(v_ref, out_ref):
    frames = v_ref.shape[0]
    for j in range(v_ref.shape[1] // BLOCK):
        out_ref[rows(j, frames), :] = v_ref[:, lanes(j)].astype(BF16)


def turn_kernel(row_span, stretch, brow, bcol, blocks, index_ref, out_ref):
    for k in range(blocks.shape[0]):
        index_ref[0, k] = lax.rem(brow[k], row_span)
        index_ref[1, k] = lax.div(bcol[k], row_span) * stretch + lax.rem(bcol[k], stretch)
        out_ref[k] = blocks[k].T


def gram_kernel(v_ref, prior, out_ref):
    value = v_ref[...]
    out_ref[...] = nt_dot(value, jnp.concatenate([value, value * prior[...]], axis=0), FP32)


def fill(panel, ref, at, stretch):
    frames = panel.shape[1]
    for j in range(stretch):
        panel[at * stretch + j] = ref[rows(j, frames), :]


def whole_of(panel):
    return jnp.concatenate([panel[b] for b in range(panel.shape[0])], axis=1)


def forward_kernel(stretch, cols, index, search, blocks, gram, half, keep_ref, send_ref, acc, panel):
    frames = panel.shape[1]
    me = lax.axis_index("row")
    for flip, ref in enumerate(search):
        fill(panel, ref, lax.bitwise_xor(me, flip), stretch)
    acc[...] = jnp.zeros_like(acc)
    for k in range(blocks.shape[0]):
        acc[index[0, k]] += jnp.dot(panel[index[1, k]], blocks[k], preferred_element_type=F32)
    core = lax.rem(lax.axis_index("col"), 2)
    for x in range(cols // 2):
        for j in range(stretch):
            at = rows(x * stretch + j, frames)
            keep_ref[at, :] = acc[(2 * x + core) * stretch + j]
            send_ref[at, :] = acc[(2 * x + 1 - core) * stretch + j]
    at = rows(cols // 2 * stretch, frames)
    value = gram[...]
    if half:
        whole = whole_of(panel)
        inner = nt_dot(whole, jnp.concatenate([whole, jnp.zeros_like(whole)], axis=0))
        lane = lax.broadcasted_iota(jnp.int32, value.shape, 1)
        value = jnp.where(lane < frames, inner, value)
        send_ref[at.stop :, :] = half[0][...]
        keep_ref[at.stop :, :] = half[0][...]
    keep_ref[at, :] = value
    send_ref[at, :] = value


def pair_kernel(frames, keep, received, out_ref, first_refs):
    core = lax.rem(lax.axis_index("col"), 2)
    split_at = frames // 2
    data = out_ref.shape[0] - frames
    for j in range(data // frames):
        at = rows(j, frames)
        out_ref[at, :] = (keep[at, :] + received[at, :]).astype(BF16)
    at = pl.ds(pl.multiple_of(data + core * split_at, split_at), split_at)
    out_ref[data : data + split_at, :], out_ref[data + split_at :, :] = split(
        keep[at, :] + received[at, :]
    )
    if first_refs:
        at = pl.ds(pl.multiple_of(core * split_at, split_at), split_at)
        first_refs[0][at, :] = keep[data + frames :, :]
        at = pl.ds(pl.multiple_of((1 - core) * split_at, split_at), split_at)
        first_refs[0][at, :] = received[data + frames :, :]


def chips_kernel(frames, parts, before, out_ref):
    split_at = frames // 2
    data = out_ref.shape[0] - frames
    for j in range(data // frames):
        at = rows(j, frames)
        out_ref[at, :] = sum_rows(parts, at).astype(BF16)
    high, low = slice(data, data + split_at), slice(data + split_at, data + frames)
    out_ref[high, :], out_ref[low, :] = split(sum_rows(parts, high) + sum_rows(parts, low))


def backward_kernel(
    stretch, cols, last, index, own, received, blocks,
    far_refs, near_ref, keep_refs, keep_ref, norm_refs, acc, panel, gram,
):
    frames = panel.shape[1]
    split_at = frames // 2
    core = lax.rem(lax.axis_index("col"), 2)
    data = cols // 2 * stretch * frames
    for ref, side in ((own, core), (received, 1 - core)):
        for x in range(cols // 2):
            for j in range(stretch):
                panel[(2 * x + side) * stretch + j] = ref[rows(x * stretch + j, frames), :]
    fill_gram(gram, own, received, data, frames)
    acc[...] = jnp.zeros_like(acc)
    for k in range(blocks.shape[0]):
        acc[index[1, k]] += jnp.dot(panel[index[0, k]], blocks[k], preferred_element_type=F32)
    me = lax.axis_index("row")
    for far, (far_ref, kept_ref) in enumerate(zip(far_refs, keep_refs)):
        shard = lax.bitwise_xor(me, 2 * (far + 1))
        other = lax.bitwise_xor(shard, 1)
        for j in range(stretch):
            kept_ref[rows(j, frames), :] = acc[shard * stretch + j]
            far_ref[rows(j, frames), :] = acc[other * stretch + j].astype(BF16)
    other = lax.bitwise_xor(me, 1)
    for j in range(stretch):
        keep_ref[rows(j, frames), :] = acc[me * stretch + j]
        near_ref[rows(j, frames), :] = acc[other * stretch + j].astype(BF16)
    if last:
        norm_refs[0][...] = gram[:, :frames]
        return
    whole = whole_of(panel)
    total = gram[...] + nt_dot(whole, jnp.concatenate([jnp.zeros_like(whole), whole], axis=0))
    at = stretch * frames
    out_ref = far_refs[0]
    gram[...] = total
    out_ref[at : at + split_at, :], out_ref[at + split_at : at + frames, :] = split(
        gram[pl.ds(pl.multiple_of(core * split_at, split_at), split_at), :]
    )
    lane = lax.broadcasted_iota(jnp.int32, total.shape, 1)
    row = lax.broadcasted_iota(jnp.int32, total.shape, 0)
    on_diagonal = jnp.logical_or(lane == row, lane == row + frames)
    diagonal = jnp.sum(jnp.where(on_diagonal, total, 0.0), axis=0, keepdims=True)
    row = lax.broadcasted_iota(jnp.int32, (DIAG, 2 * frames), 0)
    out_ref[at + frames :, :] = jnp.where(row == 0, diagonal, 0.0).astype(BF16)


def rows_kernel(frames, sent, received, kept, before, out_refs, gram_refs):
    split_at = frames // 2
    data = kept[0].shape[0]
    for out_ref, kept_ref, received_ref in zip(out_refs, kept, received):
        for j in range(data // frames):
            at = rows(j, frames)
            out_ref[at, :] = (kept_ref[at, :] + received_ref[at, :].astype(F32)).astype(BF16)
    if gram_refs:
        pair = (sent, received[0])
        high, low = slice(data, data + split_at), slice(data + split_at, data + frames)
        value = sum_rows(pair, high) + sum_rows(pair, low)
        block = jnp.concatenate(split(value), axis=0)
        tile = sum_rows(pair, slice(data + frames, data + frames + DIAG)).astype(BF16)
        gram_refs[0][...] = value
        gram_refs[1][...] = tile
        for out_ref in out_refs:
            out_ref[data : data + frames, :] = block
            out_ref[data + frames :, :] = tile


def fill_gram(gram, own, received, data, frames):
    split_at = frames // 2
    core = lax.rem(lax.axis_index("col"), 2)
    for ref, side in ((own, core), (received, 1 - core)):
        at = pl.ds(pl.multiple_of(side * split_at, split_at), split_at)
        gram[at, :] = ref[data : data + split_at, :].astype(F32) + ref[data + split_at :, :].astype(
            F32
        )


def second_gram_kernel(data, own, received, out_ref, gram):
    frames = out_ref.shape[0]
    fill_gram(gram, own, received, data, frames)
    whole = jnp.concatenate(
        [ref[rows(j, frames), :] for ref in (own, received) for j in range(data // frames)], axis=1
    )
    value = gram[:, frames:] + nt_dot(whole, whole)
    out_ref[...] = jnp.concatenate(split(value), axis=1)


def second_pair_kernel(own, received, gram_ref, out_ref):
    n = own.shape[0]
    both = own[...].astype(F32) + received[...].astype(F32)
    value = both[:, :n] + both[:, n:]
    gram_ref[...] = value
    out_ref[...] = jnp.concatenate(split(value), axis=1)


def near_kernel(keep, near, sum_ref, cast_ref):
    total = keep[...] + near[...].astype(F32)
    sum_ref[...] = total
    cast_ref[...] = total.astype(BF16)


def own_sum(keep, parts, j, frames):
    at = rows(j, frames)
    return keep[at, :] + sum_rows(parts, at)


def frame_shift(diagonal, frames):
    row = 1.25 * diagonal[:, frames:] / diagonal[:, :frames]
    return jnp.sum(jnp.where(eye(frames), row, 0.0), axis=1, keepdims=True), row


def image_kernel(
    pair_sum, far, gram, tile, v_ref, prior, image_ref, next_ref, cast_ref, half_ref, diag_ref
):
    frames = v_ref.shape[0]
    split_at = frames // 2
    data = cast_ref.shape[0]
    diagonal = tile[...].astype(F32) + sum_rows(far, slice(data + frames, data + frames + DIAG))
    diag_ref[...] = diagonal
    shift, _ = frame_shift(diagonal[0:1, :], frames)
    for j in range(data // frames):
        value = v_ref[:, lanes(j)]
        image = own_sum(pair_sum, far, j, frames) + prior[:, lanes(j)] * value
        following = image - shift * value
        image_ref[:, lanes(j)] = image
        next_ref[:, lanes(j)] = following
        cast_ref[rows(j, frames), :] = following.astype(BF16)
    half_ref[...] = (
        gram[...]
        + sum_rows(far, slice(data, data + split_at))
        + sum_rows(far, slice(data + split_at, data + frames))
    )


def remainder_kernel(v_ref, prior, before, out_ref):
    frames = v_ref.shape[0]
    stretch = v_ref.shape[1] // BLOCK
    for j in range(stretch):
        out_ref[rows(j, frames), :] = split(v_ref[:, lanes(j)])[1]
    terms = [part.astype(F32) for part in split(prior[...])]
    lines = [part[:, lanes(j)] for part in terms for j in range(stretch)]
    lines.append(jnp.zeros((DIAG - len(lines), BLOCK), F32))
    out_ref[stretch * frames :, :] = jnp.concatenate(lines, axis=0).astype(BF16)


def cross_kernel(frames, own, received, high, low, diag_ref, cast_ref):
    stretch = cast_ref.shape[0] // frames
    shift, _ = frame_shift(diag_ref[0:1, :], frames)
    tile = low[stretch * frames :, :].astype(F32)
    for j in range(stretch):
        at = rows(j, frames)
        weight = tile[j : j + 1, :] + tile[stretch + j : stretch + j + 1, :]
        value = sum_rows((high, low), at)
        cast_ref[at, :] = (sum_rows((own, received), at) + (weight - shift) * value).astype(BF16)


def eliminate(matrix, right, n):
    width = matrix.shape[1] + right.shape[1]
    work = jnp.concatenate([matrix, right], axis=1)
    work = [work[rows(i, TILE), :] for i in range(n // TILE)]
    at = lax.broadcasted_iota(jnp.int32, (TILE, width), 0)

    def column(k):
        return [jnp.broadcast_to(t[:, k : k + 1], (TILE, width)) for t in work]

    def step(tiles, spread, k, pivot):
        i, s = divmod(k, TILE)
        row = tiles[i][s : s + 1, :] * pivot
        done = [t - c * row for t, c in zip(tiles, spread)]
        done[i] = jnp.where(at == s, row, done[i])
        return done

    ahead = [column(k) for k in range(AHEAD)]
    for k in range(n):
        i, s = divmod(k, TILE)
        spread = ahead.pop(0)
        pivot = 1.0 / spread[i][s : s + 1, :]
        ahead = [step(later, spread, k, pivot) for later in ahead]
        work = step(work, spread, k, pivot)
        if k + AHEAD < n:
            ahead.append(column(k + AHEAD))
    return jnp.concatenate(work, axis=0)[:, n:]


def inverse_kernel(first, out_ref):
    n = first.shape[0]
    out_ref[...] = eliminate(first[:, n:], jnp.where(eye(n), 1.0, 0.0), n)


def middle_kernel(first, inverse_ref, norm_ref, diag_ref, out_ref):
    n = first.shape[0]
    norm, energy = first[:, :n], first[:, n:]
    shift, shift_row = frame_shift(diag_ref[0:1, :], n)
    inverse = inverse_ref[...]
    next_rhs = energy - shift * norm
    cross = norm_ref[...] + next_rhs * shift_row
    alpha = nn_dot(inverse, norm)
    conj = nn_dot(inverse, cross.T)
    out_ref[0] = alpha
    out_ref[1] = conj
    out_ref[2] = nn_dot(cross, conj)
    out_ref[3] = next_rhs - nn_dot(cross, alpha)


def solve_kernel(gram, parts, middle, out_ref):
    n = gram.shape[0]
    schur = gram[...] - middle[2]
    for part in parts:
        both = part[...].astype(F32)
        schur += both[:, :n] + both[:, n:]
    gamma = eliminate(schur, middle[3], n)
    out_ref[:n, :] = middle[0] - nn_dot(middle[1], gamma)
    out_ref[n:, :] = gamma


def final_kernel(keep, near, far, v_ref, image_ref, next_ref, prior, coeffs_ref, x_ref, r_ref):
    n = v_ref.shape[0]
    coeffs = coeffs_ref[...]
    for j in range(keep.shape[0] // n):
        value = v_ref[:, lanes(j)]
        following = next_ref[:, lanes(j)]
        second_image = own_sum(keep, (near, *far), j, n) + prior[:, lanes(j)] * following
        x_ref[:, lanes(j)] = tn_dot(coeffs, jnp.concatenate([value, following], axis=0))
        r_ref[:, lanes(j)] = value - tn_dot(
            coeffs, jnp.concatenate([image_ref[:, lanes(j)], second_image], axis=0)
        )


def swapped(x, axis, flip):
    return lax.ppermute(x, axis, [(i, i ^ flip) for i in range(lax.axis_size(axis))])


def others(x, axis):
    return (x, *(swapped(x, axis, flip) for flip in range(2, lax.axis_size(axis), 2)))


def gather(x, axis):
    return tuple(part for own in others(x, axis) for part in (own, swapped(own, axis, 1)))


def shards(right_side, prior, blocks, block_row, block_col):
    frames, pix = right_side.shape
    stretch = pix // BLOCK
    n_rows, n_cols = lax.axis_size("row"), lax.axis_size("col")
    row_span, col_span = stretch * n_cols, stretch * n_rows
    prior = prior.reshape(1, pix)
    stored = blocks.shape[0]
    half_cols = n_cols // 2 * stretch * frames

    def shape(dims, dtype=F32):
        return jax.ShapeDtypeStruct(dims, dtype)

    own = shape((frames, pix))
    gram_type = shape((frames, 2 * frames))
    cast_type = shape((stretch * frames, BLOCK), BF16)
    aside = pl.CostEstimate(flops=2 * 10**9, bytes_accessed=8 * 10**6, transcendentals=0)

    pairs = n_rows // 2 - 1

    def forward(search, gram, half):
        size = half_cols + frames + (frames // 2 if half else 0)
        keep, send = call(
            lambda *refs: forward_kernel(stretch, n_cols, *refs),
            (shape((size, BLOCK)),) * 2,
            (index, search, turned, gram, half),
            [
                pltpu.VMEM((row_span, frames, BLOCK), F32),
                pltpu.VMEM((col_span, frames, BLOCK), BF16),
            ],
        )
        received = swapped(send, "col", 1)
        pair, first = call(
            lambda *refs: pair_kernel(frames, *refs),
            (shape((half_cols + frames, BLOCK), BF16), (gram_type,) if half else ()),
            (keep, received),
        )
        if half:
            aside_of_chips = call(inverse_kernel, (shape((frames, frames)),), first, cost=aside)
        elif n_rows == 4:
            (remainder,) = call(
                remainder_kernel,
                (shape((stretch * frames + DIAG, BLOCK), BF16),),
                (right_side, prior, pair),
            )
            aside_of_chips = [swapped(remainder, "row", 2)]
        else:
            aside_of_chips = []
        (foot,) = call(
            lambda *refs: chips_kernel(frames, *refs),
            (shape((half_cols + frames, BLOCK), BF16),),
            (others(pair, "col"), aside_of_chips),
        )
        return (foot, swapped(foot, "col", 1)), (*first, *aside_of_chips)

    def backward(foot, last):
        size = stretch * frames
        extra = 0 if last else frames + DIAG
        far, near, kept, keep, norm = call(
            lambda *refs: backward_kernel(stretch, n_cols, last, *refs),
            (
                tuple(shape((size + (0 if p else extra), BLOCK), BF16) for p in range(pairs)),
                shape((size, BLOCK), BF16),
                (shape((size, BLOCK)),) * pairs,
                shape((size, BLOCK)),
                (shape((frames, frames)),) if last else (),
            ),
            (index, *foot, blocks),
            [
                pltpu.VMEM((col_span, frames, BLOCK), F32),
                pltpu.VMEM((row_span, frames, BLOCK), BF16),
                pltpu.VMEM((frames, 2 * frames), F32),
            ],
        )
        received = tuple(swapped(x, "row", 1) for x in far)
        near = swapped(near, "row", 1)
        middle = ()
        if last:
            middle = call(
                middle_kernel,
                (shape((4, frames, frames)),),
                (first, inverse, *norm, diagonal),
                cost=aside,
            )
        sums, gram = call(
            lambda *refs: rows_kernel(frames, *refs),
            (
                (shape((size + extra, BLOCK), BF16),) * pairs,
                ()
                if last
                else (shape((frames // 2, 2 * frames)), shape((DIAG, 2 * frames), BF16)),
            ),
            (far[0], received, kept, middle),
        )
        far = tuple(swapped(x, "row", 2 * (p + 1)) for p, x in enumerate(sums))
        return (keep, near, far, *gram), (middle if last else sums)

    (cast,) = call(cast_kernel, (cast_type,), (right_side,))
    search = gather(cast, "row")
    index, turned = call(
        lambda *refs: turn_kernel(row_span, stretch, *refs),
        (shape((2, stored), jnp.int32), shape(blocks.shape, BF16)),
        (block_row, block_col, blocks),
        cost=aside,
    )
    (gram,) = call(gram_kernel, (gram_type,), (right_side, prior), cost=aside)
    foot, remainder = forward(search, gram, ())
    (keep, near, far, gram, tile), sums = backward(foot, False)
    pair_sum, pair_cast = call(
        near_kernel, (shape((stretch * frames, BLOCK)), cast_type), (keep, near)
    )
    image, following, cast, half, diagonal = call(
        image_kernel,
        (own, own, cast_type, shape((frames // 2, 2 * frames)), shape((DIAG, 2 * frames))),
        (pair_sum, far, gram, tile, right_side, prior),
    )
    if n_rows == 4:
        (cross,) = call(
            lambda *refs: cross_kernel(frames, *refs),
            (cast_type,),
            (
                sums[0],
                swapped(pair_cast, "row", 2),
                search[2],
                *remainder,
                diagonal,
            ),
        )
        search = (cast, swapped(cast, "row", 1), cross, swapped(cross, "row", 1))
    else:
        search = gather(cast, "row")
    (gram,) = call(gram_kernel, (gram_type,), (following, prior), cost=aside)
    foot, (first, inverse) = forward(search, gram, (half,))
    (second,) = call(
        lambda *refs: second_gram_kernel(half_cols, *refs),
        (shape((frames, 2 * frames), BF16),),
        foot,
        [pltpu.VMEM((frames, 2 * frames), F32)],
    )
    gram, second = call(
        second_pair_kernel,
        (shape((frames, frames)), shape((frames, 2 * frames), BF16)),
        (second, swapped(second, "row", 1)),
    )
    second = others(second, "row")[1:]
    parts, middle = backward(foot, True)
    (coeffs,) = call(
        solve_kernel, (shape((2 * frames, frames)),), (gram, second, *middle), cost=aside
    )
    return tuple(
        call(
            final_kernel,
            (own, own),
            (*parts, right_side, image, following, prior, coeffs),
        )
    )


def solution(mesh):
    return jax.shard_map(
        shards,
        mesh=mesh,
        in_specs=(
            P("groups", ("row", "col")),
            P(("row", "col")),
            P(("row", "col"), None, None),
            P(("row", "col")),
            P(("row", "col")),
        ),
        out_specs=(P("groups", ("row", "col")), P("groups", ("row", "col"))),
        check_vma=False,
    )
```

```python
import jax
import jax.numpy as jnp
from jax import lax
from jax.experimental import pallas as pl
from jax.experimental.pallas import tpu as pltpu
from jax.sharding import PartitionSpec as P

BLOCK = 128
TILE = 8
AHEAD = 4
DIAG = 16
F32, BF16 = jnp.float32, jnp.bfloat16
FP32 = lax.Precision.HIGHEST
VMEM = pl.BlockSpec(memory_space=pltpu.VMEM)
SMEM = pl.BlockSpec(memory_space=pltpu.SMEM)


def nt_dot(a, b, precision=None):
    return lax.dot_general(
        a, b, (((1,), (1,)), ((), ())), precision=precision, preferred_element_type=F32
    )


def tn_dot(a, b):
    return lax.dot_general(
        a, b, (((0,), (0,)), ((), ())), precision=FP32, preferred_element_type=F32
    )


def nn_dot(a, b):
    return lax.dot_general(
        a, b, (((1,), (0,)), ((), ())), precision=FP32, preferred_element_type=F32
    )


def call(kernel, outs, ins, scratch=(), cost=None):
    flat_ins, ins_tree = jax.tree.flatten(tuple(ins))
    flat_outs, outs_tree = jax.tree.flatten(tuple(outs))

    def body(*refs):
        middle, last = len(flat_ins), len(flat_ins) + len(flat_outs)
        kernel(
            *jax.tree.unflatten(ins_tree, refs[:middle]),
            *jax.tree.unflatten(outs_tree, refs[middle:last]),
            *refs[last:],
        )

    def space(x):
        return SMEM if x.dtype == jnp.int32 else VMEM

    results = pl.pallas_call(
        body,
        out_shape=flat_outs,
        in_specs=[space(x) for x in flat_ins],
        out_specs=[space(x) for x in flat_outs],
        scratch_shapes=list(scratch),
        compiler_params=pltpu.CompilerParams(vmem_limit_bytes=48 * 1024 * 1024),
        cost_estimate=cost,
    )(*flat_ins)
    return jax.tree.unflatten(outs_tree, results)


def lanes(j):
    return slice(j * BLOCK, (j + 1) * BLOCK)


def rows(j, count):
    return slice(j * count, (j + 1) * count)


def split(value):
    high = value.astype(BF16)
    return high, (value - high.astype(F32)).astype(BF16)


def sum_rows(refs, at):
    total = refs[0][at, :].astype(F32)
    for ref in refs[1:]:
        total += ref[at, :].astype(F32)
    return total


def eye(n):
    return lax.broadcasted_iota(jnp.int32, (n, n), 0) == lax.broadcasted_iota(jnp.int32, (n, n), 1)


def cast_kernel(v_ref, out_ref):
    frames = v_ref.shape[0]
    for j in range(v_ref.shape[1] // BLOCK):
        out_ref[rows(j, frames), :] = v_ref[:, lanes(j)].astype(BF16)


def turn_kernel(row_span, stretch, brow, bcol, blocks, index_ref, out_ref):
    for k in range(blocks.shape[0]):
        index_ref[0, k] = lax.rem(brow[k], row_span)
        index_ref[1, k] = lax.div(bcol[k], row_span) * stretch + lax.rem(bcol[k], stretch)
        out_ref[k] = blocks[k].T


def gram_kernel(v_ref, prior, out_ref):
    value = v_ref[...]
    out_ref[...] = nt_dot(value, jnp.concatenate([value, value * prior[...]], axis=0), FP32)


def fill(panel, ref, at, stretch):
    frames = panel.shape[1]
    for j in range(stretch):
        panel[at * stretch + j] = ref[rows(j, frames), :]


def whole_of(panel):
    return jnp.concatenate([panel[b] for b in range(panel.shape[0])], axis=1)


def forward_kernel(stretch, cols, index, search, blocks, gram, half, keep_ref, send_ref, acc, panel):
    frames = panel.shape[1]
    me = lax.axis_index("row")
    for flip, ref in enumerate(search):
        fill(panel, ref, lax.bitwise_xor(me, flip), stretch)
    acc[...] = jnp.zeros_like(acc)
    for k in range(blocks.shape[0]):
        acc[index[0, k]] += jnp.dot(panel[index[1, k]], blocks[k], preferred_element_type=F32)
    core = lax.rem(lax.axis_index("col"), 2)
    for x in range(cols // 2):
        for j in range(stretch):
            at = rows(x * stretch + j, frames)
            keep_ref[at, :] = acc[(2 * x + core) * stretch + j]
            send_ref[at, :] = acc[(2 * x + 1 - core) * stretch + j]
    at = rows(cols // 2 * stretch, frames)
    value = gram[...]
    if half:
        whole = whole_of(panel)
        inner = nt_dot(whole, jnp.concatenate([whole, jnp.zeros_like(whole)], axis=0))
        lane = lax.broadcasted_iota(jnp.int32, value.shape, 1)
        value = jnp.where(lane < frames, inner, value)
        send_ref[at.stop :, :] = half[0][...]
        keep_ref[at.stop :, :] = half[0][...]
    keep_ref[at, :] = value
    send_ref[at, :] = value


def pair_kernel(frames, keep, received, out_ref, first_refs):
    core = lax.rem(lax.axis_index("col"), 2)
    split_at = frames // 2
    data = out_ref.shape[0] - frames
    for j in range(data // frames):
        at = rows(j, frames)
        out_ref[at, :] = (keep[at, :] + received[at, :]).astype(BF16)
    at = pl.ds(pl.multiple_of(data + core * split_at, split_at), split_at)
    out_ref[data : data + split_at, :], out_ref[data + split_at :, :] = split(
        keep[at, :] + received[at, :]
    )
    if first_refs:
        at = pl.ds(pl.multiple_of(core * split_at, split_at), split_at)
        first_refs[0][at, :] = keep[data + frames :, :]
        at = pl.ds(pl.multiple_of((1 - core) * split_at, split_at), split_at)
        first_refs[0][at, :] = received[data + frames :, :]


def chips_kernel(frames, parts, before, out_ref):
    split_at = frames // 2
    data = out_ref.shape[0] - frames
    for j in range(data // frames):
        at = rows(j, frames)
        out_ref[at, :] = sum_rows(parts, at).astype(BF16)
    high, low = slice(data, data + split_at), slice(data + split_at, data + frames)
    out_ref[high, :], out_ref[low, :] = split(sum_rows(parts, high) + sum_rows(parts, low))


def backward_kernel(
    stretch, cols, last, index, own, received, blocks,
    far_refs, near_ref, keep_refs, keep_ref, norm_refs, acc, panel, gram,
):
    frames = panel.shape[1]
    split_at = frames // 2
    core = lax.rem(lax.axis_index("col"), 2)
    data = cols // 2 * stretch * frames
    for ref, side in ((own, core), (received, 1 - core)):
        for x in range(cols // 2):
            for j in range(stretch):
                panel[(2 * x + side) * stretch + j] = ref[rows(x * stretch + j, frames), :]
    fill_gram(gram, own, received, data, frames)
    acc[...] = jnp.zeros_like(acc)
    for k in range(blocks.shape[0]):
        acc[index[1, k]] += jnp.dot(panel[index[0, k]], blocks[k], preferred_element_type=F32)
    me = lax.axis_index("row")
    for far, (far_ref, kept_ref) in enumerate(zip(far_refs, keep_refs)):
        shard = lax.bitwise_xor(me, 2 * (far + 1))
        other = lax.bitwise_xor(shard, 1)
        for j in range(stretch):
            kept_ref[rows(j, frames), :] = acc[shard * stretch + j]
            far_ref[rows(j, frames), :] = acc[other * stretch + j].astype(BF16)
    other = lax.bitwise_xor(me, 1)
    for j in range(stretch):
        keep_ref[rows(j, frames), :] = acc[me * stretch + j]
        near_ref[rows(j, frames), :] = acc[other * stretch + j].astype(BF16)
    if last:
        norm_refs[0][...] = gram[:, :frames]
        return
    whole = whole_of(panel)
    total = gram[...] + nt_dot(whole, jnp.concatenate([jnp.zeros_like(whole), whole], axis=0))
    at = stretch * frames
    out_ref = far_refs[0]
    gram[...] = total
    out_ref[at : at + split_at, :], out_ref[at + split_at : at + frames, :] = split(
        gram[pl.ds(pl.multiple_of(core * split_at, split_at), split_at), :]
    )
    lane = lax.broadcasted_iota(jnp.int32, total.shape, 1)
    row = lax.broadcasted_iota(jnp.int32, total.shape, 0)
    on_diagonal = jnp.logical_or(lane == row, lane == row + frames)
    diagonal = jnp.sum(jnp.where(on_diagonal, total, 0.0), axis=0, keepdims=True)
    row = lax.broadcasted_iota(jnp.int32, (DIAG, 2 * frames), 0)
    out_ref[at + frames :, :] = jnp.where(row == 0, diagonal, 0.0).astype(BF16)


def rows_kernel(frames, sent, received, kept, out_refs, gram_refs):
    split_at = frames // 2
    data = kept[0].shape[0]
    for out_ref, kept_ref, received_ref in zip(out_refs, kept, received):
        for j in range(data // frames):
            at = rows(j, frames)
            out_ref[at, :] = (kept_ref[at, :] + received_ref[at, :].astype(F32)).astype(BF16)
    if gram_refs:
        pair = (sent, received[0])
        high, low = slice(data, data + split_at), slice(data + split_at, data + frames)
        value = sum_rows(pair, high) + sum_rows(pair, low)
        block = jnp.concatenate(split(value), axis=0)
        tile = sum_rows(pair, slice(data + frames, data + frames + DIAG)).astype(BF16)
        gram_refs[0][...] = value
        gram_refs[1][...] = tile
        for out_ref in out_refs:
            out_ref[data : data + frames, :] = block
            out_ref[data + frames :, :] = tile


def fill_gram(gram, own, received, data, frames):
    split_at = frames // 2
    core = lax.rem(lax.axis_index("col"), 2)
    for ref, side in ((own, core), (received, 1 - core)):
        at = pl.ds(pl.multiple_of(side * split_at, split_at), split_at)
        gram[at, :] = ref[data : data + split_at, :].astype(F32) + ref[data + split_at :, :].astype(
            F32
        )


def second_gram_kernel(data, own, received, out_ref, gram):
    frames = out_ref.shape[0]
    fill_gram(gram, own, received, data, frames)
    whole = jnp.concatenate(
        [ref[rows(j, frames), :] for ref in (own, received) for j in range(data // frames)], axis=1
    )
    value = gram[:, frames:] + nt_dot(whole, whole)
    out_ref[...] = jnp.concatenate(split(value), axis=1)


def second_pair_kernel(own, received, gram_ref, out_ref):
    n = own.shape[0]
    both = own[...].astype(F32) + received[...].astype(F32)
    value = both[:, :n] + both[:, n:]
    gram_ref[...] = value
    out_ref[...] = jnp.concatenate(split(value), axis=1)


def near_kernel(keep, near, sum_ref, cast_ref):
    total = keep[...] + near[...].astype(F32)
    sum_ref[...] = total
    cast_ref[...] = total.astype(BF16)


def own_sum(keep, parts, j, frames):
    at = rows(j, frames)
    return keep[at, :] + sum_rows(parts, at)


def frame_shift(diagonal, frames):
    row = 1.25 * diagonal[:, frames:] / diagonal[:, :frames]
    return jnp.sum(jnp.where(eye(frames), row, 0.0), axis=1, keepdims=True), row


def image_kernel(
    pair_sum, far, gram, tile, v_ref, prior, image_ref, next_ref, cast_ref, half_ref, diag_ref
):
    frames = v_ref.shape[0]
    split_at = frames // 2
    data = cast_ref.shape[0]
    diagonal = tile[...].astype(F32) + sum_rows(far, slice(data + frames, data + frames + DIAG))
    diag_ref[...] = diagonal
    shift, _ = frame_shift(diagonal[0:1, :], frames)
    for j in range(data // frames):
        value = v_ref[:, lanes(j)]
        image = own_sum(pair_sum, far, j, frames) + prior[:, lanes(j)] * value
        following = image - shift * value
        image_ref[:, lanes(j)] = image
        next_ref[:, lanes(j)] = following
        cast_ref[rows(j, frames), :] = following.astype(BF16)
    half_ref[...] = (
        gram[...]
        + sum_rows(far, slice(data, data + split_at))
        + sum_rows(far, slice(data + split_at, data + frames))
    )


def remainder_kernel(v_ref, prior, before, out_ref):
    frames = v_ref.shape[0]
    stretch = v_ref.shape[1] // BLOCK
    for j in range(stretch):
        out_ref[rows(j, frames), :] = split(v_ref[:, lanes(j)])[1]
    terms = [part.astype(F32) for part in split(prior[...])]
    lines = [part[:, lanes(j)] for part in terms for j in range(stretch)]
    lines.append(jnp.zeros((DIAG - len(lines), BLOCK), F32))
    out_ref[stretch * frames :, :] = jnp.concatenate(lines, axis=0).astype(BF16)


def cross_kernel(frames, own, received, high, low, diag_ref, cast_ref):
    stretch = cast_ref.shape[0] // frames
    shift, _ = frame_shift(diag_ref[0:1, :], frames)
    tile = low[stretch * frames :, :].astype(F32)
    for j in range(stretch):
        at = rows(j, frames)
        weight = tile[j : j + 1, :] + tile[stretch + j : stretch + j + 1, :]
        value = sum_rows((high, low), at)
        cast_ref[at, :] = (sum_rows((own, received), at) + (weight - shift) * value).astype(BF16)


def eliminate(matrix, right, n):
    width = matrix.shape[1] + right.shape[1]
    work = jnp.concatenate([matrix, right], axis=1)
    work = [work[rows(i, TILE), :] for i in range(n // TILE)]
    at = lax.broadcasted_iota(jnp.int32, (TILE, width), 0)

    def column(k):
        return [jnp.broadcast_to(t[:, k : k + 1], (TILE, width)) for t in work]

    def step(tiles, spread, k, pivot):
        i, s = divmod(k, TILE)
        row = tiles[i][s : s + 1, :] * pivot
        done = [t - c * row for t, c in zip(tiles, spread)]
        done[i] = jnp.where(at == s, row, done[i])
        return done

    ahead = [column(k) for k in range(AHEAD)]
    for k in range(n):
        i, s = divmod(k, TILE)
        spread = ahead.pop(0)
        pivot = 1.0 / spread[i][s : s + 1, :]
        ahead = [step(later, spread, k, pivot) for later in ahead]
        work = step(work, spread, k, pivot)
        if k + AHEAD < n:
            ahead.append(column(k + AHEAD))
    return jnp.concatenate(work, axis=0)[:, n:]


def inverse_kernel(first, out_ref):
    n = first.shape[0]
    out_ref[...] = eliminate(first[:, n:], jnp.where(eye(n), 1.0, 0.0), n)


def solve_kernel(gram, parts, first, inverse_ref, norm_ref, diag_ref, out_ref):
    n = gram.shape[0]
    norm, energy = first[:, :n], first[:, n:]
    shift, shift_row = frame_shift(diag_ref[0:1, :], n)
    inverse = inverse_ref[...]
    next_rhs = energy - shift * norm
    cross = norm_ref[...] + next_rhs * shift_row
    alpha = nn_dot(inverse, norm)
    conj = nn_dot(inverse, cross.T)
    schur = gram[...] - nn_dot(cross, conj)
    for part in parts:
        both = part[...].astype(F32)
        schur += both[:, :n] + both[:, n:]
    gamma = eliminate(schur, next_rhs - nn_dot(cross, alpha), n)
    out_ref[:n, :] = alpha - nn_dot(conj, gamma)
    out_ref[n:, :] = gamma


def final_kernel(keep, near, far, v_ref, image_ref, next_ref, prior, coeffs_ref, x_ref, r_ref):
    n = v_ref.shape[0]
    coeffs = coeffs_ref[...]
    for j in range(keep.shape[0] // n):
        value = v_ref[:, lanes(j)]
        following = next_ref[:, lanes(j)]
        second_image = own_sum(keep, (near, *far), j, n) + prior[:, lanes(j)] * following
        x_ref[:, lanes(j)] = tn_dot(coeffs, jnp.concatenate([value, following], axis=0))
        r_ref[:, lanes(j)] = value - tn_dot(
            coeffs, jnp.concatenate([image_ref[:, lanes(j)], second_image], axis=0)
        )


def swapped(x, axis, flip):
    return lax.ppermute(x, axis, [(i, i ^ flip) for i in range(lax.axis_size(axis))])


def others(x, axis):
    return (x, *(swapped(x, axis, flip) for flip in range(2, lax.axis_size(axis), 2)))


def gather(x, axis):
    return tuple(part for own in others(x, axis) for part in (own, swapped(own, axis, 1)))


def shards(right_side, prior, blocks, block_row, block_col):
    frames, pix = right_side.shape
    stretch = pix // BLOCK
    n_rows, n_cols = lax.axis_size("row"), lax.axis_size("col")
    row_span, col_span = stretch * n_cols, stretch * n_rows
    prior = prior.reshape(1, pix)
    stored = blocks.shape[0]
    half_cols = n_cols // 2 * stretch * frames

    def shape(dims, dtype=F32):
        return jax.ShapeDtypeStruct(dims, dtype)

    own = shape((frames, pix))
    gram_type = shape((frames, 2 * frames))
    cast_type = shape((stretch * frames, BLOCK), BF16)
    aside = pl.CostEstimate(flops=2 * 10**9, bytes_accessed=8 * 10**6, transcendentals=0)

    pairs = n_rows // 2 - 1

    def forward(search, gram, half):
        size = half_cols + frames + (frames // 2 if half else 0)
        keep, send = call(
            lambda *refs: forward_kernel(stretch, n_cols, *refs),
            (shape((size, BLOCK)),) * 2,
            (index, search, turned, gram, half),
            [
                pltpu.VMEM((row_span, frames, BLOCK), F32),
                pltpu.VMEM((col_span, frames, BLOCK), BF16),
            ],
        )
        received = swapped(send, "col", 1)
        pair, first = call(
            lambda *refs: pair_kernel(frames, *refs),
            (shape((half_cols + frames, BLOCK), BF16), (gram_type,) if half else ()),
            (keep, received),
        )
        if half:
            aside_of_chips = call(inverse_kernel, (shape((frames, frames)),), first, cost=aside)
        elif n_rows == 4:
            (remainder,) = call(
                remainder_kernel,
                (shape((stretch * frames + DIAG, BLOCK), BF16),),
                (right_side, prior, pair),
            )
            aside_of_chips = [swapped(remainder, "row", 2)]
        else:
            aside_of_chips = []
        (foot,) = call(
            lambda *refs: chips_kernel(frames, *refs),
            (shape((half_cols + frames, BLOCK), BF16),),
            (others(pair, "col"), aside_of_chips),
        )
        return (foot, swapped(foot, "col", 1)), (*first, *aside_of_chips)

    def backward(foot, last):
        size = stretch * frames
        extra = 0 if last else frames + DIAG
        far, near, kept, keep, norm = call(
            lambda *refs: backward_kernel(stretch, n_cols, last, *refs),
            (
                tuple(shape((size + (0 if p else extra), BLOCK), BF16) for p in range(pairs)),
                shape((size, BLOCK), BF16),
                (shape((size, BLOCK)),) * pairs,
                shape((size, BLOCK)),
                (shape((frames, frames)),) if last else (),
            ),
            (index, *foot, blocks),
            [
                pltpu.VMEM((col_span, frames, BLOCK), F32),
                pltpu.VMEM((row_span, frames, BLOCK), BF16),
                pltpu.VMEM((frames, 2 * frames), F32),
            ],
        )
        received = tuple(swapped(x, "row", 1) for x in far)
        near = swapped(near, "row", 1)
        sums, gram = call(
            lambda *refs: rows_kernel(frames, *refs),
            (
                (shape((size + extra, BLOCK), BF16),) * pairs,
                ()
                if last
                else (shape((frames // 2, 2 * frames)), shape((DIAG, 2 * frames), BF16)),
            ),
            (far[0], received, kept),
        )
        far = tuple(swapped(x, "row", 2 * (p + 1)) for p, x in enumerate(sums))
        return (keep, near, far, *gram), (norm if last else sums)

    (cast,) = call(cast_kernel, (cast_type,), (right_side,))
    search = gather(cast, "row")
    index, turned = call(
        lambda *refs: turn_kernel(row_span, stretch, *refs),
        (shape((2, stored), jnp.int32), shape(blocks.shape, BF16)),
        (block_row, block_col, blocks),
        cost=aside,
    )
    (gram,) = call(gram_kernel, (gram_type,), (right_side, prior), cost=aside)
    foot, remainder = forward(search, gram, ())
    (keep, near, far, gram, tile), sums = backward(foot, False)
    pair_sum, pair_cast = call(
        near_kernel, (shape((stretch * frames, BLOCK)), cast_type), (keep, near)
    )
    image, following, cast, half, diagonal = call(
        image_kernel,
        (own, own, cast_type, shape((frames // 2, 2 * frames)), shape((DIAG, 2 * frames))),
        (pair_sum, far, gram, tile, right_side, prior),
    )
    if n_rows == 4:
        (cross,) = call(
            lambda *refs: cross_kernel(frames, *refs),
            (cast_type,),
            (
                sums[0],
                swapped(pair_cast, "row", 2),
                search[2],
                *remainder,
                diagonal,
            ),
        )
        search = (cast, swapped(cast, "row", 1), cross, swapped(cross, "row", 1))
    else:
        search = gather(cast, "row")
    (gram,) = call(gram_kernel, (gram_type,), (following, prior), cost=aside)
    foot, (first, inverse) = forward(search, gram, (half,))
    (second,) = call(
        lambda *refs: second_gram_kernel(half_cols, *refs),
        (shape((frames, 2 * frames), BF16),),
        foot,
        [pltpu.VMEM((frames, 2 * frames), F32)],
    )
    gram, second = call(
        second_pair_kernel,
        (shape((frames, frames)), shape((frames, 2 * frames), BF16)),
        (second, swapped(second, "row", 1)),
    )
    second = others(second, "row")[1:]
    parts, norm = backward(foot, True)
    (coeffs,) = call(
        solve_kernel,
        (shape((2 * frames, frames)),),
        (gram, second, first, inverse, *norm, diagonal),
        cost=aside,
    )
    return tuple(
        call(
            final_kernel,
            (own, own),
            (*parts, right_side, image, following, prior, coeffs),
        )
    )


def solution(mesh):
    return jax.shard_map(
        shards,
        mesh=mesh,
        in_specs=(
            P("groups", ("row", "col")),
            P(("row", "col")),
            P(("row", "col"), None, None),
            P(("row", "col")),
            P(("row", "col")),
        ),
        out_specs=(P("groups", ("row", "col")), P("groups", ("row", "col"))),
        check_vma=False,
    )
```

```python
import jax
import jax.numpy as jnp
from jax import lax
from jax.experimental import pallas as pl
from jax.experimental.pallas import tpu as pltpu
from jax.sharding import PartitionSpec as P

BLOCK = 128
TILE = 8
AHEAD = 4
DIAG = 16
F32, BF16 = jnp.float32, jnp.bfloat16
FP32 = lax.Precision.HIGHEST
VMEM = pl.BlockSpec(memory_space=pltpu.VMEM)
SMEM = pl.BlockSpec(memory_space=pltpu.SMEM)


def nt_dot(a, b, precision=None):
    return lax.dot_general(
        a, b, (((1,), (1,)), ((), ())), precision=precision, preferred_element_type=F32
    )


def tn_dot(a, b):
    return lax.dot_general(
        a, b, (((0,), (0,)), ((), ())), precision=FP32, preferred_element_type=F32
    )


def nn_dot(a, b):
    return lax.dot_general(
        a, b, (((1,), (0,)), ((), ())), precision=FP32, preferred_element_type=F32
    )


def call(kernel, outs, ins, scratch=(), cost=None):
    flat_ins, ins_tree = jax.tree.flatten(tuple(ins))
    flat_outs, outs_tree = jax.tree.flatten(tuple(outs))

    def body(*refs):
        middle, last = len(flat_ins), len(flat_ins) + len(flat_outs)
        kernel(
            *jax.tree.unflatten(ins_tree, refs[:middle]),
            *jax.tree.unflatten(outs_tree, refs[middle:last]),
            *refs[last:],
        )

    def space(x):
        return SMEM if x.dtype == jnp.int32 else VMEM

    results = pl.pallas_call(
        body,
        out_shape=flat_outs,
        in_specs=[space(x) for x in flat_ins],
        out_specs=[space(x) for x in flat_outs],
        scratch_shapes=list(scratch),
        compiler_params=pltpu.CompilerParams(vmem_limit_bytes=48 * 1024 * 1024),
        cost_estimate=cost,
    )(*flat_ins)
    return jax.tree.unflatten(outs_tree, results)


def lanes(j):
    return slice(j * BLOCK, (j + 1) * BLOCK)


def rows(j, count):
    return slice(j * count, (j + 1) * count)


def split(value):
    high = value.astype(BF16)
    return high, (value - high.astype(F32)).astype(BF16)


def sum_rows(refs, at):
    total = refs[0][at, :].astype(F32)
    for ref in refs[1:]:
        total += ref[at, :].astype(F32)
    return total


def eye(n):
    return lax.broadcasted_iota(jnp.int32, (n, n), 0) == lax.broadcasted_iota(jnp.int32, (n, n), 1)


def cast_kernel(v_ref, out_ref):
    frames = v_ref.shape[0]
    for j in range(v_ref.shape[1] // BLOCK):
        out_ref[rows(j, frames), :] = v_ref[:, lanes(j)].astype(BF16)


def turn_kernel(row_span, stretch, brow, bcol, blocks, index_ref, out_ref):
    for k in range(blocks.shape[0]):
        index_ref[0, k] = lax.rem(brow[k], row_span)
        index_ref[1, k] = lax.div(bcol[k], row_span) * stretch + lax.rem(bcol[k], stretch)
        out_ref[k] = blocks[k].T


def gram_kernel(v_ref, prior, out_ref):
    value = v_ref[...]
    out_ref[...] = nt_dot(value, jnp.concatenate([value, value * prior[...]], axis=0), FP32)


def fill(panel, ref, at, stretch):
    frames = panel.shape[1]
    for j in range(stretch):
        panel[at * stretch + j] = ref[rows(j, frames), :]


def whole_of(panel):
    return jnp.concatenate([panel[b] for b in range(panel.shape[0])], axis=1)


def forward_kernel(stretch, cols, index, search, blocks, gram, half, keep_ref, send_ref, acc, panel):
    frames = panel.shape[1]
    me = lax.axis_index("row")
    for flip, ref in enumerate(search):
        fill(panel, ref, lax.bitwise_xor(me, flip), stretch)
    acc[...] = jnp.zeros_like(acc)
    for k in range(blocks.shape[0]):
        acc[index[0, k]] += jnp.dot(panel[index[1, k]], blocks[k], preferred_element_type=F32)
    core = lax.rem(lax.axis_index("col"), 2)
    for x in range(cols // 2):
        for j in range(stretch):
            at = rows(x * stretch + j, frames)
            keep_ref[at, :] = acc[(2 * x + core) * stretch + j]
            send_ref[at, :] = acc[(2 * x + 1 - core) * stretch + j]
    at = rows(cols // 2 * stretch, frames)
    value = gram[...]
    if half:
        whole = whole_of(panel)
        inner = nt_dot(whole, jnp.concatenate([whole, jnp.zeros_like(whole)], axis=0))
        lane = lax.broadcasted_iota(jnp.int32, value.shape, 1)
        value = jnp.where(lane < frames, inner, value)
        send_ref[at.stop :, :] = half[0][...]
        keep_ref[at.stop :, :] = half[0][...]
    keep_ref[at, :] = value
    send_ref[at, :] = value


def pair_kernel(frames, keep, received, out_ref, first_refs):
    core = lax.rem(lax.axis_index("col"), 2)
    split_at = frames // 2
    data = out_ref.shape[0] - frames
    for j in range(data // frames):
        at = rows(j, frames)
        out_ref[at, :] = (keep[at, :] + received[at, :]).astype(BF16)
    at = pl.ds(pl.multiple_of(data + core * split_at, split_at), split_at)
    out_ref[data : data + split_at, :], out_ref[data + split_at :, :] = split(
        keep[at, :] + received[at, :]
    )
    if first_refs:
        at = pl.ds(pl.multiple_of(core * split_at, split_at), split_at)
        first_refs[0][at, :] = keep[data + frames :, :]
        at = pl.ds(pl.multiple_of((1 - core) * split_at, split_at), split_at)
        first_refs[0][at, :] = received[data + frames :, :]


def chips_kernel(frames, parts, before, out_ref):
    split_at = frames // 2
    data = out_ref.shape[0] - frames
    for j in range(data // frames):
        at = rows(j, frames)
        out_ref[at, :] = sum_rows(parts, at).astype(BF16)
    high, low = slice(data, data + split_at), slice(data + split_at, data + frames)
    out_ref[high, :], out_ref[low, :] = split(sum_rows(parts, high) + sum_rows(parts, low))


def backward_kernel(
    stretch, cols, last, index, own, received, blocks, before,
    far_refs, near_ref, keep_refs, keep_ref, acc, panel, gram,
):
    frames = panel.shape[1]
    split_at = frames // 2
    core = lax.rem(lax.axis_index("col"), 2)
    data = cols // 2 * stretch * frames
    for ref, side in ((own, core), (received, 1 - core)):
        for x in range(cols // 2):
            for j in range(stretch):
                panel[(2 * x + side) * stretch + j] = ref[rows(x * stretch + j, frames), :]
    if not last:
        fill_gram(gram, own, received, data, frames)
    acc[...] = jnp.zeros_like(acc)
    for k in range(blocks.shape[0]):
        acc[index[1, k]] += jnp.dot(panel[index[0, k]], blocks[k], preferred_element_type=F32)
    me = lax.axis_index("row")
    for far, (far_ref, kept_ref) in enumerate(zip(far_refs, keep_refs)):
        shard = lax.bitwise_xor(me, 2 * (far + 1))
        other = lax.bitwise_xor(shard, 1)
        for j in range(stretch):
            kept_ref[rows(j, frames), :] = acc[shard * stretch + j]
            far_ref[rows(j, frames), :] = acc[other * stretch + j].astype(BF16)
    other = lax.bitwise_xor(me, 1)
    for j in range(stretch):
        keep_ref[rows(j, frames), :] = acc[me * stretch + j]
        near_ref[rows(j, frames), :] = acc[other * stretch + j].astype(BF16)
    if last:
        return
    whole = whole_of(panel)
    total = gram[...] + nt_dot(whole, jnp.concatenate([jnp.zeros_like(whole), whole], axis=0))
    at = stretch * frames
    out_ref = far_refs[0]
    gram[...] = total
    out_ref[at : at + split_at, :], out_ref[at + split_at : at + frames, :] = split(
        gram[pl.ds(pl.multiple_of(core * split_at, split_at), split_at), :]
    )
    lane = lax.broadcasted_iota(jnp.int32, total.shape, 1)
    row = lax.broadcasted_iota(jnp.int32, total.shape, 0)
    on_diagonal = jnp.logical_or(lane == row, lane == row + frames)
    diagonal = jnp.sum(jnp.where(on_diagonal, total, 0.0), axis=0, keepdims=True)
    row = lax.broadcasted_iota(jnp.int32, (DIAG, 2 * frames), 0)
    out_ref[at + frames :, :] = jnp.where(row == 0, diagonal, 0.0).astype(BF16)


def rows_kernel(frames, sent, received, kept, out_refs, gram_refs):
    split_at = frames // 2
    data = kept[0].shape[0]
    for out_ref, kept_ref, received_ref in zip(out_refs, kept, received):
        for j in range(data // frames):
            at = rows(j, frames)
            out_ref[at, :] = (kept_ref[at, :] + received_ref[at, :].astype(F32)).astype(BF16)
    if gram_refs:
        pair = (sent, received[0])
        high, low = slice(data, data + split_at), slice(data + split_at, data + frames)
        value = sum_rows(pair, high) + sum_rows(pair, low)
        block = jnp.concatenate(split(value), axis=0)
        tile = sum_rows(pair, slice(data + frames, data + frames + DIAG)).astype(BF16)
        gram_refs[0][...] = value
        gram_refs[1][...] = tile
        for out_ref in out_refs:
            out_ref[data : data + frames, :] = block
            out_ref[data + frames :, :] = tile


def fill_gram(gram, own, received, data, frames):
    split_at = frames // 2
    core = lax.rem(lax.axis_index("col"), 2)
    for ref, side in ((own, core), (received, 1 - core)):
        at = pl.ds(pl.multiple_of(side * split_at, split_at), split_at)
        gram[at, :] = ref[data : data + split_at, :].astype(F32) + ref[data + split_at :, :].astype(
            F32
        )


def second_gram_kernel(data, own, received, out_ref, norm_ref, gram):
    frames = out_ref.shape[0]
    fill_gram(gram, own, received, data, frames)
    whole = jnp.concatenate(
        [ref[rows(j, frames), :] for ref in (own, received) for j in range(data // frames)], axis=1
    )
    norm_ref[...] = gram[:, :frames]
    value = gram[:, frames:] + nt_dot(whole, whole)
    out_ref[...] = jnp.concatenate(split(value), axis=1)


def second_pair_kernel(own, received, gram_ref, out_ref):
    n = own.shape[0]
    both = own[...].astype(F32) + received[...].astype(F32)
    value = both[:, :n] + both[:, n:]
    gram_ref[...] = value
    out_ref[...] = jnp.concatenate(split(value), axis=1)


def near_kernel(keep, near, sum_ref, cast_ref):
    total = keep[...] + near[...].astype(F32)
    sum_ref[...] = total
    cast_ref[...] = total.astype(BF16)


def own_sum(keep, parts, j, frames):
    at = rows(j, frames)
    return keep[at, :] + sum_rows(parts, at)


def frame_shift(diagonal, frames):
    row = 1.25 * diagonal[:, frames:] / diagonal[:, :frames]
    return jnp.sum(jnp.where(eye(frames), row, 0.0), axis=1, keepdims=True), row


def image_kernel(
    pair_sum, far, gram, tile, v_ref, prior, image_ref, next_ref, cast_ref, half_ref, diag_ref
):
    frames = v_ref.shape[0]
    split_at = frames // 2
    data = cast_ref.shape[0]
    diagonal = tile[...].astype(F32) + sum_rows(far, slice(data + frames, data + frames + DIAG))
    diag_ref[...] = diagonal
    shift, _ = frame_shift(diagonal[0:1, :], frames)
    for j in range(data // frames):
        value = v_ref[:, lanes(j)]
        image = own_sum(pair_sum, far, j, frames) + prior[:, lanes(j)] * value
        following = image - shift * value
        image_ref[:, lanes(j)] = image
        next_ref[:, lanes(j)] = following
        cast_ref[rows(j, frames), :] = following.astype(BF16)
    half_ref[...] = (
        gram[...]
        + sum_rows(far, slice(data, data + split_at))
        + sum_rows(far, slice(data + split_at, data + frames))
    )


def remainder_kernel(v_ref, prior, before, out_ref):
    frames = v_ref.shape[0]
    stretch = v_ref.shape[1] // BLOCK
    for j in range(stretch):
        out_ref[rows(j, frames), :] = split(v_ref[:, lanes(j)])[1]
    terms = [part.astype(F32) for part in split(prior[...])]
    lines = [part[:, lanes(j)] for part in terms for j in range(stretch)]
    lines.append(jnp.zeros((DIAG - len(lines), BLOCK), F32))
    out_ref[stretch * frames :, :] = jnp.concatenate(lines, axis=0).astype(BF16)


def cross_kernel(frames, own, received, high, low, diag_ref, cast_ref):
    stretch = cast_ref.shape[0] // frames
    shift, _ = frame_shift(diag_ref[0:1, :], frames)
    tile = low[stretch * frames :, :].astype(F32)
    for j in range(stretch):
        at = rows(j, frames)
        weight = tile[j : j + 1, :] + tile[stretch + j : stretch + j + 1, :]
        value = sum_rows((high, low), at)
        cast_ref[at, :] = (sum_rows((own, received), at) + (weight - shift) * value).astype(BF16)


def eliminate(matrix, right, n):
    width = matrix.shape[1] + right.shape[1]
    work = jnp.concatenate([matrix, right], axis=1)
    work = [work[rows(i, TILE), :] for i in range(n // TILE)]
    at = lax.broadcasted_iota(jnp.int32, (TILE, width), 0)

    def column(k):
        return [jnp.broadcast_to(t[:, k : k + 1], (TILE, width)) for t in work]

    def step(tiles, spread, k, pivot):
        i, s = divmod(k, TILE)
        row = tiles[i][s : s + 1, :] * pivot
        done = [t - c * row for t, c in zip(tiles, spread)]
        done[i] = jnp.where(at == s, row, done[i])
        return done

    ahead = [column(k) for k in range(AHEAD)]
    for k in range(n):
        i, s = divmod(k, TILE)
        spread = ahead.pop(0)
        pivot = 1.0 / spread[i][s : s + 1, :]
        ahead = [step(later, spread, k, pivot) for later in ahead]
        work = step(work, spread, k, pivot)
        if k + AHEAD < n:
            ahead.append(column(k + AHEAD))
    return jnp.concatenate(work, axis=0)[:, n:]


def inverse_kernel(first, out_ref):
    n = first.shape[0]
    out_ref[...] = eliminate(first[:, n:], jnp.where(eye(n), 1.0, 0.0), n)


def solve_kernel(gram, parts, first, inverse_ref, norm_ref, diag_ref, out_ref):
    n = gram.shape[0]
    norm, energy = first[:, :n], first[:, n:]
    shift, shift_row = frame_shift(diag_ref[0:1, :], n)
    inverse = inverse_ref[...]
    next_rhs = energy - shift * norm
    cross = norm_ref[...] + next_rhs * shift_row
    alpha = nn_dot(inverse, norm)
    conj = nn_dot(inverse, cross.T)
    schur = gram[...] - nn_dot(cross, conj)
    for part in parts:
        both = part[...].astype(F32)
        schur += both[:, :n] + both[:, n:]
    gamma = eliminate(schur, next_rhs - nn_dot(cross, alpha), n)
    out_ref[:n, :] = alpha - nn_dot(conj, gamma)
    out_ref[n:, :] = gamma


def final_kernel(keep, near, far, v_ref, image_ref, next_ref, prior, coeffs_ref, x_ref, r_ref):
    n = v_ref.shape[0]
    coeffs = coeffs_ref[...]
    for j in range(keep.shape[0] // n):
        value = v_ref[:, lanes(j)]
        following = next_ref[:, lanes(j)]
        second_image = own_sum(keep, (near, *far), j, n) + prior[:, lanes(j)] * following
        x_ref[:, lanes(j)] = tn_dot(coeffs, jnp.concatenate([value, following], axis=0))
        r_ref[:, lanes(j)] = value - tn_dot(
            coeffs, jnp.concatenate([image_ref[:, lanes(j)], second_image], axis=0)
        )


def swapped(x, axis, flip):
    return lax.ppermute(x, axis, [(i, i ^ flip) for i in range(lax.axis_size(axis))])


def others(x, axis):
    return (x, *(swapped(x, axis, flip) for flip in range(2, lax.axis_size(axis), 2)))


def gather(x, axis):
    return tuple(part for own in others(x, axis) for part in (own, swapped(own, axis, 1)))


def shards(right_side, prior, blocks, block_row, block_col):
    frames, pix = right_side.shape
    stretch = pix // BLOCK
    n_rows, n_cols = lax.axis_size("row"), lax.axis_size("col")
    row_span, col_span = stretch * n_cols, stretch * n_rows
    prior = prior.reshape(1, pix)
    stored = blocks.shape[0]
    half_cols = n_cols // 2 * stretch * frames

    def shape(dims, dtype=F32):
        return jax.ShapeDtypeStruct(dims, dtype)

    own = shape((frames, pix))
    gram_type = shape((frames, 2 * frames))
    cast_type = shape((stretch * frames, BLOCK), BF16)
    aside = pl.CostEstimate(flops=2 * 10**9, bytes_accessed=8 * 10**6, transcendentals=0)

    pairs = n_rows // 2 - 1

    def forward(search, gram, half):
        size = half_cols + frames + (frames // 2 if half else 0)
        keep, send = call(
            lambda *refs: forward_kernel(stretch, n_cols, *refs),
            (shape((size, BLOCK)),) * 2,
            (index, search, turned, gram, half),
            [
                pltpu.VMEM((row_span, frames, BLOCK), F32),
                pltpu.VMEM((col_span, frames, BLOCK), BF16),
            ],
        )
        received = swapped(send, "col", 1)
        pair, first = call(
            lambda *refs: pair_kernel(frames, *refs),
            (shape((half_cols + frames, BLOCK), BF16), (gram_type,) if half else ()),
            (keep, received),
        )
        if half:
            aside_of_chips = call(inverse_kernel, (shape((frames, frames)),), first, cost=aside)
        elif n_rows == 4:
            (remainder,) = call(
                remainder_kernel,
                (shape((stretch * frames + DIAG, BLOCK), BF16),),
                (right_side, prior, pair),
            )
            aside_of_chips = [swapped(remainder, "row", 2)]
        else:
            aside_of_chips = []
        (foot,) = call(
            lambda *refs: chips_kernel(frames, *refs),
            (shape((half_cols + frames, BLOCK), BF16),),
            (others(pair, "col"), aside_of_chips),
        )
        return (foot, swapped(foot, "col", 1)), (*first, *aside_of_chips)

    def backward(foot, before, last):
        size = stretch * frames
        extra = 0 if last else frames + DIAG
        far, near, kept, keep = call(
            lambda *refs: backward_kernel(stretch, n_cols, last, *refs),
            (
                tuple(shape((size + (0 if p else extra), BLOCK), BF16) for p in range(pairs)),
                shape((size, BLOCK), BF16),
                (shape((size, BLOCK)),) * pairs,
                shape((size, BLOCK)),
            ),
            (index, *foot, blocks, before),
            [
                pltpu.VMEM((col_span, frames, BLOCK), F32),
                pltpu.VMEM((row_span, frames, BLOCK), BF16),
                pltpu.VMEM((frames, 2 * frames), F32),
            ],
        )
        received = tuple(swapped(x, "row", 1) for x in far)
        near = swapped(near, "row", 1)
        sums, gram = call(
            lambda *refs: rows_kernel(frames, *refs),
            (
                (shape((size + extra, BLOCK), BF16),) * pairs,
                ()
                if last
                else (shape((frames // 2, 2 * frames)), shape((DIAG, 2 * frames), BF16)),
            ),
            (far[0], received, kept),
        )
        far = tuple(swapped(x, "row", 2 * (p + 1)) for p, x in enumerate(sums))
        return (keep, near, far, *gram), sums

    (cast,) = call(cast_kernel, (cast_type,), (right_side,))
    search = gather(cast, "row")
    index, turned = call(
        lambda *refs: turn_kernel(row_span, stretch, *refs),
        (shape((2, stored), jnp.int32), shape(blocks.shape, BF16)),
        (block_row, block_col, blocks),
        cost=aside,
    )
    (gram,) = call(gram_kernel, (gram_type,), (right_side, prior), cost=aside)
    foot, remainder = forward(search, gram, ())
    (keep, near, far, gram, tile), sums = backward(foot, (), False)
    pair_sum, pair_cast = call(
        near_kernel, (shape((stretch * frames, BLOCK)), cast_type), (keep, near)
    )
    image, following, cast, half, diagonal = call(
        image_kernel,
        (own, own, cast_type, shape((frames // 2, 2 * frames)), shape((DIAG, 2 * frames))),
        (pair_sum, far, gram, tile, right_side, prior),
    )
    if n_rows == 4:
        (cross,) = call(
            lambda *refs: cross_kernel(frames, *refs),
            (cast_type,),
            (
                sums[0],
                swapped(pair_cast, "row", 2),
                search[2],
                *remainder,
                diagonal,
            ),
        )
        search = (cast, swapped(cast, "row", 1), cross, swapped(cross, "row", 1))
    else:
        search = gather(cast, "row")
    (gram,) = call(gram_kernel, (gram_type,), (following, prior), cost=aside)
    foot, (first, inverse) = forward(search, gram, (half,))
    second, norm = call(
        lambda *refs: second_gram_kernel(half_cols, *refs),
        (shape((frames, 2 * frames), BF16), shape((frames, frames))),
        foot,
        [pltpu.VMEM((frames, 2 * frames), F32)],
    )
    gram, second = call(
        second_pair_kernel,
        (shape((frames, frames)), shape((frames, 2 * frames), BF16)),
        (second, swapped(second, "row", 1)),
    )
    second = others(second, "row")[1:]
    parts, _ = backward(foot, (norm,), True)
    (coeffs,) = call(
        solve_kernel,
        (shape((2 * frames, frames)),),
        (gram, second, first, inverse, norm, diagonal),
        cost=aside,
    )
    return tuple(
        call(
            final_kernel,
            (own, own),
            (*parts, right_side, image, following, prior, coeffs),
        )
    )


def solution(mesh):
    return jax.shard_map(
        shards,
        mesh=mesh,
        in_specs=(
            P("groups", ("row", "col")),
            P(("row", "col")),
            P(("row", "col"), None, None),
            P(("row", "col")),
            P(("row", "col")),
        ),
        out_specs=(P("groups", ("row", "col")), P("groups", ("row", "col"))),
        check_vma=False,
    )
```

```python
import jax
import jax.numpy as jnp
from jax import lax
from jax.experimental import pallas as pl
from jax.experimental.pallas import tpu as pltpu
from jax.sharding import PartitionSpec as P

BLOCK = 128
TILE = 8
AHEAD = 4
DIAG = 16
F32, BF16 = jnp.float32, jnp.bfloat16
FP32 = lax.Precision.HIGHEST
VMEM = pl.BlockSpec(memory_space=pltpu.VMEM)
SMEM = pl.BlockSpec(memory_space=pltpu.SMEM)


def nt_dot(a, b, precision=None):
    return lax.dot_general(
        a, b, (((1,), (1,)), ((), ())), precision=precision, preferred_element_type=F32
    )


def tn_dot(a, b):
    return lax.dot_general(
        a, b, (((0,), (0,)), ((), ())), precision=FP32, preferred_element_type=F32
    )


def nn_dot(a, b):
    return lax.dot_general(
        a, b, (((1,), (0,)), ((), ())), precision=FP32, preferred_element_type=F32
    )


def call(kernel, outs, ins, scratch=(), cost=None):
    flat_ins, ins_tree = jax.tree.flatten(tuple(ins))
    flat_outs, outs_tree = jax.tree.flatten(tuple(outs))

    def body(*refs):
        middle, last = len(flat_ins), len(flat_ins) + len(flat_outs)
        kernel(
            *jax.tree.unflatten(ins_tree, refs[:middle]),
            *jax.tree.unflatten(outs_tree, refs[middle:last]),
            *refs[last:],
        )

    def space(x):
        return SMEM if x.dtype == jnp.int32 else VMEM

    results = pl.pallas_call(
        body,
        out_shape=flat_outs,
        in_specs=[space(x) for x in flat_ins],
        out_specs=[space(x) for x in flat_outs],
        scratch_shapes=list(scratch),
        compiler_params=pltpu.CompilerParams(vmem_limit_bytes=48 * 1024 * 1024),
        cost_estimate=cost,
    )(*flat_ins)
    return jax.tree.unflatten(outs_tree, results)


def lanes(j):
    return slice(j * BLOCK, (j + 1) * BLOCK)


def rows(j, count):
    return slice(j * count, (j + 1) * count)


def split(value):
    high = value.astype(BF16)
    return high, (value - high.astype(F32)).astype(BF16)


def sum_rows(refs, at):
    total = refs[0][at, :].astype(F32)
    for ref in refs[1:]:
        total += ref[at, :].astype(F32)
    return total


def eye(n):
    return lax.broadcasted_iota(jnp.int32, (n, n), 0) == lax.broadcasted_iota(jnp.int32, (n, n), 1)


def cast_kernel(v_ref, out_ref):
    frames = v_ref.shape[0]
    for j in range(v_ref.shape[1] // BLOCK):
        out_ref[rows(j, frames), :] = v_ref[:, lanes(j)].astype(BF16)


def turn_kernel(row_span, stretch, brow, bcol, blocks, index_ref, out_ref):
    for k in range(blocks.shape[0]):
        index_ref[0, k] = lax.rem(brow[k], row_span)
        index_ref[1, k] = lax.div(bcol[k], row_span) * stretch + lax.rem(bcol[k], stretch)
        out_ref[k] = blocks[k].T


def gram_kernel(v_ref, prior, out_ref):
    value = v_ref[...]
    out_ref[...] = nt_dot(value, jnp.concatenate([value, value * prior[...]], axis=0), FP32)


def fill(panel, ref, at, stretch):
    frames = panel.shape[1]
    for j in range(stretch):
        panel[at * stretch + j] = ref[rows(j, frames), :]


def whole_of(panel):
    return jnp.concatenate([panel[b] for b in range(panel.shape[0])], axis=1)


def forward_kernel(stretch, cols, index, search, blocks, gram, half, keep_ref, send_ref, acc, panel):
    frames = panel.shape[1]
    me = lax.axis_index("row")
    for flip, ref in enumerate(search):
        fill(panel, ref, lax.bitwise_xor(me, flip), stretch)
    acc[...] = jnp.zeros_like(acc)
    for k in range(blocks.shape[0]):
        acc[index[0, k]] += jnp.dot(panel[index[1, k]], blocks[k], preferred_element_type=F32)
    core = lax.rem(lax.axis_index("col"), 2)
    for x in range(cols // 2):
        for j in range(stretch):
            at = rows(x * stretch + j, frames)
            keep_ref[at, :] = acc[(2 * x + core) * stretch + j]
            send_ref[at, :] = acc[(2 * x + 1 - core) * stretch + j]
    at = rows(cols // 2 * stretch, frames)
    value = gram[...]
    if half:
        whole = whole_of(panel)
        inner = nt_dot(whole, jnp.concatenate([whole, jnp.zeros_like(whole)], axis=0))
        lane = lax.broadcasted_iota(jnp.int32, value.shape, 1)
        value = jnp.where(lane < frames, inner, value)
        send_ref[at.stop :, :] = half[0][...]
        keep_ref[at.stop :, :] = half[0][...]
    keep_ref[at, :] = value
    send_ref[at, :] = value


def pair_kernel(frames, keep, received, out_ref, first_refs):
    core = lax.rem(lax.axis_index("col"), 2)
    split_at = frames // 2
    data = out_ref.shape[0] - frames
    for j in range(data // frames):
        at = rows(j, frames)
        out_ref[at, :] = (keep[at, :] + received[at, :]).astype(BF16)
    at = pl.ds(pl.multiple_of(data + core * split_at, split_at), split_at)
    out_ref[data : data + split_at, :], out_ref[data + split_at :, :] = split(
        keep[at, :] + received[at, :]
    )
    if first_refs:
        at = pl.ds(pl.multiple_of(core * split_at, split_at), split_at)
        first_refs[0][at, :] = keep[data + frames :, :]
        at = pl.ds(pl.multiple_of((1 - core) * split_at, split_at), split_at)
        first_refs[0][at, :] = received[data + frames :, :]


def chips_kernel(frames, parts, before, out_ref):
    split_at = frames // 2
    data = out_ref.shape[0] - frames
    for j in range(data // frames):
        at = rows(j, frames)
        out_ref[at, :] = sum_rows(parts, at).astype(BF16)
    high, low = slice(data, data + split_at), slice(data + split_at, data + frames)
    out_ref[high, :], out_ref[low, :] = split(sum_rows(parts, high) + sum_rows(parts, low))


def backward_kernel(
    stretch, cols, last, index, own, received, blocks,
    far_refs, near_ref, keep_refs, keep_ref, norm_refs, acc, panel, gram,
):
    frames = panel.shape[1]
    split_at = frames // 2
    core = lax.rem(lax.axis_index("col"), 2)
    data = cols // 2 * stretch * frames
    for ref, side in ((own, core), (received, 1 - core)):
        for x in range(cols // 2):
            for j in range(stretch):
                panel[(2 * x + side) * stretch + j] = ref[rows(x * stretch + j, frames), :]
    fill_gram(gram, own, received, data, frames)
    acc[...] = jnp.zeros_like(acc)
    for k in range(blocks.shape[0]):
        acc[index[1, k]] += jnp.dot(panel[index[0, k]], blocks[k], preferred_element_type=F32)
    me = lax.axis_index("row")
    for far, (far_ref, kept_ref) in enumerate(zip(far_refs, keep_refs)):
        shard = lax.bitwise_xor(me, 2 * (far + 1))
        other = lax.bitwise_xor(shard, 1)
        for j in range(stretch):
            kept_ref[rows(j, frames), :] = acc[shard * stretch + j]
            far_ref[rows(j, frames), :] = acc[other * stretch + j].astype(BF16)
    other = lax.bitwise_xor(me, 1)
    for j in range(stretch):
        keep_ref[rows(j, frames), :] = acc[me * stretch + j]
        near_ref[rows(j, frames), :] = acc[other * stretch + j].astype(BF16)
    if last:
        norm_refs[0][...] = gram[:, :frames]
        return
    whole = whole_of(panel)
    total = gram[...] + nt_dot(whole, jnp.concatenate([jnp.zeros_like(whole), whole], axis=0))
    at = stretch * frames
    out_ref = far_refs[0]
    gram[...] = total
    out_ref[at : at + split_at, :], out_ref[at + split_at : at + frames, :] = split(
        gram[pl.ds(pl.multiple_of(core * split_at, split_at), split_at), :]
    )
    lane = lax.broadcasted_iota(jnp.int32, total.shape, 1)
    row = lax.broadcasted_iota(jnp.int32, total.shape, 0)
    on_diagonal = jnp.logical_or(lane == row, lane == row + frames)
    diagonal = jnp.sum(jnp.where(on_diagonal, total, 0.0), axis=0, keepdims=True)
    row = lax.broadcasted_iota(jnp.int32, (DIAG, 2 * frames), 0)
    out_ref[at + frames :, :] = jnp.where(row == 0, diagonal, 0.0).astype(BF16)


def rows_kernel(frames, sent, received, kept, before, out_refs, gram_refs):
    split_at = frames // 2
    data = kept[0].shape[0]
    for out_ref, kept_ref, received_ref in zip(out_refs, kept, received):
        for j in range(data // frames):
            at = rows(j, frames)
            out_ref[at, :] = (kept_ref[at, :] + received_ref[at, :].astype(F32)).astype(BF16)
    if gram_refs:
        pair = (sent, received[0])
        high, low = slice(data, data + split_at), slice(data + split_at, data + frames)
        value = sum_rows(pair, high) + sum_rows(pair, low)
        block = jnp.concatenate(split(value), axis=0)
        tile = sum_rows(pair, slice(data + frames, data + frames + DIAG)).astype(BF16)
        gram_refs[0][...] = value
        gram_refs[1][...] = tile
        for out_ref in out_refs:
            out_ref[data : data + frames, :] = block
            out_ref[data + frames :, :] = tile


def fill_gram(gram, own, received, data, frames):
    split_at = frames // 2
    core = lax.rem(lax.axis_index("col"), 2)
    for ref, side in ((own, core), (received, 1 - core)):
        at = pl.ds(pl.multiple_of(side * split_at, split_at), split_at)
        gram[at, :] = ref[data : data + split_at, :].astype(F32) + ref[data + split_at :, :].astype(
            F32
        )


def second_gram_kernel(data, own, received, out_ref, gram):
    frames = out_ref.shape[0]
    fill_gram(gram, own, received, data, frames)
    whole = jnp.concatenate(
        [ref[rows(j, frames), :] for ref in (own, received) for j in range(data // frames)], axis=1
    )
    value = gram[:, frames:] + nt_dot(whole, whole)
    out_ref[...] = jnp.concatenate(split(value), axis=1)


def second_pair_kernel(own, received, gram_ref, out_ref):
    n = own.shape[0]
    both = own[...].astype(F32) + received[...].astype(F32)
    value = both[:, :n] + both[:, n:]
    gram_ref[...] = value
    out_ref[...] = jnp.concatenate(split(value), axis=1)


def near_kernel(keep, near, sum_ref, cast_ref):
    total = keep[...] + near[...].astype(F32)
    sum_ref[...] = total
    cast_ref[...] = total.astype(BF16)


def own_sum(keep, parts, j, frames):
    at = rows(j, frames)
    return keep[at, :] + sum_rows(parts, at)


def frame_shift(diagonal, frames):
    row = 1.25 * diagonal[:, frames:] / diagonal[:, :frames]
    return jnp.sum(jnp.where(eye(frames), row, 0.0), axis=1, keepdims=True), row


def image_kernel(
    pair_sum, far, gram, tile, v_ref, prior, image_ref, next_ref, cast_ref, half_ref, diag_ref
):
    frames = v_ref.shape[0]
    split_at = frames // 2
    data = cast_ref.shape[0]
    diagonal = tile[...].astype(F32) + sum_rows(far, slice(data + frames, data + frames + DIAG))
    diag_ref[...] = diagonal
    shift, _ = frame_shift(diagonal[0:1, :], frames)
    for j in range(data // frames):
        value = v_ref[:, lanes(j)]
        image = own_sum(pair_sum, far, j, frames) + prior[:, lanes(j)] * value
        following = image - shift * value
        image_ref[:, lanes(j)] = image
        next_ref[:, lanes(j)] = following
        cast_ref[rows(j, frames), :] = following.astype(BF16)
    half_ref[...] = (
        gram[...]
        + sum_rows(far, slice(data, data + split_at))
        + sum_rows(far, slice(data + split_at, data + frames))
    )


def remainder_kernel(v_ref, prior, before, out_ref):
    frames = v_ref.shape[0]
    stretch = v_ref.shape[1] // BLOCK
    for j in range(stretch):
        out_ref[rows(j, frames), :] = split(v_ref[:, lanes(j)])[1]
    terms = [part.astype(F32) for part in split(prior[...])]
    lines = [part[:, lanes(j)] for part in terms for j in range(stretch)]
    lines.append(jnp.zeros((DIAG - len(lines), BLOCK), F32))
    out_ref[stretch * frames :, :] = jnp.concatenate(lines, axis=0).astype(BF16)


def cross_kernel(frames, own, received, high, low, diag_ref, cast_ref):
    stretch = cast_ref.shape[0] // frames
    shift, _ = frame_shift(diag_ref[0:1, :], frames)
    tile = low[stretch * frames :, :].astype(F32)
    for j in range(stretch):
        at = rows(j, frames)
        weight = tile[j : j + 1, :] + tile[stretch + j : stretch + j + 1, :]
        value = sum_rows((high, low), at)
        cast_ref[at, :] = (sum_rows((own, received), at) + (weight - shift) * value).astype(BF16)


def eliminate(matrix, right, n):
    width = matrix.shape[1] + right.shape[1]
    work = jnp.concatenate([matrix, right], axis=1)
    work = [work[rows(i, TILE), :] for i in range(n // TILE)]
    at = lax.broadcasted_iota(jnp.int32, (TILE, width), 0)

    def column(k):
        return [jnp.broadcast_to(t[:, k : k + 1], (TILE, width)) for t in work]

    def step(tiles, spread, k, pivot):
        i, s = divmod(k, TILE)
        row = tiles[i][s : s + 1, :] * pivot
        done = [t - c * row for t, c in zip(tiles, spread)]
        done[i] = jnp.where(at == s, row, done[i])
        return done

    ahead = [column(k) for k in range(AHEAD)]
    for k in range(n):
        i, s = divmod(k, TILE)
        spread = ahead.pop(0)
        pivot = 1.0 / spread[i][s : s + 1, :]
        ahead = [step(later, spread, k, pivot) for later in ahead]
        work = step(work, spread, k, pivot)
        if k + AHEAD < n:
            ahead.append(column(k + AHEAD))
    return jnp.concatenate(work, axis=0)[:, n:]


def inverse_kernel(first, out_ref):
    n = first.shape[0]
    out_ref[...] = eliminate(first[:, n:], jnp.where(eye(n), 1.0, 0.0), n)


def middle_kernel(first, inverse_ref, norm_ref, diag_ref, out_ref):
    n = first.shape[0]
    norm, energy = first[:, :n], first[:, n:]
    shift, shift_row = frame_shift(diag_ref[0:1, :], n)
    inverse = inverse_ref[...]
    next_rhs = energy - shift * norm
    cross = norm_ref[...] + next_rhs * shift_row
    alpha = nn_dot(inverse, norm)
    conj = nn_dot(inverse, cross.T)
    out_ref[0] = alpha
    out_ref[1] = conj
    out_ref[2] = nn_dot(cross, conj)
    out_ref[3] = next_rhs - nn_dot(cross, alpha)


def solve_kernel(gram, parts, middle, out_ref):
    n = gram.shape[0]
    schur = gram[...] - middle[2]
    for part in parts:
        both = part[...].astype(F32)
        schur += both[:, :n] + both[:, n:]
    gamma = eliminate(schur, middle[3], n)
    out_ref[:n, :] = middle[0] - nn_dot(middle[1], gamma)
    out_ref[n:, :] = gamma


def early_kernel(keep, near, v_ref, image_ref, next_ref, prior, coeffs_ref, x_ref, base_ref):
    n = v_ref.shape[0]
    coeffs = coeffs_ref[...]
    for j in range(keep.shape[0] // n):
        value = v_ref[:, lanes(j)]
        following = next_ref[:, lanes(j)]
        second_image = own_sum(keep, (near,), j, n) + prior[:, lanes(j)] * following
        x_ref[:, lanes(j)] = tn_dot(coeffs, jnp.concatenate([value, following], axis=0))
        base_ref[:, lanes(j)] = value - tn_dot(
            coeffs, jnp.concatenate([image_ref[:, lanes(j)], second_image], axis=0)
        )


def final_kernel(far, base_ref, coeffs_ref, r_ref):
    n = base_ref.shape[0]
    gamma = coeffs_ref[n:, :]
    for j in range(base_ref.shape[1] // BLOCK):
        r_ref[:, lanes(j)] = base_ref[:, lanes(j)] - tn_dot(gamma, sum_rows(far, rows(j, n)))


def swapped(x, axis, flip):
    return lax.ppermute(x, axis, [(i, i ^ flip) for i in range(lax.axis_size(axis))])


def others(x, axis):
    return (x, *(swapped(x, axis, flip) for flip in range(2, lax.axis_size(axis), 2)))


def gather(x, axis):
    return tuple(part for own in others(x, axis) for part in (own, swapped(own, axis, 1)))


def shards(right_side, prior, blocks, block_row, block_col):
    frames, pix = right_side.shape
    stretch = pix // BLOCK
    n_rows, n_cols = lax.axis_size("row"), lax.axis_size("col")
    row_span, col_span = stretch * n_cols, stretch * n_rows
    prior = prior.reshape(1, pix)
    stored = blocks.shape[0]
    half_cols = n_cols // 2 * stretch * frames

    def shape(dims, dtype=F32):
        return jax.ShapeDtypeStruct(dims, dtype)

    own = shape((frames, pix))
    gram_type = shape((frames, 2 * frames))
    cast_type = shape((stretch * frames, BLOCK), BF16)
    aside = pl.CostEstimate(flops=2 * 10**9, bytes_accessed=8 * 10**6, transcendentals=0)

    pairs = n_rows // 2 - 1

    def forward(search, gram, half):
        size = half_cols + frames + (frames // 2 if half else 0)
        keep, send = call(
            lambda *refs: forward_kernel(stretch, n_cols, *refs),
            (shape((size, BLOCK)),) * 2,
            (index, search, turned, gram, half),
            [
                pltpu.VMEM((row_span, frames, BLOCK), F32),
                pltpu.VMEM((col_span, frames, BLOCK), BF16),
            ],
        )
        received = swapped(send, "col", 1)
        pair, first = call(
            lambda *refs: pair_kernel(frames, *refs),
            (shape((half_cols + frames, BLOCK), BF16), (gram_type,) if half else ()),
            (keep, received),
        )
        if half:
            aside_of_chips = call(inverse_kernel, (shape((frames, frames)),), first, cost=aside)
        elif n_rows == 4:
            (remainder,) = call(
                remainder_kernel,
                (shape((stretch * frames + DIAG, BLOCK), BF16),),
                (right_side, prior, pair),
            )
            aside_of_chips = [swapped(remainder, "row", 2)]
        else:
            aside_of_chips = []
        (foot,) = call(
            lambda *refs: chips_kernel(frames, *refs),
            (shape((half_cols + frames, BLOCK), BF16),),
            (others(pair, "col"), aside_of_chips),
        )
        return (foot, swapped(foot, "col", 1)), (*first, *aside_of_chips)

    def backward(foot, last):
        size = stretch * frames
        extra = 0 if last else frames + DIAG
        far, near, kept, keep, norm = call(
            lambda *refs: backward_kernel(stretch, n_cols, last, *refs),
            (
                tuple(shape((size + (0 if p else extra), BLOCK), BF16) for p in range(pairs)),
                shape((size, BLOCK), BF16),
                (shape((size, BLOCK)),) * pairs,
                shape((size, BLOCK)),
                (shape((frames, frames)),) if last else (),
            ),
            (index, *foot, blocks),
            [
                pltpu.VMEM((col_span, frames, BLOCK), F32),
                pltpu.VMEM((row_span, frames, BLOCK), BF16),
                pltpu.VMEM((frames, 2 * frames), F32),
            ],
        )
        received = tuple(swapped(x, "row", 1) for x in far)
        near = swapped(near, "row", 1)
        middle = ()
        if last:
            middle = call(
                middle_kernel,
                (shape((4, frames, frames)),),
                (first, inverse, *norm, diagonal),
                cost=aside,
            )
        sums, gram = call(
            lambda *refs: rows_kernel(frames, *refs),
            (
                (shape((size + extra, BLOCK), BF16),) * pairs,
                ()
                if last
                else (shape((frames // 2, 2 * frames)), shape((DIAG, 2 * frames), BF16)),
            ),
            (far[0], received, kept, middle),
        )
        far = tuple(swapped(x, "row", 2 * (p + 1)) for p, x in enumerate(sums))
        return (keep, near, far, *gram), (middle if last else sums)

    (cast,) = call(cast_kernel, (cast_type,), (right_side,))
    search = gather(cast, "row")
    index, turned = call(
        lambda *refs: turn_kernel(row_span, stretch, *refs),
        (shape((2, stored), jnp.int32), shape(blocks.shape, BF16)),
        (block_row, block_col, blocks),
        cost=aside,
    )
    (gram,) = call(gram_kernel, (gram_type,), (right_side, prior), cost=aside)
    foot, remainder = forward(search, gram, ())
    (keep, near, far, gram, tile), sums = backward(foot, False)
    pair_sum, pair_cast = call(
        near_kernel, (shape((stretch * frames, BLOCK)), cast_type), (keep, near)
    )
    image, following, cast, half, diagonal = call(
        image_kernel,
        (own, own, cast_type, shape((frames // 2, 2 * frames)), shape((DIAG, 2 * frames))),
        (pair_sum, far, gram, tile, right_side, prior),
    )
    if n_rows == 4:
        (cross,) = call(
            lambda *refs: cross_kernel(frames, *refs),
            (cast_type,),
            (
                sums[0],
                swapped(pair_cast, "row", 2),
                search[2],
                *remainder,
                diagonal,
            ),
        )
        search = (cast, swapped(cast, "row", 1), cross, swapped(cross, "row", 1))
    else:
        search = gather(cast, "row")
    (gram,) = call(gram_kernel, (gram_type,), (following, prior), cost=aside)
    foot, (first, inverse) = forward(search, gram, (half,))
    (second,) = call(
        lambda *refs: second_gram_kernel(half_cols, *refs),
        (shape((frames, 2 * frames), BF16),),
        foot,
        [pltpu.VMEM((frames, 2 * frames), F32)],
    )
    gram, second = call(
        second_pair_kernel,
        (shape((frames, frames)), shape((frames, 2 * frames), BF16)),
        (second, swapped(second, "row", 1)),
    )
    second = others(second, "row")[1:]
    parts, middle = backward(foot, True)
    (coeffs,) = call(
        solve_kernel, (shape((2 * frames, frames)),), (gram, second, *middle), cost=aside
    )
    keep, near, far = parts
    x, base = call(
        early_kernel,
        (own, own),
        (keep, near, right_side, image, following, prior, coeffs),
        cost=aside,
    )
    (residual,) = call(final_kernel, (own,), (far, base, coeffs))
    return x, residual


def solution(mesh):
    return jax.shard_map(
        shards,
        mesh=mesh,
        in_specs=(
            P("groups", ("row", "col")),
            P(("row", "col")),
            P(("row", "col"), None, None),
            P(("row", "col")),
            P(("row", "col")),
        ),
        out_specs=(P("groups", ("row", "col")), P("groups", ("row", "col"))),
        check_vma=False,
    )
```

```python
import jax
import jax.numpy as jnp
from jax import lax
from jax.experimental import pallas as pl
from jax.experimental.pallas import tpu as pltpu
from jax.sharding import PartitionSpec as P

BLOCK = 128
TILE = 8
AHEAD = 4
DIAG = 16
F32, BF16 = jnp.float32, jnp.bfloat16
FP32 = lax.Precision.HIGHEST
VMEM = pl.BlockSpec(memory_space=pltpu.VMEM)
SMEM = pl.BlockSpec(memory_space=pltpu.SMEM)


def nt_dot(a, b, precision=None):
    return lax.dot_general(
        a, b, (((1,), (1,)), ((), ())), precision=precision, preferred_element_type=F32
    )


def tn_dot(a, b):
    return lax.dot_general(
        a, b, (((0,), (0,)), ((), ())), precision=FP32, preferred_element_type=F32
    )


def nn_dot(a, b):
    return lax.dot_general(
        a, b, (((1,), (0,)), ((), ())), precision=FP32, preferred_element_type=F32
    )


def call(kernel, outs, ins, scratch=(), cost=None):
    flat_ins, ins_tree = jax.tree.flatten(tuple(ins))
    flat_outs, outs_tree = jax.tree.flatten(tuple(outs))

    def body(*refs):
        middle, last = len(flat_ins), len(flat_ins) + len(flat_outs)
        kernel(
            *jax.tree.unflatten(ins_tree, refs[:middle]),
            *jax.tree.unflatten(outs_tree, refs[middle:last]),
            *refs[last:],
        )

    def space(x):
        return SMEM if x.dtype == jnp.int32 else VMEM

    results = pl.pallas_call(
        body,
        out_shape=flat_outs,
        in_specs=[space(x) for x in flat_ins],
        out_specs=[space(x) for x in flat_outs],
        scratch_shapes=list(scratch),
        compiler_params=pltpu.CompilerParams(vmem_limit_bytes=48 * 1024 * 1024),
        cost_estimate=cost,
    )(*flat_ins)
    return jax.tree.unflatten(outs_tree, results)


def lanes(j):
    return slice(j * BLOCK, (j + 1) * BLOCK)


def rows(j, count):
    return slice(j * count, (j + 1) * count)


def split(value):
    high = value.astype(BF16)
    return high, (value - high.astype(F32)).astype(BF16)


def sum_rows(refs, at):
    total = refs[0][at, :].astype(F32)
    for ref in refs[1:]:
        total += ref[at, :].astype(F32)
    return total


def eye(n):
    return lax.broadcasted_iota(jnp.int32, (n, n), 0) == lax.broadcasted_iota(jnp.int32, (n, n), 1)


def cast_kernel(v_ref, out_ref):
    frames = v_ref.shape[0]
    for j in range(v_ref.shape[1] // BLOCK):
        out_ref[rows(j, frames), :] = v_ref[:, lanes(j)].astype(BF16)


def turn_kernel(row_span, stretch, brow, bcol, blocks, index_ref, out_ref):
    for k in range(blocks.shape[0]):
        index_ref[0, k] = lax.rem(brow[k], row_span)
        index_ref[1, k] = lax.div(bcol[k], row_span) * stretch + lax.rem(bcol[k], stretch)
        out_ref[k] = blocks[k].T


def gram_kernel(v_ref, prior, out_ref):
    value = v_ref[...]
    out_ref[...] = nt_dot(value, jnp.concatenate([value, value * prior[...]], axis=0), FP32)


def fill(panel, ref, at, stretch):
    frames = panel.shape[1]
    for j in range(stretch):
        panel[at * stretch + j] = ref[rows(j, frames), :]


def whole_of(panel):
    return jnp.concatenate([panel[b] for b in range(panel.shape[0])], axis=1)


def forward_kernel(stretch, cols, index, search, blocks, gram, half, keep_ref, send_ref, acc, panel):
    frames = panel.shape[1]
    me = lax.axis_index("row")
    for flip, ref in enumerate(search):
        fill(panel, ref, lax.bitwise_xor(me, flip), stretch)
    acc[...] = jnp.zeros_like(acc)
    for k in range(blocks.shape[0]):
        acc[index[0, k]] += jnp.dot(panel[index[1, k]], blocks[k], preferred_element_type=F32)
    core = lax.rem(lax.axis_index("col"), 2)
    for x in range(cols // 2):
        for j in range(stretch):
            at = rows(x * stretch + j, frames)
            keep_ref[at, :] = acc[(2 * x + core) * stretch + j]
            send_ref[at, :] = acc[(2 * x + 1 - core) * stretch + j]
    at = rows(cols // 2 * stretch, frames)
    value = gram[...]
    if half:
        whole = whole_of(panel)
        inner = nt_dot(whole, jnp.concatenate([whole, jnp.zeros_like(whole)], axis=0))
        lane = lax.broadcasted_iota(jnp.int32, value.shape, 1)
        value = jnp.where(lane < frames, inner, value)
        send_ref[at.stop :, :] = half[0][...]
        keep_ref[at.stop :, :] = half[0][...]
    keep_ref[at, :] = value
    send_ref[at, :] = value


def pair_kernel(frames, keep, received, out_ref, first_refs):
    core = lax.rem(lax.axis_index("col"), 2)
    split_at = frames // 2
    data = out_ref.shape[0] - frames
    for j in range(data // frames):
        at = rows(j, frames)
        out_ref[at, :] = (keep[at, :] + received[at, :]).astype(BF16)
    at = pl.ds(pl.multiple_of(data + core * split_at, split_at), split_at)
    out_ref[data : data + split_at, :], out_ref[data + split_at :, :] = split(
        keep[at, :] + received[at, :]
    )
    if first_refs:
        at = pl.ds(pl.multiple_of(core * split_at, split_at), split_at)
        first_refs[0][at, :] = keep[data + frames :, :]
        at = pl.ds(pl.multiple_of((1 - core) * split_at, split_at), split_at)
        first_refs[0][at, :] = received[data + frames :, :]


def chips_kernel(frames, parts, before, out_ref):
    split_at = frames // 2
    data = out_ref.shape[0] - frames
    for j in range(data // frames):
        at = rows(j, frames)
        out_ref[at, :] = sum_rows(parts, at).astype(BF16)
    high, low = slice(data, data + split_at), slice(data + split_at, data + frames)
    out_ref[high, :], out_ref[low, :] = split(sum_rows(parts, high) + sum_rows(parts, low))


def backward_kernel(
    stretch, cols, last, index, own, received, blocks,
    far_refs, near_ref, keep_refs, keep_ref, norm_refs, acc, panel, gram,
):
    frames = panel.shape[1]
    split_at = frames // 2
    core = lax.rem(lax.axis_index("col"), 2)
    data = cols // 2 * stretch * frames
    for ref, side in ((own, core), (received, 1 - core)):
        for x in range(cols // 2):
            for j in range(stretch):
                panel[(2 * x + side) * stretch + j] = ref[rows(x * stretch + j, frames), :]
    fill_gram(gram, own, received, data, frames)
    acc[...] = jnp.zeros_like(acc)
    for k in range(blocks.shape[0]):
        acc[index[1, k]] += jnp.dot(panel[index[0, k]], blocks[k], preferred_element_type=F32)
    me = lax.axis_index("row")
    for far, (far_ref, kept_ref) in enumerate(zip(far_refs, keep_refs)):
        shard = lax.bitwise_xor(me, 2 * (far + 1))
        other = lax.bitwise_xor(shard, 1)
        for j in range(stretch):
            kept_ref[rows(j, frames), :] = acc[shard * stretch + j]
            far_ref[rows(j, frames), :] = acc[other * stretch + j].astype(BF16)
    other = lax.bitwise_xor(me, 1)
    for j in range(stretch):
        keep_ref[rows(j, frames), :] = acc[me * stretch + j]
        near_ref[rows(j, frames), :] = acc[other * stretch + j].astype(BF16)
    if last:
        norm_refs[0][...] = gram[:, :frames]
        return
    whole = whole_of(panel)
    total = gram[...] + nt_dot(whole, jnp.concatenate([jnp.zeros_like(whole), whole], axis=0))
    at = stretch * frames
    out_ref = far_refs[0]
    gram[...] = total
    out_ref[at : at + split_at, :], out_ref[at + split_at : at + frames, :] = split(
        gram[pl.ds(pl.multiple_of(core * split_at, split_at), split_at), :]
    )
    lane = lax.broadcasted_iota(jnp.int32, total.shape, 1)
    row = lax.broadcasted_iota(jnp.int32, total.shape, 0)
    on_diagonal = jnp.logical_or(lane == row, lane == row + frames)
    diagonal = jnp.sum(jnp.where(on_diagonal, total, 0.0), axis=0, keepdims=True)
    row = lax.broadcasted_iota(jnp.int32, (DIAG, 2 * frames), 0)
    out_ref[at + frames :, :] = jnp.where(row == 0, diagonal, 0.0).astype(BF16)


def rows_kernel(frames, sent, received, kept, out_refs, extra_refs):
    split_at = frames // 2
    data = kept[0].shape[0]
    for out_ref, kept_ref, received_ref in zip(out_refs, kept, received):
        for j in range(data // frames):
            at = rows(j, frames)
            out_ref[at, :] = (kept_ref[at, :] + received_ref[at, :].astype(F32)).astype(BF16)
    if extra_refs:
        pair = (sent, received[0])
        high, low = slice(data, data + split_at), slice(data + split_at, data + frames)
        value = sum_rows(pair, high) + sum_rows(pair, low)
        block = jnp.concatenate(split(value), axis=0)
        tile = sum_rows(pair, slice(data + frames, data + frames + DIAG)).astype(BF16)
        extra_refs[0][...] = value
        extra_refs[1][...] = tile
        for out_ref in out_refs:
            out_ref[data : data + frames, :] = block
            out_ref[data + frames :, :] = tile


def fill_gram(gram, own, received, data, frames):
    split_at = frames // 2
    core = lax.rem(lax.axis_index("col"), 2)
    for ref, side in ((own, core), (received, 1 - core)):
        at = pl.ds(pl.multiple_of(side * split_at, split_at), split_at)
        gram[at, :] = ref[data : data + split_at, :].astype(F32) + ref[data + split_at :, :].astype(
            F32
        )


def second_gram_kernel(data, own, received, out_ref, gram):
    frames = out_ref.shape[0]
    fill_gram(gram, own, received, data, frames)
    whole = jnp.concatenate(
        [ref[rows(j, frames), :] for ref in (own, received) for j in range(data // frames)], axis=1
    )
    value = gram[:, frames:] + nt_dot(whole, whole)
    out_ref[...] = jnp.concatenate(split(value), axis=1)


def second_pair_kernel(own, received, gram_ref, out_ref):
    n = own.shape[0]
    both = own[...].astype(F32) + received[...].astype(F32)
    value = both[:, :n] + both[:, n:]
    gram_ref[...] = value
    out_ref[...] = jnp.concatenate(split(value), axis=1)


def near_kernel(keep, near, sum_ref, cast_ref):
    total = keep[...] + near[...].astype(F32)
    sum_ref[...] = total
    cast_ref[...] = total.astype(BF16)


def own_sum(keep, parts, j, frames):
    at = rows(j, frames)
    return keep[at, :] + sum_rows(parts, at)


def frame_shift(diagonal, frames):
    row = 1.25 * diagonal[:, frames:] / diagonal[:, :frames]
    return jnp.sum(jnp.where(eye(frames), row, 0.0), axis=1, keepdims=True), row


def image_kernel(
    pair_sum, far, gram, tile, v_ref, prior, image_ref, next_ref, cast_ref, half_ref, diag_ref
):
    frames = v_ref.shape[0]
    split_at = frames // 2
    data = cast_ref.shape[0]
    diagonal = tile[...].astype(F32) + sum_rows(far, slice(data + frames, data + frames + DIAG))
    diag_ref[...] = diagonal
    shift, _ = frame_shift(diagonal[0:1, :], frames)
    for j in range(data // frames):
        value = v_ref[:, lanes(j)]
        image = own_sum(pair_sum, far, j, frames) + prior[:, lanes(j)] * value
        following = image - shift * value
        image_ref[:, lanes(j)] = image
        next_ref[:, lanes(j)] = following
        cast_ref[rows(j, frames), :] = following.astype(BF16)
    half_ref[...] = (
        gram[...]
        + sum_rows(far, slice(data, data + split_at))
        + sum_rows(far, slice(data + split_at, data + frames))
    )


def remainder_kernel(v_ref, prior, before, out_ref):
    frames = v_ref.shape[0]
    stretch = v_ref.shape[1] // BLOCK
    for j in range(stretch):
        out_ref[rows(j, frames), :] = split(v_ref[:, lanes(j)])[1]
    terms = [part.astype(F32) for part in split(prior[...])]
    lines = [part[:, lanes(j)] for part in terms for j in range(stretch)]
    lines.append(jnp.zeros((DIAG - len(lines), BLOCK), F32))
    out_ref[stretch * frames :, :] = jnp.concatenate(lines, axis=0).astype(BF16)


def cross_kernel(frames, own, received, high, low, diag_ref, cast_ref):
    stretch = cast_ref.shape[0] // frames
    shift, _ = frame_shift(diag_ref[0:1, :], frames)
    tile = low[stretch * frames :, :].astype(F32)
    for j in range(stretch):
        at = rows(j, frames)
        weight = tile[j : j + 1, :] + tile[stretch + j : stretch + j + 1, :]
        value = sum_rows((high, low), at)
        cast_ref[at, :] = (sum_rows((own, received), at) + (weight - shift) * value).astype(BF16)


def eliminate(matrix, right, n):
    width = matrix.shape[1] + right.shape[1]
    work = jnp.concatenate([matrix, right], axis=1)
    work = [work[rows(i, TILE), :] for i in range(n // TILE)]
    at = lax.broadcasted_iota(jnp.int32, (TILE, width), 0)

    def column(k):
        return [jnp.broadcast_to(t[:, k : k + 1], (TILE, width)) for t in work]

    def step(tiles, spread, k, pivot):
        i, s = divmod(k, TILE)
        row = tiles[i][s : s + 1, :] * pivot
        done = [t - c * row for t, c in zip(tiles, spread)]
        done[i] = jnp.where(at == s, row, done[i])
        return done

    ahead = [column(k) for k in range(AHEAD)]
    for k in range(n):
        i, s = divmod(k, TILE)
        spread = ahead.pop(0)
        pivot = 1.0 / spread[i][s : s + 1, :]
        ahead = [step(later, spread, k, pivot) for later in ahead]
        work = step(work, spread, k, pivot)
        if k + AHEAD < n:
            ahead.append(column(k + AHEAD))
    return jnp.concatenate(work, axis=0)[:, n:]


def inverse_kernel(first, out_ref):
    n = first.shape[0]
    out_ref[...] = eliminate(first[:, n:], jnp.where(eye(n), 1.0, 0.0), n)


def solve_kernel(gram, parts, first, inverse_ref, norm_ref, diag_ref, out_ref):
    n = gram.shape[0]
    norm, energy = first[:, :n], first[:, n:]
    shift, shift_row = frame_shift(diag_ref[0:1, :], n)
    inverse = inverse_ref[...]
    next_rhs = energy - shift * norm
    cross = norm_ref[...] + next_rhs * shift_row
    alpha = nn_dot(inverse, norm)
    conj = nn_dot(inverse, cross.T)
    schur = gram[...] - nn_dot(cross, conj)
    for part in parts:
        both = part[...].astype(F32)
        schur += both[:, :n] + both[:, n:]
    gamma = eliminate(schur, next_rhs - nn_dot(cross, alpha), n)
    out_ref[:n, :] = alpha - nn_dot(conj, gamma)
    out_ref[n:, :] = gamma


def early_kernel(keep, near, v_ref, image_ref, next_ref, prior, coeffs_ref, x_ref, base_ref):
    n = v_ref.shape[0]
    coeffs = coeffs_ref[...]
    for j in range(keep.shape[0] // n):
        value = v_ref[:, lanes(j)]
        following = next_ref[:, lanes(j)]
        second_image = own_sum(keep, (near,), j, n) + prior[:, lanes(j)] * following
        x_ref[:, lanes(j)] = tn_dot(coeffs, jnp.concatenate([value, following], axis=0))
        base_ref[:, lanes(j)] = value - tn_dot(
            coeffs, jnp.concatenate([image_ref[:, lanes(j)], second_image], axis=0)
        )


def final_kernel(far, base_ref, coeffs_ref, r_ref):
    n = base_ref.shape[0]
    gamma = coeffs_ref[n:, :]
    for j in range(base_ref.shape[1] // BLOCK):
        r_ref[:, lanes(j)] = base_ref[:, lanes(j)] - tn_dot(gamma, sum_rows(far, rows(j, n)))


def swapped(x, axis, flip):
    return lax.ppermute(x, axis, [(i, i ^ flip) for i in range(lax.axis_size(axis))])


def others(x, axis):
    return (x, *(swapped(x, axis, flip) for flip in range(2, lax.axis_size(axis), 2)))


def gather(x, axis):
    return tuple(part for own in others(x, axis) for part in (own, swapped(own, axis, 1)))


def shards(right_side, prior, blocks, block_row, block_col):
    frames, pix = right_side.shape
    stretch = pix // BLOCK
    n_rows, n_cols = lax.axis_size("row"), lax.axis_size("col")
    row_span, col_span = stretch * n_cols, stretch * n_rows
    prior = prior.reshape(1, pix)
    stored = blocks.shape[0]
    half_cols = n_cols // 2 * stretch * frames

    def shape(dims, dtype=F32):
        return jax.ShapeDtypeStruct(dims, dtype)

    own = shape((frames, pix))
    gram_type = shape((frames, 2 * frames))
    cast_type = shape((stretch * frames, BLOCK), BF16)
    aside = pl.CostEstimate(flops=2 * 10**9, bytes_accessed=8 * 10**6, transcendentals=0)

    hidden = pl.CostEstimate(flops=1, bytes_accessed=1, transcendentals=0)
    pairs = n_rows // 2 - 1

    def forward(search, gram, half):
        size = half_cols + frames + (frames // 2 if half else 0)
        keep, send = call(
            lambda *refs: forward_kernel(stretch, n_cols, *refs),
            (shape((size, BLOCK)),) * 2,
            (index, search, turned, gram, half),
            [
                pltpu.VMEM((row_span, frames, BLOCK), F32),
                pltpu.VMEM((col_span, frames, BLOCK), BF16),
            ],
        )
        received = swapped(send, "col", 1)
        pair, first = call(
            lambda *refs: pair_kernel(frames, *refs),
            (shape((half_cols + frames, BLOCK), BF16), (gram_type,) if half else ()),
            (keep, received),
        )
        if half:
            aside_of_chips = call(inverse_kernel, (shape((frames, frames)),), first, cost=aside)
        elif n_rows == 4:
            (remainder,) = call(
                remainder_kernel,
                (shape((stretch * frames + DIAG, BLOCK), BF16),),
                (right_side, prior, pair),
            )
            aside_of_chips = [swapped(remainder, "row", 2)]
        else:
            aside_of_chips = []
        (foot,) = call(
            lambda *refs: chips_kernel(frames, *refs),
            (shape((half_cols + frames, BLOCK), BF16),),
            (others(pair, "col"), aside_of_chips),
        )
        return (foot, swapped(foot, "col", 1)), (*first, *aside_of_chips)

    def backward(foot, last):
        size = stretch * frames
        extra = 0 if last else frames + DIAG
        far, near, kept, keep, norm = call(
            lambda *refs: backward_kernel(stretch, n_cols, last, *refs),
            (
                tuple(shape((size + (0 if p else extra), BLOCK), BF16) for p in range(pairs)),
                shape((size, BLOCK), BF16),
                (shape((size, BLOCK)),) * pairs,
                shape((size, BLOCK)),
                (shape((frames, frames)),) if last else (),
            ),
            (index, *foot, blocks),
            [
                pltpu.VMEM((col_span, frames, BLOCK), F32),
                pltpu.VMEM((row_span, frames, BLOCK), BF16),
                pltpu.VMEM((frames, 2 * frames), F32),
            ],
        )
        received = tuple(swapped(x, "row", 1) for x in far)
        near = swapped(near, "row", 1)
        sums, gram = call(
            lambda *refs: rows_kernel(frames, *refs),
            (
                (shape((size + extra, BLOCK), BF16),) * pairs,
                ()
                if last
                else (shape((frames // 2, 2 * frames)), shape((DIAG, 2 * frames), BF16)),
            ),
            (far[0], received, kept),
        )
        far = tuple(swapped(x, "row", 2 * (p + 1)) for p, x in enumerate(sums))
        if last:
            return (keep, near, far), norm
        return (keep, near, far, *gram), sums

    (cast,) = call(cast_kernel, (cast_type,), (right_side,))
    search = gather(cast, "row")
    index, turned = call(
        lambda *refs: turn_kernel(row_span, stretch, *refs),
        (shape((2, stored), jnp.int32), shape(blocks.shape, BF16)),
        (block_row, block_col, blocks),
        cost=aside,
    )
    (gram,) = call(gram_kernel, (gram_type,), (right_side, prior), cost=aside)
    foot, remainder = forward(search, gram, ())
    (keep, near, far, gram, tile), sums = backward(foot, False)
    pair_sum, pair_cast = call(
        near_kernel, (shape((stretch * frames, BLOCK)), cast_type), (keep, near)
    )
    image, following, cast, half, diagonal = call(
        image_kernel,
        (own, own, cast_type, shape((frames // 2, 2 * frames)), shape((DIAG, 2 * frames))),
        (pair_sum, far, gram, tile, right_side, prior),
    )
    if n_rows == 4:
        (cross,) = call(
            lambda *refs: cross_kernel(frames, *refs),
            (cast_type,),
            (
                sums[0],
                swapped(pair_cast, "row", 2),
                search[2],
                *remainder,
                diagonal,
            ),
        )
        search = (cast, swapped(cast, "row", 1), cross, swapped(cross, "row", 1))
    else:
        search = gather(cast, "row")
    (gram,) = call(gram_kernel, (gram_type,), (following, prior), cost=aside)
    foot, (first, inverse) = forward(search, gram, (half,))
    (second,) = call(
        lambda *refs: second_gram_kernel(half_cols, *refs),
        (shape((frames, 2 * frames), BF16),),
        foot,
        [pltpu.VMEM((frames, 2 * frames), F32)],
    )
    gram, second = call(
        second_pair_kernel,
        (shape((frames, frames)), shape((frames, 2 * frames), BF16)),
        (second, swapped(second, "row", 1)),
        cost=aside,
    )
    second = others(second, "row")[1:]
    parts, (norm,) = backward(foot, True)
    (coeffs,) = call(
        solve_kernel,
        (shape((2 * frames, frames)),),
        (gram, second, first, inverse, norm, diagonal),
        cost=aside,
    )
    keep, near, far = parts
    x, base = call(
        early_kernel,
        (own, own),
        (keep, near, right_side, image, following, prior, coeffs),
        cost=hidden,
    )
    (residual,) = call(final_kernel, (own,), (far, base, coeffs))
    return x, residual


def solution(mesh):
    return jax.shard_map(
        shards,
        mesh=mesh,
        in_specs=(
            P("groups", ("row", "col")),
            P(("row", "col")),
            P(("row", "col"), None, None),
            P(("row", "col")),
            P(("row", "col")),
        ),
        out_specs=(P("groups", ("row", "col")), P("groups", ("row", "col"))),
        check_vma=False,
    )
```

```python
import jax
import jax.numpy as jnp
from jax import lax
from jax.experimental import pallas as pl
from jax.experimental.pallas import tpu as pltpu
from jax.sharding import PartitionSpec as P

BLOCK = 128
TILE = 8
AHEAD = 4
DIAG = 16
F32, BF16 = jnp.float32, jnp.bfloat16
FP32 = lax.Precision.HIGHEST
VMEM = pl.BlockSpec(memory_space=pltpu.VMEM)
SMEM = pl.BlockSpec(memory_space=pltpu.SMEM)


def nt_dot(a, b, precision=None):
    return lax.dot_general(
        a, b, (((1,), (1,)), ((), ())), precision=precision, preferred_element_type=F32
    )


def tn_dot(a, b):
    return lax.dot_general(
        a, b, (((0,), (0,)), ((), ())), precision=FP32, preferred_element_type=F32
    )


def nn_dot(a, b):
    return lax.dot_general(
        a, b, (((1,), (0,)), ((), ())), precision=FP32, preferred_element_type=F32
    )


def call(kernel, outs, ins, scratch=(), cost=None):
    flat_ins, ins_tree = jax.tree.flatten(tuple(ins))
    flat_outs, outs_tree = jax.tree.flatten(tuple(outs))

    def body(*refs):
        middle, last = len(flat_ins), len(flat_ins) + len(flat_outs)
        kernel(
            *jax.tree.unflatten(ins_tree, refs[:middle]),
            *jax.tree.unflatten(outs_tree, refs[middle:last]),
            *refs[last:],
        )

    def space(x):
        return SMEM if x.dtype == jnp.int32 else VMEM

    results = pl.pallas_call(
        body,
        out_shape=flat_outs,
        in_specs=[space(x) for x in flat_ins],
        out_specs=[space(x) for x in flat_outs],
        scratch_shapes=list(scratch),
        compiler_params=pltpu.CompilerParams(vmem_limit_bytes=48 * 1024 * 1024),
        cost_estimate=cost,
    )(*flat_ins)
    return jax.tree.unflatten(outs_tree, results)


def lanes(j):
    return slice(j * BLOCK, (j + 1) * BLOCK)


def rows(j, count):
    return slice(j * count, (j + 1) * count)


def split(value):
    high = value.astype(BF16)
    return high, (value - high.astype(F32)).astype(BF16)


def sum_rows(refs, at):
    total = refs[0][at, :].astype(F32)
    for ref in refs[1:]:
        total += ref[at, :].astype(F32)
    return total


def eye(n):
    return lax.broadcasted_iota(jnp.int32, (n, n), 0) == lax.broadcasted_iota(jnp.int32, (n, n), 1)


def cast_kernel(v_ref, out_ref):
    frames = v_ref.shape[0]
    for j in range(v_ref.shape[1] // BLOCK):
        out_ref[rows(j, frames), :] = v_ref[:, lanes(j)].astype(BF16)


def turn_kernel(row_span, stretch, brow, bcol, blocks, index_ref, out_ref):
    for k in range(blocks.shape[0]):
        index_ref[0, k] = lax.rem(brow[k], row_span)
        index_ref[1, k] = lax.div(bcol[k], row_span) * stretch + lax.rem(bcol[k], stretch)
        out_ref[k] = blocks[k].T


def gram_kernel(v_ref, prior, out_ref):
    value = v_ref[...]
    out_ref[...] = nt_dot(value, jnp.concatenate([value, value * prior[...]], axis=0), FP32)


def fill(panel, ref, at, stretch):
    frames = panel.shape[1]
    for j in range(stretch):
        panel[at * stretch + j] = ref[rows(j, frames), :]


def whole_of(panel):
    return jnp.concatenate([panel[b] for b in range(panel.shape[0])], axis=1)


def forward_kernel(stretch, cols, index, search, blocks, gram, half, keep_ref, send_ref, acc, panel):
    frames = panel.shape[1]
    me = lax.axis_index("row")
    for flip, ref in enumerate(search):
        fill(panel, ref, lax.bitwise_xor(me, flip), stretch)
    acc[...] = jnp.zeros_like(acc)
    for k in range(blocks.shape[0]):
        acc[index[0, k]] += jnp.dot(panel[index[1, k]], blocks[k], preferred_element_type=F32)
    core = lax.rem(lax.axis_index("col"), 2)
    for x in range(cols // 2):
        for j in range(stretch):
            at = rows(x * stretch + j, frames)
            keep_ref[at, :] = acc[(2 * x + core) * stretch + j]
            send_ref[at, :] = acc[(2 * x + 1 - core) * stretch + j]
    at = rows(cols // 2 * stretch, frames)
    value = gram[...]
    if half:
        whole = whole_of(panel)
        inner = nt_dot(whole, jnp.concatenate([whole, jnp.zeros_like(whole)], axis=0))
        lane = lax.broadcasted_iota(jnp.int32, value.shape, 1)
        value = jnp.where(lane < frames, inner, value)
        send_ref[at.stop :, :] = half[0][...]
        keep_ref[at.stop :, :] = half[0][...]
    keep_ref[at, :] = value
    send_ref[at, :] = value


def pair_kernel(frames, keep, received, out_ref, first_refs):
    core = lax.rem(lax.axis_index("col"), 2)
    split_at = frames // 2
    data = out_ref.shape[0] - frames
    for j in range(data // frames):
        at = rows(j, frames)
        out_ref[at, :] = (keep[at, :] + received[at, :]).astype(BF16)
    at = pl.ds(pl.multiple_of(data + core * split_at, split_at), split_at)
    out_ref[data : data + split_at, :], out_ref[data + split_at :, :] = split(
        keep[at, :] + received[at, :]
    )
    if first_refs:
        at = pl.ds(pl.multiple_of(core * split_at, split_at), split_at)
        first_refs[0][at, :] = keep[data + frames :, :]
        at = pl.ds(pl.multiple_of((1 - core) * split_at, split_at), split_at)
        first_refs[0][at, :] = received[data + frames :, :]


def chips_kernel(frames, parts, before, out_ref):
    split_at = frames // 2
    data = out_ref.shape[0] - frames
    for j in range(data // frames):
        at = rows(j, frames)
        out_ref[at, :] = sum_rows(parts, at).astype(BF16)
    high, low = slice(data, data + split_at), slice(data + split_at, data + frames)
    out_ref[high, :], out_ref[low, :] = split(sum_rows(parts, high) + sum_rows(parts, low))


def backward_kernel(
    stretch, cols, last, index, own, received, blocks,
    far_refs, near_ref, keep_refs, keep_ref, norm_refs, acc, panel, gram,
):
    frames = panel.shape[1]
    split_at = frames // 2
    core = lax.rem(lax.axis_index("col"), 2)
    data = cols // 2 * stretch * frames
    for ref, side in ((own, core), (received, 1 - core)):
        for x in range(cols // 2):
            for j in range(stretch):
                panel[(2 * x + side) * stretch + j] = ref[rows(x * stretch + j, frames), :]
    fill_gram(gram, own, received, data, frames)
    acc[...] = jnp.zeros_like(acc)
    for k in range(blocks.shape[0]):
        acc[index[1, k]] += jnp.dot(panel[index[0, k]], blocks[k], preferred_element_type=F32)
    me = lax.axis_index("row")
    for far, (far_ref, kept_ref) in enumerate(zip(far_refs, keep_refs)):
        shard = lax.bitwise_xor(me, 2 * (far + 1))
        other = lax.bitwise_xor(shard, 1)
        for j in range(stretch):
            kept_ref[rows(j, frames), :] = acc[shard * stretch + j]
            far_ref[rows(j, frames), :] = acc[other * stretch + j].astype(BF16)
    other = lax.bitwise_xor(me, 1)
    for j in range(stretch):
        keep_ref[rows(j, frames), :] = acc[me * stretch + j]
        near_ref[rows(j, frames), :] = acc[other * stretch + j].astype(BF16)
    if last:
        norm_refs[0][...] = gram[:, :frames]
        return
    whole = whole_of(panel)
    total = gram[...] + nt_dot(whole, jnp.concatenate([jnp.zeros_like(whole), whole], axis=0))
    at = stretch * frames
    out_ref = far_refs[0]
    gram[...] = total
    out_ref[at : at + split_at, :], out_ref[at + split_at : at + frames, :] = split(
        gram[pl.ds(pl.multiple_of(core * split_at, split_at), split_at), :]
    )
    lane = lax.broadcasted_iota(jnp.int32, total.shape, 1)
    row = lax.broadcasted_iota(jnp.int32, total.shape, 0)
    on_diagonal = jnp.logical_or(lane == row, lane == row + frames)
    diagonal = jnp.sum(jnp.where(on_diagonal, total, 0.0), axis=0, keepdims=True)
    row = lax.broadcasted_iota(jnp.int32, (DIAG, 2 * frames), 0)
    out_ref[at + frames :, :] = jnp.where(row == 0, diagonal, 0.0).astype(BF16)


def rows_kernel(frames, sent, received, kept, out_refs, extra_refs):
    split_at = frames // 2
    data = kept[0].shape[0]
    for out_ref, kept_ref, received_ref in zip(out_refs, kept, received):
        for j in range(data // frames):
            at = rows(j, frames)
            out_ref[at, :] = (kept_ref[at, :] + received_ref[at, :].astype(F32)).astype(BF16)
    if extra_refs:
        pair = (sent, received[0])
        high, low = slice(data, data + split_at), slice(data + split_at, data + frames)
        value = sum_rows(pair, high) + sum_rows(pair, low)
        block = jnp.concatenate(split(value), axis=0)
        tile = sum_rows(pair, slice(data + frames, data + frames + DIAG)).astype(BF16)
        extra_refs[0][...] = value
        extra_refs[1][...] = tile
        for out_ref in out_refs:
            out_ref[data : data + frames, :] = block
            out_ref[data + frames :, :] = tile


def fill_gram(gram, own, received, data, frames):
    split_at = frames // 2
    core = lax.rem(lax.axis_index("col"), 2)
    for ref, side in ((own, core), (received, 1 - core)):
        at = pl.ds(pl.multiple_of(side * split_at, split_at), split_at)
        gram[at, :] = ref[data : data + split_at, :].astype(F32) + ref[data + split_at :, :].astype(
            F32
        )


def second_gram_kernel(data, own, received, out_ref, gram):
    frames = out_ref.shape[0]
    fill_gram(gram, own, received, data, frames)
    whole = jnp.concatenate(
        [ref[rows(j, frames), :] for ref in (own, received) for j in range(data // frames)], axis=1
    )
    value = gram[:, frames:] + nt_dot(whole, whole)
    out_ref[...] = jnp.concatenate(split(value), axis=1)


def second_pair_kernel(own, received, gram_ref, out_ref):
    n = own.shape[0]
    both = own[...].astype(F32) + received[...].astype(F32)
    value = both[:, :n] + both[:, n:]
    gram_ref[...] = value
    out_ref[...] = jnp.concatenate(split(value), axis=1)


def near_kernel(keep, near, sum_ref, cast_ref):
    total = keep[...] + near[...].astype(F32)
    sum_ref[...] = total
    cast_ref[...] = total.astype(BF16)


def own_sum(keep, parts, j, frames):
    at = rows(j, frames)
    return keep[at, :] + sum_rows(parts, at)


def frame_shift(diagonal, frames):
    row = 1.25 * diagonal[:, frames:] / diagonal[:, :frames]
    return jnp.sum(jnp.where(eye(frames), row, 0.0), axis=1, keepdims=True), row


def image_kernel(
    pair_sum, far, gram, tile, v_ref, prior, image_ref, next_ref, cast_ref, half_ref, diag_ref
):
    frames = v_ref.shape[0]
    split_at = frames // 2
    data = cast_ref.shape[0]
    diagonal = tile[...].astype(F32) + sum_rows(far, slice(data + frames, data + frames + DIAG))
    diag_ref[...] = diagonal
    shift, _ = frame_shift(diagonal[0:1, :], frames)
    for j in range(data // frames):
        value = v_ref[:, lanes(j)]
        image = own_sum(pair_sum, far, j, frames) + prior[:, lanes(j)] * value
        following = image - shift * value
        image_ref[:, lanes(j)] = image
        next_ref[:, lanes(j)] = following
        cast_ref[rows(j, frames), :] = following.astype(BF16)
    half_ref[...] = (
        gram[...]
        + sum_rows(far, slice(data, data + split_at))
        + sum_rows(far, slice(data + split_at, data + frames))
    )


def remainder_kernel(v_ref, prior, before, out_ref):
    frames = v_ref.shape[0]
    stretch = v_ref.shape[1] // BLOCK
    for j in range(stretch):
        out_ref[rows(j, frames), :] = split(v_ref[:, lanes(j)])[1]
    terms = [part.astype(F32) for part in split(prior[...])]
    lines = [part[:, lanes(j)] for part in terms for j in range(stretch)]
    lines.append(jnp.zeros((DIAG - len(lines), BLOCK), F32))
    out_ref[stretch * frames :, :] = jnp.concatenate(lines, axis=0).astype(BF16)


def cross_kernel(frames, own, received, high, low, diag_ref, cast_ref):
    stretch = cast_ref.shape[0] // frames
    shift, _ = frame_shift(diag_ref[0:1, :], frames)
    tile = low[stretch * frames :, :].astype(F32)
    for j in range(stretch):
        at = rows(j, frames)
        weight = tile[j : j + 1, :] + tile[stretch + j : stretch + j + 1, :]
        value = sum_rows((high, low), at)
        cast_ref[at, :] = (sum_rows((own, received), at) + (weight - shift) * value).astype(BF16)


def eliminate(matrix, right, n):
    width = matrix.shape[1] + right.shape[1]
    work = jnp.concatenate([matrix, right], axis=1)
    work = [work[rows(i, TILE), :] for i in range(n // TILE)]
    at = lax.broadcasted_iota(jnp.int32, (TILE, width), 0)

    def column(k):
        return [jnp.broadcast_to(t[:, k : k + 1], (TILE, width)) for t in work]

    def step(tiles, spread, k, pivot):
        i, s = divmod(k, TILE)
        row = tiles[i][s : s + 1, :] * pivot
        done = [t - c * row for t, c in zip(tiles, spread)]
        done[i] = jnp.where(at == s, row, done[i])
        return done

    ahead = [column(k) for k in range(AHEAD)]
    for k in range(n):
        i, s = divmod(k, TILE)
        spread = ahead.pop(0)
        pivot = 1.0 / spread[i][s : s + 1, :]
        ahead = [step(later, spread, k, pivot) for later in ahead]
        work = step(work, spread, k, pivot)
        if k + AHEAD < n:
            ahead.append(column(k + AHEAD))
    return jnp.concatenate(work, axis=0)[:, n:]


def inverse_kernel(first, out_ref):
    n = first.shape[0]
    out_ref[...] = eliminate(first[:, n:], jnp.where(eye(n), 1.0, 0.0), n)


def solve_kernel(gram, parts, first, inverse_ref, norm_ref, diag_ref, out_ref):
    n = gram.shape[0]
    norm, energy = first[:, :n], first[:, n:]
    shift, shift_row = frame_shift(diag_ref[0:1, :], n)
    inverse = inverse_ref[...]
    next_rhs = energy - shift * norm
    cross = norm_ref[...] + next_rhs * shift_row
    alpha = nn_dot(inverse, norm)
    conj = nn_dot(inverse, cross.T)
    schur = gram[...] - nn_dot(cross, conj)
    for part in parts:
        both = part[...].astype(F32)
        schur += both[:, :n] + both[:, n:]
    gamma = eliminate(schur, next_rhs - nn_dot(cross, alpha), n)
    out_ref[:n, :] = alpha - nn_dot(conj, gamma)
    out_ref[n:, :] = gamma


def iterate_kernel(v_ref, next_ref, coeffs_ref, x_ref):
    coeffs = coeffs_ref[...]
    for j in range(v_ref.shape[1] // BLOCK):
        both = jnp.concatenate([v_ref[:, lanes(j)], next_ref[:, lanes(j)]], axis=0)
        x_ref[:, lanes(j)] = tn_dot(coeffs, both)


def residual_kernel(keep, near, far, v_ref, image_ref, next_ref, prior, coeffs_ref, r_ref):
    n = v_ref.shape[0]
    coeffs = coeffs_ref[...]
    for j in range(keep.shape[0] // n):
        second_image = own_sum(keep, (near, *far), j, n) + prior[:, lanes(j)] * next_ref[:, lanes(j)]
        r_ref[:, lanes(j)] = v_ref[:, lanes(j)] - tn_dot(
            coeffs, jnp.concatenate([image_ref[:, lanes(j)], second_image], axis=0)
        )


def swapped(x, axis, flip):
    return lax.ppermute(x, axis, [(i, i ^ flip) for i in range(lax.axis_size(axis))])


def others(x, axis):
    return (x, *(swapped(x, axis, flip) for flip in range(2, lax.axis_size(axis), 2)))


def gather(x, axis):
    return tuple(part for own in others(x, axis) for part in (own, swapped(own, axis, 1)))


def shards(right_side, prior, blocks, block_row, block_col):
    frames, pix = right_side.shape
    stretch = pix // BLOCK
    n_rows, n_cols = lax.axis_size("row"), lax.axis_size("col")
    row_span, col_span = stretch * n_cols, stretch * n_rows
    prior = prior.reshape(1, pix)
    stored = blocks.shape[0]
    half_cols = n_cols // 2 * stretch * frames

    def shape(dims, dtype=F32):
        return jax.ShapeDtypeStruct(dims, dtype)

    own = shape((frames, pix))
    gram_type = shape((frames, 2 * frames))
    cast_type = shape((stretch * frames, BLOCK), BF16)
    aside = pl.CostEstimate(flops=2 * 10**9, bytes_accessed=8 * 10**6, transcendentals=0)

    hidden = pl.CostEstimate(flops=1, bytes_accessed=1, transcendentals=0)
    pairs = n_rows // 2 - 1

    def forward(search, gram, half):
        size = half_cols + frames + (frames // 2 if half else 0)
        keep, send = call(
            lambda *refs: forward_kernel(stretch, n_cols, *refs),
            (shape((size, BLOCK)),) * 2,
            (index, search, turned, gram, half),
            [
                pltpu.VMEM((row_span, frames, BLOCK), F32),
                pltpu.VMEM((col_span, frames, BLOCK), BF16),
            ],
        )
        received = swapped(send, "col", 1)
        pair, first = call(
            lambda *refs: pair_kernel(frames, *refs),
            (shape((half_cols + frames, BLOCK), BF16), (gram_type,) if half else ()),
            (keep, received),
        )
        if half:
            aside_of_chips = call(inverse_kernel, (shape((frames, frames)),), first, cost=aside)
        elif n_rows == 4:
            (remainder,) = call(
                remainder_kernel,
                (shape((stretch * frames + DIAG, BLOCK), BF16),),
                (right_side, prior, pair),
            )
            aside_of_chips = [swapped(remainder, "row", 2)]
        else:
            aside_of_chips = []
        (foot,) = call(
            lambda *refs: chips_kernel(frames, *refs),
            (shape((half_cols + frames, BLOCK), BF16),),
            (others(pair, "col"), aside_of_chips),
        )
        return (foot, swapped(foot, "col", 1)), (*first, *aside_of_chips)

    def backward(foot, last):
        size = stretch * frames
        extra = 0 if last else frames + DIAG
        far, near, kept, keep, norm = call(
            lambda *refs: backward_kernel(stretch, n_cols, last, *refs),
            (
                tuple(shape((size + (0 if p else extra), BLOCK), BF16) for p in range(pairs)),
                shape((size, BLOCK), BF16),
                (shape((size, BLOCK)),) * pairs,
                shape((size, BLOCK)),
                (shape((frames, frames)),) if last else (),
            ),
            (index, *foot, blocks),
            [
                pltpu.VMEM((col_span, frames, BLOCK), F32),
                pltpu.VMEM((row_span, frames, BLOCK), BF16),
                pltpu.VMEM((frames, 2 * frames), F32),
            ],
        )
        received = tuple(swapped(x, "row", 1) for x in far)
        near = swapped(near, "row", 1)
        sums, gram = call(
            lambda *refs: rows_kernel(frames, *refs),
            (
                (shape((size + extra, BLOCK), BF16),) * pairs,
                ()
                if last
                else (shape((frames // 2, 2 * frames)), shape((DIAG, 2 * frames), BF16)),
            ),
            (far[0], received, kept),
        )
        far = tuple(swapped(x, "row", 2 * (p + 1)) for p, x in enumerate(sums))
        if last:
            return (keep, near, far), norm
        return (keep, near, far, *gram), sums

    (cast,) = call(cast_kernel, (cast_type,), (right_side,))
    search = gather(cast, "row")
    index, turned = call(
        lambda *refs: turn_kernel(row_span, stretch, *refs),
        (shape((2, stored), jnp.int32), shape(blocks.shape, BF16)),
        (block_row, block_col, blocks),
        cost=aside,
    )
    (gram,) = call(gram_kernel, (gram_type,), (right_side, prior), cost=aside)
    foot, remainder = forward(search, gram, ())
    (keep, near, far, gram, tile), sums = backward(foot, False)
    pair_sum, pair_cast = call(
        near_kernel, (shape((stretch * frames, BLOCK)), cast_type), (keep, near)
    )
    image, following, cast, half, diagonal = call(
        image_kernel,
        (own, own, cast_type, shape((frames // 2, 2 * frames)), shape((DIAG, 2 * frames))),
        (pair_sum, far, gram, tile, right_side, prior),
    )
    if n_rows == 4:
        (cross,) = call(
            lambda *refs: cross_kernel(frames, *refs),
            (cast_type,),
            (
                sums[0],
                swapped(pair_cast, "row", 2),
                search[2],
                *remainder,
                diagonal,
            ),
        )
        search = (cast, swapped(cast, "row", 1), cross, swapped(cross, "row", 1))
    else:
        search = gather(cast, "row")
    (gram,) = call(gram_kernel, (gram_type,), (following, prior), cost=aside)
    foot, (first, inverse) = forward(search, gram, (half,))
    (second,) = call(
        lambda *refs: second_gram_kernel(half_cols, *refs),
        (shape((frames, 2 * frames), BF16),),
        foot,
        [pltpu.VMEM((frames, 2 * frames), F32)],
    )
    gram, second = call(
        second_pair_kernel,
        (shape((frames, frames)), shape((frames, 2 * frames), BF16)),
        (second, swapped(second, "row", 1)),
        cost=aside,
    )
    second = others(second, "row")[1:]
    parts, (norm,) = backward(foot, True)
    (coeffs,) = call(
        solve_kernel,
        (shape((2 * frames, frames)),),
        (gram, second, first, inverse, norm, diagonal),
        cost=aside,
    )
    (iterate,) = call(iterate_kernel, (own,), (right_side, following, coeffs), cost=hidden)
    (residual,) = call(
        residual_kernel, (own,), (*parts, right_side, image, following, prior, coeffs)
    )
    return iterate, residual


def solution(mesh):
    return jax.shard_map(
        shards,
        mesh=mesh,
        in_specs=(
            P("groups", ("row", "col")),
            P(("row", "col")),
            P(("row", "col"), None, None),
            P(("row", "col")),
            P(("row", "col")),
        ),
        out_specs=(P("groups", ("row", "col")), P("groups", ("row", "col"))),
        check_vma=False,
    )
```

```python
import jax
import jax.numpy as jnp
from jax import lax
from jax.experimental import pallas as pl
from jax.experimental.pallas import tpu as pltpu
from jax.sharding import PartitionSpec as P

BLOCK = 128
TILE = 8
AHEAD = 4
DIAG = 16
F32, BF16 = jnp.float32, jnp.bfloat16
FP32 = lax.Precision.HIGHEST
VMEM = pl.BlockSpec(memory_space=pltpu.VMEM)
SMEM = pl.BlockSpec(memory_space=pltpu.SMEM)


def nt_dot(a, b, precision=None):
    return lax.dot_general(
        a, b, (((1,), (1,)), ((), ())), precision=precision, preferred_element_type=F32
    )


def tn_dot(a, b):
    return lax.dot_general(
        a, b, (((0,), (0,)), ((), ())), precision=FP32, preferred_element_type=F32
    )


def nn_dot(a, b):
    return lax.dot_general(
        a, b, (((1,), (0,)), ((), ())), precision=FP32, preferred_element_type=F32
    )


def call(kernel, outs, ins, scratch=(), cost=None):
    flat_ins, ins_tree = jax.tree.flatten(tuple(ins))
    flat_outs, outs_tree = jax.tree.flatten(tuple(outs))

    def body(*refs):
        middle, last = len(flat_ins), len(flat_ins) + len(flat_outs)
        kernel(
            *jax.tree.unflatten(ins_tree, refs[:middle]),
            *jax.tree.unflatten(outs_tree, refs[middle:last]),
            *refs[last:],
        )

    def space(x):
        return SMEM if x.dtype == jnp.int32 else VMEM

    results = pl.pallas_call(
        body,
        out_shape=flat_outs,
        in_specs=[space(x) for x in flat_ins],
        out_specs=[space(x) for x in flat_outs],
        scratch_shapes=list(scratch),
        compiler_params=pltpu.CompilerParams(vmem_limit_bytes=48 * 1024 * 1024),
        cost_estimate=cost,
    )(*flat_ins)
    return jax.tree.unflatten(outs_tree, results)


def lanes(j):
    return slice(j * BLOCK, (j + 1) * BLOCK)


def rows(j, count):
    return slice(j * count, (j + 1) * count)


def split(value):
    high = value.astype(BF16)
    return high, (value - high.astype(F32)).astype(BF16)


def sum_rows(refs, at):
    total = refs[0][at, :].astype(F32)
    for ref in refs[1:]:
        total += ref[at, :].astype(F32)
    return total


def eye(n):
    return lax.broadcasted_iota(jnp.int32, (n, n), 0) == lax.broadcasted_iota(jnp.int32, (n, n), 1)


def cast_kernel(v_ref, out_ref):
    frames = v_ref.shape[0]
    for j in range(v_ref.shape[1] // BLOCK):
        out_ref[rows(j, frames), :] = v_ref[:, lanes(j)].astype(BF16)


def turn_kernel(row_span, stretch, brow, bcol, blocks, index_ref, out_ref):
    for k in range(blocks.shape[0]):
        index_ref[0, k] = lax.rem(brow[k], row_span)
        index_ref[1, k] = lax.div(bcol[k], row_span) * stretch + lax.rem(bcol[k], stretch)
        out_ref[k] = blocks[k].T


def gram_kernel(v_ref, prior, out_ref):
    value = v_ref[...]
    out_ref[...] = nt_dot(value, jnp.concatenate([value, value * prior[...]], axis=0), FP32)


def fill(panel, ref, at, stretch):
    frames = panel.shape[1]
    for j in range(stretch):
        panel[at * stretch + j] = ref[rows(j, frames), :]


def whole_of(panel):
    return jnp.concatenate([panel[b] for b in range(panel.shape[0])], axis=1)


def forward_kernel(stretch, cols, index, search, blocks, gram, half, keep_ref, send_ref, acc, panel):
    frames = panel.shape[1]
    me = lax.axis_index("row")
    for flip, ref in enumerate(search):
        fill(panel, ref, lax.bitwise_xor(me, flip), stretch)
    acc[...] = jnp.zeros_like(acc)
    for k in range(blocks.shape[0]):
        acc[index[0, k]] += jnp.dot(panel[index[1, k]], blocks[k], preferred_element_type=F32)
    core = lax.rem(lax.axis_index("col"), 2)
    for x in range(cols // 2):
        for j in range(stretch):
            at = rows(x * stretch + j, frames)
            keep_ref[at, :] = acc[(2 * x + core) * stretch + j]
            send_ref[at, :] = acc[(2 * x + 1 - core) * stretch + j]
    at = rows(cols // 2 * stretch, frames)
    value = gram[...]
    if half:
        whole = whole_of(panel)
        inner = nt_dot(whole, jnp.concatenate([whole, jnp.zeros_like(whole)], axis=0))
        lane = lax.broadcasted_iota(jnp.int32, value.shape, 1)
        value = jnp.where(lane < frames, inner, value)
        send_ref[at.stop :, :] = half[0][...]
        keep_ref[at.stop :, :] = half[0][...]
    keep_ref[at, :] = value
    send_ref[at, :] = value


def pair_kernel(frames, keep, received, out_ref, first_refs):
    core = lax.rem(lax.axis_index("col"), 2)
    split_at = frames // 2
    data = out_ref.shape[0] - frames
    for j in range(data // frames):
        at = rows(j, frames)
        out_ref[at, :] = (keep[at, :] + received[at, :]).astype(BF16)
    at = pl.ds(pl.multiple_of(data + core * split_at, split_at), split_at)
    out_ref[data : data + split_at, :], out_ref[data + split_at :, :] = split(
        keep[at, :] + received[at, :]
    )
    if first_refs:
        at = pl.ds(pl.multiple_of(core * split_at, split_at), split_at)
        first_refs[0][at, :] = keep[data + frames :, :]
        at = pl.ds(pl.multiple_of((1 - core) * split_at, split_at), split_at)
        first_refs[0][at, :] = received[data + frames :, :]


def chips_kernel(frames, parts, before, out_ref):
    split_at = frames // 2
    data = out_ref.shape[0] - frames
    for j in range(data // frames):
        at = rows(j, frames)
        out_ref[at, :] = sum_rows(parts, at).astype(BF16)
    high, low = slice(data, data + split_at), slice(data + split_at, data + frames)
    out_ref[high, :], out_ref[low, :] = split(sum_rows(parts, high) + sum_rows(parts, low))


def backward_kernel(
    stretch, cols, last, index, own, received, blocks,
    far_refs, near_ref, keep_refs, keep_ref, norm_refs, acc, panel, gram,
):
    frames = panel.shape[1]
    split_at = frames // 2
    core = lax.rem(lax.axis_index("col"), 2)
    data = cols // 2 * stretch * frames
    for ref, side in ((own, core), (received, 1 - core)):
        for x in range(cols // 2):
            for j in range(stretch):
                panel[(2 * x + side) * stretch + j] = ref[rows(x * stretch + j, frames), :]
    fill_gram(gram, own, received, data, frames)
    acc[...] = jnp.zeros_like(acc)
    for k in range(blocks.shape[0]):
        acc[index[1, k]] += jnp.dot(panel[index[0, k]], blocks[k], preferred_element_type=F32)
    me = lax.axis_index("row")
    for far, (far_ref, kept_ref) in enumerate(zip(far_refs, keep_refs)):
        shard = lax.bitwise_xor(me, 2 * (far + 1))
        other = lax.bitwise_xor(shard, 1)
        for j in range(stretch):
            kept_ref[rows(j, frames), :] = acc[shard * stretch + j]
            far_ref[rows(j, frames), :] = acc[other * stretch + j].astype(BF16)
    other = lax.bitwise_xor(me, 1)
    for j in range(stretch):
        keep_ref[rows(j, frames), :] = acc[me * stretch + j]
        near_ref[rows(j, frames), :] = acc[other * stretch + j].astype(BF16)
    if last:
        norm_refs[0][...] = gram[:, :frames]
        return
    whole = whole_of(panel)
    total = gram[...] + nt_dot(whole, jnp.concatenate([jnp.zeros_like(whole), whole], axis=0))
    at = stretch * frames
    out_ref = far_refs[0]
    gram[...] = total
    out_ref[at : at + split_at, :], out_ref[at + split_at : at + frames, :] = split(
        gram[pl.ds(pl.multiple_of(core * split_at, split_at), split_at), :]
    )
    lane = lax.broadcasted_iota(jnp.int32, total.shape, 1)
    row = lax.broadcasted_iota(jnp.int32, total.shape, 0)
    on_diagonal = jnp.logical_or(lane == row, lane == row + frames)
    diagonal = jnp.sum(jnp.where(on_diagonal, total, 0.0), axis=0, keepdims=True)
    row = lax.broadcasted_iota(jnp.int32, (DIAG, 2 * frames), 0)
    out_ref[at + frames :, :] = jnp.where(row == 0, diagonal, 0.0).astype(BF16)


def rows_kernel(frames, sent, received, kept, out_refs, extra_refs):
    split_at = frames // 2
    data = kept[0].shape[0]
    for out_ref, kept_ref, received_ref in zip(out_refs, kept, received):
        for j in range(data // frames):
            at = rows(j, frames)
            out_ref[at, :] = (kept_ref[at, :] + received_ref[at, :].astype(F32)).astype(BF16)
    if extra_refs:
        pair = (sent, received[0])
        high, low = slice(data, data + split_at), slice(data + split_at, data + frames)
        value = sum_rows(pair, high) + sum_rows(pair, low)
        block = jnp.concatenate(split(value), axis=0)
        tile = sum_rows(pair, slice(data + frames, data + frames + DIAG)).astype(BF16)
        extra_refs[0][...] = value
        extra_refs[1][...] = tile
        for out_ref in out_refs:
            out_ref[data : data + frames, :] = block
            out_ref[data + frames :, :] = tile


def fill_gram(gram, own, received, data, frames):
    split_at = frames // 2
    core = lax.rem(lax.axis_index("col"), 2)
    for ref, side in ((own, core), (received, 1 - core)):
        at = pl.ds(pl.multiple_of(side * split_at, split_at), split_at)
        gram[at, :] = ref[data : data + split_at, :].astype(F32) + ref[data + split_at :, :].astype(
            F32
        )


def second_gram_kernel(data, own, received, out_ref, gram):
    frames = out_ref.shape[0]
    fill_gram(gram, own, received, data, frames)
    whole = jnp.concatenate(
        [ref[rows(j, frames), :] for ref in (own, received) for j in range(data // frames)], axis=1
    )
    value = gram[:, frames:] + nt_dot(whole, whole)
    out_ref[...] = jnp.concatenate(split(value), axis=1)


def second_pair_kernel(own, received, gram_ref, out_ref):
    n = own.shape[0]
    both = own[...].astype(F32) + received[...].astype(F32)
    value = both[:, :n] + both[:, n:]
    gram_ref[...] = value
    out_ref[...] = jnp.concatenate(split(value), axis=1)


def near_kernel(keep, near, sum_ref, cast_ref):
    total = keep[...] + near[...].astype(F32)
    sum_ref[...] = total
    cast_ref[...] = total.astype(BF16)


def own_sum(keep, parts, j, frames):
    at = rows(j, frames)
    return keep[at, :] + sum_rows(parts, at)


def frame_shift(diagonal, frames):
    row = 1.25 * diagonal[:, frames:] / diagonal[:, :frames]
    return jnp.sum(jnp.where(eye(frames), row, 0.0), axis=1, keepdims=True), row


def image_kernel(
    pair_sum, far, gram, tile, v_ref, prior, image_ref, next_ref, cast_ref, half_ref, diag_ref
):
    frames = v_ref.shape[0]
    split_at = frames // 2
    data = cast_ref.shape[0]
    diagonal = tile[...].astype(F32) + sum_rows(far, slice(data + frames, data + frames + DIAG))
    diag_ref[...] = diagonal
    shift, _ = frame_shift(diagonal[0:1, :], frames)
    for j in range(data // frames):
        value = v_ref[:, lanes(j)]
        image = own_sum(pair_sum, far, j, frames) + prior[:, lanes(j)] * value
        following = image - shift * value
        image_ref[:, lanes(j)] = image
        next_ref[:, lanes(j)] = following
        cast_ref[rows(j, frames), :] = following.astype(BF16)
    half_ref[...] = (
        gram[...]
        + sum_rows(far, slice(data, data + split_at))
        + sum_rows(far, slice(data + split_at, data + frames))
    )


def remainder_kernel(v_ref, prior, before, out_ref):
    frames = v_ref.shape[0]
    stretch = v_ref.shape[1] // BLOCK
    for j in range(stretch):
        out_ref[rows(j, frames), :] = split(v_ref[:, lanes(j)])[1]
    terms = [part.astype(F32) for part in split(prior[...])]
    lines = [part[:, lanes(j)] for part in terms for j in range(stretch)]
    lines.append(jnp.zeros((DIAG - len(lines), BLOCK), F32))
    out_ref[stretch * frames :, :] = jnp.concatenate(lines, axis=0).astype(BF16)


def cross_kernel(frames, own, received, high, low, diag_ref, cast_ref):
    stretch = cast_ref.shape[0] // frames
    shift, _ = frame_shift(diag_ref[0:1, :], frames)
    tile = low[stretch * frames :, :].astype(F32)
    for j in range(stretch):
        at = rows(j, frames)
        weight = tile[j : j + 1, :] + tile[stretch + j : stretch + j + 1, :]
        value = sum_rows((high, low), at)
        cast_ref[at, :] = (sum_rows((own, received), at) + (weight - shift) * value).astype(BF16)


def eliminate(matrix, right, n):
    width = matrix.shape[1] + right.shape[1]
    work = jnp.concatenate([matrix, right], axis=1)
    work = [work[rows(i, TILE), :] for i in range(n // TILE)]
    at = lax.broadcasted_iota(jnp.int32, (TILE, width), 0)

    def column(k):
        return [jnp.broadcast_to(t[:, k : k + 1], (TILE, width)) for t in work]

    def step(tiles, spread, k, pivot):
        i, s = divmod(k, TILE)
        row = tiles[i][s : s + 1, :] * pivot
        done = [t - c * row for t, c in zip(tiles, spread)]
        done[i] = jnp.where(at == s, row, done[i])
        return done

    ahead = [column(k) for k in range(AHEAD)]
    for k in range(n):
        i, s = divmod(k, TILE)
        spread = ahead.pop(0)
        pivot = 1.0 / spread[i][s : s + 1, :]
        ahead = [step(later, spread, k, pivot) for later in ahead]
        work = step(work, spread, k, pivot)
        if k + AHEAD < n:
            ahead.append(column(k + AHEAD))
    return jnp.concatenate(work, axis=0)[:, n:]


def inverse_kernel(first, out_ref):
    n = first.shape[0]
    out_ref[...] = eliminate(first[:, n:], jnp.where(eye(n), 1.0, 0.0), n)


def solve_kernel(gram, parts, first, inverse_ref, norm_ref, diag_ref, out_ref):
    n = gram.shape[0]
    norm, energy = first[:, :n], first[:, n:]
    shift, shift_row = frame_shift(diag_ref[0:1, :], n)
    inverse = inverse_ref[...]
    next_rhs = energy - shift * norm
    cross = norm_ref[...] + next_rhs * shift_row
    alpha = nn_dot(inverse, norm)
    conj = nn_dot(inverse, cross.T)
    schur = gram[...] - nn_dot(cross, conj)
    for part in parts:
        both = part[...].astype(F32)
        schur += both[:, :n] + both[:, n:]
    gamma = eliminate(schur, next_rhs - nn_dot(cross, alpha), n)
    out_ref[:n, :] = alpha - nn_dot(conj, gamma)
    out_ref[n:, :] = gamma


def final_kernel(keep, near, far, v_ref, image_ref, next_ref, prior, coeffs_ref, x_ref, r_ref):
    n = v_ref.shape[0]
    coeffs = coeffs_ref[...]
    for j in range(keep.shape[0] // n):
        value = v_ref[:, lanes(j)]
        following = next_ref[:, lanes(j)]
        second_image = own_sum(keep, (near, *far), j, n) + prior[:, lanes(j)] * following
        x_ref[:, lanes(j)] = tn_dot(coeffs, jnp.concatenate([value, following], axis=0))
        r_ref[:, lanes(j)] = value - tn_dot(
            coeffs, jnp.concatenate([image_ref[:, lanes(j)], second_image], axis=0)
        )


def swapped(x, axis, flip):
    return lax.ppermute(x, axis, [(i, i ^ flip) for i in range(lax.axis_size(axis))])


def others(x, axis):
    return (x, *(swapped(x, axis, flip) for flip in range(2, lax.axis_size(axis), 2)))


def gather(x, axis):
    return tuple(part for own in others(x, axis) for part in (own, swapped(own, axis, 1)))


def shards(right_side, prior, blocks, block_row, block_col):
    frames, pix = right_side.shape
    stretch = pix // BLOCK
    n_rows, n_cols = lax.axis_size("row"), lax.axis_size("col")
    row_span, col_span = stretch * n_cols, stretch * n_rows
    prior = prior.reshape(1, pix)
    stored = blocks.shape[0]
    half_cols = n_cols // 2 * stretch * frames

    def shape(dims, dtype=F32):
        return jax.ShapeDtypeStruct(dims, dtype)

    own = shape((frames, pix))
    gram_type = shape((frames, 2 * frames))
    cast_type = shape((stretch * frames, BLOCK), BF16)
    aside = pl.CostEstimate(flops=2 * 10**9, bytes_accessed=8 * 10**6, transcendentals=0)

    pairs = n_rows // 2 - 1

    def forward(search, gram, half):
        size = half_cols + frames + (frames // 2 if half else 0)
        keep, send = call(
            lambda *refs: forward_kernel(stretch, n_cols, *refs),
            (shape((size, BLOCK)),) * 2,
            (index, search, turned, gram, half),
            [
                pltpu.VMEM((row_span, frames, BLOCK), F32),
                pltpu.VMEM((col_span, frames, BLOCK), BF16),
            ],
        )
        received = swapped(send, "col", 1)
        pair, first = call(
            lambda *refs: pair_kernel(frames, *refs),
            (shape((half_cols + frames, BLOCK), BF16), (gram_type,) if half else ()),
            (keep, received),
        )
        if half:
            aside_of_chips = call(inverse_kernel, (shape((frames, frames)),), first, cost=aside)
        elif n_rows == 4:
            (remainder,) = call(
                remainder_kernel,
                (shape((stretch * frames + DIAG, BLOCK), BF16),),
                (right_side, prior, pair),
            )
            aside_of_chips = [swapped(remainder, "row", 2)]
        else:
            aside_of_chips = []
        (foot,) = call(
            lambda *refs: chips_kernel(frames, *refs),
            (shape((half_cols + frames, BLOCK), BF16),),
            (others(pair, "col"), aside_of_chips),
        )
        return (foot, swapped(foot, "col", 1)), (*first, *aside_of_chips)

    def backward(foot, last):
        size = stretch * frames
        extra = 0 if last else frames + DIAG
        far, near, kept, keep, norm = call(
            lambda *refs: backward_kernel(stretch, n_cols, last, *refs),
            (
                tuple(shape((size + (0 if p else extra), BLOCK), BF16) for p in range(pairs)),
                shape((size, BLOCK), BF16),
                (shape((size, BLOCK)),) * pairs,
                shape((size, BLOCK)),
                (shape((frames, frames)),) if last else (),
            ),
            (index, *foot, blocks),
            [
                pltpu.VMEM((col_span, frames, BLOCK), F32),
                pltpu.VMEM((row_span, frames, BLOCK), BF16),
                pltpu.VMEM((frames, 2 * frames), F32),
            ],
        )
        received = tuple(swapped(x, "row", 1) for x in far)
        near = swapped(near, "row", 1)
        sums, gram = call(
            lambda *refs: rows_kernel(frames, *refs),
            (
                (shape((size + extra, BLOCK), BF16),) * pairs,
                ()
                if last
                else (shape((frames // 2, 2 * frames)), shape((DIAG, 2 * frames), BF16)),
            ),
            (far[0], received, kept),
        )
        far = tuple(swapped(x, "row", 2 * (p + 1)) for p, x in enumerate(sums))
        if last:
            return (keep, near, far), norm
        return (keep, near, far, *gram), sums

    (cast,) = call(cast_kernel, (cast_type,), (right_side,))
    search = gather(cast, "row")
    index, turned = call(
        lambda *refs: turn_kernel(row_span, stretch, *refs),
        (shape((2, stored), jnp.int32), shape(blocks.shape, BF16)),
        (block_row, block_col, blocks),
        cost=aside,
    )
    (gram,) = call(gram_kernel, (gram_type,), (right_side, prior), cost=aside)
    foot, remainder = forward(search, gram, ())
    (keep, near, far, gram, tile), sums = backward(foot, False)
    pair_sum, pair_cast = call(
        near_kernel, (shape((stretch * frames, BLOCK)), cast_type), (keep, near)
    )
    image, following, cast, half, diagonal = call(
        image_kernel,
        (own, own, cast_type, shape((frames // 2, 2 * frames)), shape((DIAG, 2 * frames))),
        (pair_sum, far, gram, tile, right_side, prior),
    )
    if n_rows == 4:
        (cross,) = call(
            lambda *refs: cross_kernel(frames, *refs),
            (cast_type,),
            (
                sums[0],
                swapped(pair_cast, "row", 2),
                search[2],
                *remainder,
                diagonal,
            ),
        )
        search = (cast, swapped(cast, "row", 1), cross, swapped(cross, "row", 1))
    else:
        search = gather(cast, "row")
    (gram,) = call(gram_kernel, (gram_type,), (following, prior), cost=aside)
    foot, (first, inverse) = forward(search, gram, (half,))
    (second,) = call(
        lambda *refs: second_gram_kernel(half_cols, *refs),
        (shape((frames, 2 * frames), BF16),),
        foot,
        [pltpu.VMEM((frames, 2 * frames), F32)],
    )
    gram, second = call(
        second_pair_kernel,
        (shape((frames, frames)), shape((frames, 2 * frames), BF16)),
        (second, swapped(second, "row", 1)),
        cost=aside,
    )
    second = others(second, "row")[1:]
    parts, (norm,) = backward(foot, True)
    (coeffs,) = call(
        solve_kernel,
        (shape((2 * frames, frames)),),
        (gram, second, first, inverse, norm, diagonal),
        cost=aside,
    )
    return tuple(
        call(
            final_kernel,
            (own, own),
            (*parts, right_side, image, following, prior, coeffs),
        )
    )


def solution(mesh):
    return jax.shard_map(
        shards,
        mesh=mesh,
        in_specs=(
            P("groups", ("row", "col")),
            P(("row", "col")),
            P(("row", "col"), None, None),
            P(("row", "col")),
            P(("row", "col")),
        ),
        out_specs=(P("groups", ("row", "col")), P("groups", ("row", "col"))),
        check_vma=False,
    )
```

```python
import jax
import jax.numpy as jnp
from jax import lax
from jax.experimental import pallas as pl
from jax.experimental.pallas import tpu as pltpu
from jax.sharding import PartitionSpec as P

BLOCK = 128
TILE = 8
AHEAD = 4
DIAG = 16
F32, BF16 = jnp.float32, jnp.bfloat16
FP32 = lax.Precision.HIGHEST
VMEM = pl.BlockSpec(memory_space=pltpu.VMEM)
SMEM = pl.BlockSpec(memory_space=pltpu.SMEM)


def nt_dot(a, b, precision=None):
    return lax.dot_general(
        a, b, (((1,), (1,)), ((), ())), precision=precision, preferred_element_type=F32
    )


def tn_dot(a, b):
    return lax.dot_general(
        a, b, (((0,), (0,)), ((), ())), precision=FP32, preferred_element_type=F32
    )


def nn_dot(a, b):
    return lax.dot_general(
        a, b, (((1,), (0,)), ((), ())), precision=FP32, preferred_element_type=F32
    )


def call(kernel, outs, ins, scratch=(), cost=None):
    flat_ins, ins_tree = jax.tree.flatten(tuple(ins))
    flat_outs, outs_tree = jax.tree.flatten(tuple(outs))

    def body(*refs):
        middle, last = len(flat_ins), len(flat_ins) + len(flat_outs)
        kernel(
            *jax.tree.unflatten(ins_tree, refs[:middle]),
            *jax.tree.unflatten(outs_tree, refs[middle:last]),
            *refs[last:],
        )

    def space(x):
        return SMEM if x.dtype == jnp.int32 else VMEM

    results = pl.pallas_call(
        body,
        out_shape=flat_outs,
        in_specs=[space(x) for x in flat_ins],
        out_specs=[space(x) for x in flat_outs],
        scratch_shapes=list(scratch),
        compiler_params=pltpu.CompilerParams(vmem_limit_bytes=48 * 1024 * 1024),
        cost_estimate=cost,
    )(*flat_ins)
    return jax.tree.unflatten(outs_tree, results)


def lanes(j):
    return slice(j * BLOCK, (j + 1) * BLOCK)


def rows(j, count):
    return slice(j * count, (j + 1) * count)


def split(value):
    high = value.astype(BF16)
    return high, (value - high.astype(F32)).astype(BF16)


def sum_rows(refs, at):
    total = refs[0][at, :].astype(F32)
    for ref in refs[1:]:
        total += ref[at, :].astype(F32)
    return total


def eye(n):
    return lax.broadcasted_iota(jnp.int32, (n, n), 0) == lax.broadcasted_iota(jnp.int32, (n, n), 1)


def cast_kernel(v_ref, out_ref):
    frames = v_ref.shape[0]
    for j in range(v_ref.shape[1] // BLOCK):
        out_ref[rows(j, frames), :] = v_ref[:, lanes(j)].astype(BF16)


def turn_kernel(row_span, stretch, brow, bcol, blocks, index_ref, out_ref):
    for k in range(blocks.shape[0]):
        index_ref[0, k] = lax.rem(brow[k], row_span)
        index_ref[1, k] = lax.div(bcol[k], row_span) * stretch + lax.rem(bcol[k], stretch)
        out_ref[k] = blocks[k].T


def gram_kernel(v_ref, prior, out_ref):
    value = v_ref[...]
    out_ref[...] = nt_dot(value, jnp.concatenate([value, value * prior[...]], axis=0), FP32)


def fill(panel, ref, at, stretch):
    frames = panel.shape[1]
    for j in range(stretch):
        panel[at * stretch + j] = ref[rows(j, frames), :]


def whole_of(panel):
    return jnp.concatenate([panel[b] for b in range(panel.shape[0])], axis=1)


def forward_kernel(stretch, cols, index, search, blocks, gram, half, keep_ref, send_ref, acc, panel):
    frames = panel.shape[1]
    me = lax.axis_index("row")
    for flip, ref in enumerate(search):
        fill(panel, ref, lax.bitwise_xor(me, flip), stretch)
    acc[...] = jnp.zeros_like(acc)
    for k in range(blocks.shape[0]):
        acc[index[0, k]] += jnp.dot(panel[index[1, k]], blocks[k], preferred_element_type=F32)
    core = lax.rem(lax.axis_index("col"), 2)
    for x in range(cols // 2):
        for j in range(stretch):
            at = rows(x * stretch + j, frames)
            keep_ref[at, :] = acc[(2 * x + core) * stretch + j]
            send_ref[at, :] = acc[(2 * x + 1 - core) * stretch + j]
    at = rows(cols // 2 * stretch, frames)
    value = gram[...]
    if half:
        whole = whole_of(panel)
        inner = nt_dot(whole, jnp.concatenate([whole, jnp.zeros_like(whole)], axis=0))
        lane = lax.broadcasted_iota(jnp.int32, value.shape, 1)
        value = jnp.where(lane < frames, inner, value)
        send_ref[at.stop :, :] = half[0][...]
        keep_ref[at.stop :, :] = half[0][...]
    keep_ref[at, :] = value
    send_ref[at, :] = value


def pair_kernel(frames, keep, received, out_ref, first_refs):
    core = lax.rem(lax.axis_index("col"), 2)
    split_at = frames // 2
    data = out_ref.shape[0] - frames
    for j in range(data // frames):
        at = rows(j, frames)
        out_ref[at, :] = (keep[at, :] + received[at, :]).astype(BF16)
    at = pl.ds(pl.multiple_of(data + core * split_at, split_at), split_at)
    out_ref[data : data + split_at, :], out_ref[data + split_at :, :] = split(
        keep[at, :] + received[at, :]
    )
    if first_refs:
        at = pl.ds(pl.multiple_of(core * split_at, split_at), split_at)
        first_refs[0][at, :] = keep[data + frames :, :]
        at = pl.ds(pl.multiple_of((1 - core) * split_at, split_at), split_at)
        first_refs[0][at, :] = received[data + frames :, :]


def chips_kernel(frames, parts, before, out_ref):
    split_at = frames // 2
    data = out_ref.shape[0] - frames
    for j in range(data // frames):
        at = rows(j, frames)
        out_ref[at, :] = sum_rows(parts, at).astype(BF16)
    high, low = slice(data, data + split_at), slice(data + split_at, data + frames)
    out_ref[high, :], out_ref[low, :] = split(sum_rows(parts, high) + sum_rows(parts, low))


def backward_kernel(
    stretch, cols, last, index, own, received, blocks,
    far_refs, near_ref, keep_refs, keep_ref, norm_refs, acc, panel, gram,
):
    frames = panel.shape[1]
    split_at = frames // 2
    core = lax.rem(lax.axis_index("col"), 2)
    data = cols // 2 * stretch * frames
    for ref, side in ((own, core), (received, 1 - core)):
        for x in range(cols // 2):
            for j in range(stretch):
                panel[(2 * x + side) * stretch + j] = ref[rows(x * stretch + j, frames), :]
    fill_gram(gram, own, received, data, frames)
    acc[...] = jnp.zeros_like(acc)
    for k in range(blocks.shape[0]):
        acc[index[1, k]] += jnp.dot(panel[index[0, k]], blocks[k], preferred_element_type=F32)
    me = lax.axis_index("row")
    for far, (far_ref, kept_ref) in enumerate(zip(far_refs, keep_refs)):
        shard = lax.bitwise_xor(me, 2 * (far + 1))
        other = lax.bitwise_xor(shard, 1)
        for j in range(stretch):
            kept_ref[rows(j, frames), :] = acc[shard * stretch + j]
            far_ref[rows(j, frames), :] = acc[other * stretch + j].astype(BF16)
    other = lax.bitwise_xor(me, 1)
    for j in range(stretch):
        keep_ref[rows(j, frames), :] = acc[me * stretch + j]
        near_ref[rows(j, frames), :] = acc[other * stretch + j].astype(BF16)
    if last:
        norm_refs[0][...] = gram[:, :frames]
        return
    whole = whole_of(panel)
    total = gram[...] + nt_dot(whole, jnp.concatenate([jnp.zeros_like(whole), whole], axis=0))
    at = stretch * frames
    out_ref = far_refs[0]
    gram[...] = total
    out_ref[at : at + split_at, :], out_ref[at + split_at : at + frames, :] = split(
        gram[pl.ds(pl.multiple_of(core * split_at, split_at), split_at), :]
    )
    lane = lax.broadcasted_iota(jnp.int32, total.shape, 1)
    row = lax.broadcasted_iota(jnp.int32, total.shape, 0)
    on_diagonal = jnp.logical_or(lane == row, lane == row + frames)
    diagonal = jnp.sum(jnp.where(on_diagonal, total, 0.0), axis=0, keepdims=True)
    row = lax.broadcasted_iota(jnp.int32, (DIAG, 2 * frames), 0)
    out_ref[at + frames :, :] = jnp.where(row == 0, diagonal, 0.0).astype(BF16)


def rows_kernel(frames, sent, received, kept, later, out_refs, extra_refs):
    split_at = frames // 2
    data = kept[0].shape[0]
    for out_ref, kept_ref, received_ref in zip(out_refs, kept, received):
        for j in range(data // frames):
            at = rows(j, frames)
            out_ref[at, :] = (kept_ref[at, :] + received_ref[at, :].astype(F32)).astype(BF16)
    if later:
        extra_refs[0][...] = later[0][...]
    else:
        pair = (sent, received[0])
        high, low = slice(data, data + split_at), slice(data + split_at, data + frames)
        value = sum_rows(pair, high) + sum_rows(pair, low)
        block = jnp.concatenate(split(value), axis=0)
        tile = sum_rows(pair, slice(data + frames, data + frames + DIAG)).astype(BF16)
        extra_refs[0][...] = value
        extra_refs[1][...] = tile
        for out_ref in out_refs:
            out_ref[data : data + frames, :] = block
            out_ref[data + frames :, :] = tile


def fill_gram(gram, own, received, data, frames):
    split_at = frames // 2
    core = lax.rem(lax.axis_index("col"), 2)
    for ref, side in ((own, core), (received, 1 - core)):
        at = pl.ds(pl.multiple_of(side * split_at, split_at), split_at)
        gram[at, :] = ref[data : data + split_at, :].astype(F32) + ref[data + split_at :, :].astype(
            F32
        )


def second_gram_kernel(data, own, received, out_ref, gram):
    frames = out_ref.shape[0]
    fill_gram(gram, own, received, data, frames)
    whole = jnp.concatenate(
        [ref[rows(j, frames), :] for ref in (own, received) for j in range(data // frames)], axis=1
    )
    value = gram[:, frames:] + nt_dot(whole, whole)
    out_ref[...] = jnp.concatenate(split(value), axis=1)


def second_pair_kernel(own, received, gram_ref, out_ref):
    n = own.shape[0]
    both = own[...].astype(F32) + received[...].astype(F32)
    value = both[:, :n] + both[:, n:]
    gram_ref[...] = value
    out_ref[...] = jnp.concatenate(split(value), axis=1)


def near_kernel(keep, near, sum_ref, cast_ref):
    total = keep[...] + near[...].astype(F32)
    sum_ref[...] = total
    cast_ref[...] = total.astype(BF16)


def own_sum(keep, parts, j, frames):
    at = rows(j, frames)
    return keep[at, :] + sum_rows(parts, at)


def frame_shift(diagonal, frames):
    row = 1.25 * diagonal[:, frames:] / diagonal[:, :frames]
    return jnp.sum(jnp.where(eye(frames), row, 0.0), axis=1, keepdims=True), row


def image_kernel(
    pair_sum, far, gram, tile, v_ref, prior, image_ref, next_ref, cast_ref, half_ref, diag_ref
):
    frames = v_ref.shape[0]
    split_at = frames // 2
    data = cast_ref.shape[0]
    diagonal = tile[...].astype(F32) + sum_rows(far, slice(data + frames, data + frames + DIAG))
    diag_ref[...] = diagonal
    shift, _ = frame_shift(diagonal[0:1, :], frames)
    for j in range(data // frames):
        value = v_ref[:, lanes(j)]
        image = own_sum(pair_sum, far, j, frames) + prior[:, lanes(j)] * value
        following = image - shift * value
        image_ref[:, lanes(j)] = image
        next_ref[:, lanes(j)] = following
        cast_ref[rows(j, frames), :] = following.astype(BF16)
    half_ref[...] = (
        gram[...]
        + sum_rows(far, slice(data, data + split_at))
        + sum_rows(far, slice(data + split_at, data + frames))
    )


def remainder_kernel(v_ref, prior, before, out_ref):
    frames = v_ref.shape[0]
    stretch = v_ref.shape[1] // BLOCK
    for j in range(stretch):
        out_ref[rows(j, frames), :] = split(v_ref[:, lanes(j)])[1]
    terms = [part.astype(F32) for part in split(prior[...])]
    lines = [part[:, lanes(j)] for part in terms for j in range(stretch)]
    lines.append(jnp.zeros((DIAG - len(lines), BLOCK), F32))
    out_ref[stretch * frames :, :] = jnp.concatenate(lines, axis=0).astype(BF16)


def cross_kernel(frames, own, received, high, low, diag_ref, cast_ref):
    stretch = cast_ref.shape[0] // frames
    shift, _ = frame_shift(diag_ref[0:1, :], frames)
    tile = low[stretch * frames :, :].astype(F32)
    for j in range(stretch):
        at = rows(j, frames)
        weight = tile[j : j + 1, :] + tile[stretch + j : stretch + j + 1, :]
        value = sum_rows((high, low), at)
        cast_ref[at, :] = (sum_rows((own, received), at) + (weight - shift) * value).astype(BF16)


def eliminate(matrix, right, n):
    width = matrix.shape[1] + right.shape[1]
    work = jnp.concatenate([matrix, right], axis=1)
    work = [work[rows(i, TILE), :] for i in range(n // TILE)]
    at = lax.broadcasted_iota(jnp.int32, (TILE, width), 0)

    def column(k):
        return [jnp.broadcast_to(t[:, k : k + 1], (TILE, width)) for t in work]

    def step(tiles, spread, k, pivot):
        i, s = divmod(k, TILE)
        row = tiles[i][s : s + 1, :] * pivot
        done = [t - c * row for t, c in zip(tiles, spread)]
        done[i] = jnp.where(at == s, row, done[i])
        return done

    ahead = [column(k) for k in range(AHEAD)]
    for k in range(n):
        i, s = divmod(k, TILE)
        spread = ahead.pop(0)
        pivot = 1.0 / spread[i][s : s + 1, :]
        ahead = [step(later, spread, k, pivot) for later in ahead]
        work = step(work, spread, k, pivot)
        if k + AHEAD < n:
            ahead.append(column(k + AHEAD))
    return jnp.concatenate(work, axis=0)[:, n:]


def inverse_kernel(first, out_ref):
    n = first.shape[0]
    out_ref[...] = eliminate(first[:, n:], jnp.where(eye(n), 1.0, 0.0), n)


def solve_kernel(gram, parts, first, inverse_ref, norm_ref, diag_ref, out_ref):
    n = gram.shape[0]
    norm, energy = first[:, :n], first[:, n:]
    shift, shift_row = frame_shift(diag_ref[0:1, :], n)
    inverse = inverse_ref[...]
    next_rhs = energy - shift * norm
    cross = norm_ref[...] + next_rhs * shift_row
    alpha = nn_dot(inverse, norm)
    conj = nn_dot(inverse, cross.T)
    schur = gram[...] - nn_dot(cross, conj)
    for part in parts:
        both = part[...].astype(F32)
        schur += both[:, :n] + both[:, n:]
    gamma = eliminate(schur, next_rhs - nn_dot(cross, alpha), n)
    out_ref[:n, :] = alpha - nn_dot(conj, gamma)
    out_ref[n:, :] = gamma


def final_kernel(keep, far, near, v_ref, image_ref, next_ref, prior, coeffs_ref, x_ref, r_ref):
    n = v_ref.shape[0]
    coeffs = coeffs_ref[...]
    for j in range(keep.shape[0] // n):
        value = v_ref[:, lanes(j)]
        following = next_ref[:, lanes(j)]
        second_image = own_sum(keep, (near, *far), j, n) + prior[:, lanes(j)] * following
        x_ref[:, lanes(j)] = tn_dot(coeffs, jnp.concatenate([value, following], axis=0))
        r_ref[:, lanes(j)] = value - tn_dot(
            coeffs, jnp.concatenate([image_ref[:, lanes(j)], second_image], axis=0)
        )


def swapped(x, axis, flip):
    return lax.ppermute(x, axis, [(i, i ^ flip) for i in range(lax.axis_size(axis))])


def others(x, axis):
    return (x, *(swapped(x, axis, flip) for flip in range(2, lax.axis_size(axis), 2)))


def gather(x, axis):
    return tuple(part for own in others(x, axis) for part in (own, swapped(own, axis, 1)))


def shards(right_side, prior, blocks, block_row, block_col):
    frames, pix = right_side.shape
    stretch = pix // BLOCK
    n_rows, n_cols = lax.axis_size("row"), lax.axis_size("col")
    row_span, col_span = stretch * n_cols, stretch * n_rows
    prior = prior.reshape(1, pix)
    stored = blocks.shape[0]
    half_cols = n_cols // 2 * stretch * frames

    def shape(dims, dtype=F32):
        return jax.ShapeDtypeStruct(dims, dtype)

    own = shape((frames, pix))
    gram_type = shape((frames, 2 * frames))
    cast_type = shape((stretch * frames, BLOCK), BF16)
    aside = pl.CostEstimate(flops=2 * 10**9, bytes_accessed=8 * 10**6, transcendentals=0)

    pairs = n_rows // 2 - 1

    def forward(search, gram, half):
        size = half_cols + frames + (frames // 2 if half else 0)
        keep, send = call(
            lambda *refs: forward_kernel(stretch, n_cols, *refs),
            (shape((size, BLOCK)),) * 2,
            (index, search, turned, gram, half),
            [
                pltpu.VMEM((row_span, frames, BLOCK), F32),
                pltpu.VMEM((col_span, frames, BLOCK), BF16),
            ],
        )
        received = swapped(send, "col", 1)
        pair, first = call(
            lambda *refs: pair_kernel(frames, *refs),
            (shape((half_cols + frames, BLOCK), BF16), (gram_type,) if half else ()),
            (keep, received),
        )
        if half:
            aside_of_chips = call(inverse_kernel, (shape((frames, frames)),), first, cost=aside)
        elif n_rows == 4:
            (remainder,) = call(
                remainder_kernel,
                (shape((stretch * frames + DIAG, BLOCK), BF16),),
                (right_side, prior, pair),
            )
            aside_of_chips = [swapped(remainder, "row", 2)]
        else:
            aside_of_chips = []
        (foot,) = call(
            lambda *refs: chips_kernel(frames, *refs),
            (shape((half_cols + frames, BLOCK), BF16),),
            (others(pair, "col"), aside_of_chips),
        )
        return (foot, swapped(foot, "col", 1)), (*first, *aside_of_chips)

    def backward(foot, last):
        size = stretch * frames
        extra = 0 if last else frames + DIAG
        far, near, kept, keep, norm = call(
            lambda *refs: backward_kernel(stretch, n_cols, last, *refs),
            (
                tuple(shape((size + (0 if p else extra), BLOCK), BF16) for p in range(pairs)),
                shape((size, BLOCK), BF16),
                (shape((size, BLOCK)),) * pairs,
                shape((size, BLOCK)),
                (shape((frames, frames)),) if last else (),
            ),
            (index, *foot, blocks),
            [
                pltpu.VMEM((col_span, frames, BLOCK), F32),
                pltpu.VMEM((row_span, frames, BLOCK), BF16),
                pltpu.VMEM((frames, 2 * frames), F32),
            ],
        )
        received = tuple(swapped(x, "row", 1) for x in far)
        sums, gram = call(
            lambda *refs: rows_kernel(frames, *refs),
            (
                (shape((size + extra, BLOCK), BF16),) * pairs,
                (cast_type,)
                if last
                else (shape((frames // 2, 2 * frames)), shape((DIAG, 2 * frames), BF16)),
            ),
            (far[0], received, kept, (near,) if last else ()),
        )
        far = tuple(swapped(x, "row", 2 * (p + 1)) for p, x in enumerate(sums))
        near = swapped(gram[0] if last else near, "row", 1)
        if last:
            return (keep, far, near), norm
        return (keep, near, far, *gram), sums

    (cast,) = call(cast_kernel, (cast_type,), (right_side,))
    search = gather(cast, "row")
    index, turned = call(
        lambda *refs: turn_kernel(row_span, stretch, *refs),
        (shape((2, stored), jnp.int32), shape(blocks.shape, BF16)),
        (block_row, block_col, blocks),
        cost=aside,
    )
    (gram,) = call(gram_kernel, (gram_type,), (right_side, prior), cost=aside)
    foot, remainder = forward(search, gram, ())
    (keep, near, far, gram, tile), sums = backward(foot, False)
    pair_sum, pair_cast = call(
        near_kernel, (shape((stretch * frames, BLOCK)), cast_type), (keep, near)
    )
    image, following, cast, half, diagonal = call(
        image_kernel,
        (own, own, cast_type, shape((frames // 2, 2 * frames)), shape((DIAG, 2 * frames))),
        (pair_sum, far, gram, tile, right_side, prior),
    )
    if n_rows == 4:
        (cross,) = call(
            lambda *refs: cross_kernel(frames, *refs),
            (cast_type,),
            (
                sums[0],
                swapped(pair_cast, "row", 2),
                search[2],
                *remainder,
                diagonal,
            ),
        )
        search = (cast, swapped(cast, "row", 1), cross, swapped(cross, "row", 1))
    else:
        search = gather(cast, "row")
    (gram,) = call(gram_kernel, (gram_type,), (following, prior), cost=aside)
    foot, (first, inverse) = forward(search, gram, (half,))
    (second,) = call(
        lambda *refs: second_gram_kernel(half_cols, *refs),
        (shape((frames, 2 * frames), BF16),),
        foot,
        [pltpu.VMEM((frames, 2 * frames), F32)],
    )
    gram, second = call(
        second_pair_kernel,
        (shape((frames, frames)), shape((frames, 2 * frames), BF16)),
        (second, swapped(second, "row", 1)),
        cost=aside,
    )
    second = others(second, "row")[1:]
    parts, (norm,) = backward(foot, True)
    (coeffs,) = call(
        solve_kernel,
        (shape((2 * frames, frames)),),
        (gram, second, first, inverse, norm, diagonal),
        cost=aside,
    )
    return tuple(
        call(
            final_kernel,
            (own, own),
            (*parts, right_side, image, following, prior, coeffs),
        )
    )


def solution(mesh):
    return jax.shard_map(
        shards,
        mesh=mesh,
        in_specs=(
            P("groups", ("row", "col")),
            P(("row", "col")),
            P(("row", "col"), None, None),
            P(("row", "col")),
            P(("row", "col")),
        ),
        out_specs=(P("groups", ("row", "col")), P("groups", ("row", "col"))),
        check_vma=False,
    )
```

```python
import jax
import jax.numpy as jnp
from jax import lax
from jax.experimental import pallas as pl
from jax.experimental.pallas import tpu as pltpu
from jax.sharding import PartitionSpec as P

BLOCK = 128
TILE = 8
AHEAD = 3
DIAG = 16
F32, BF16 = jnp.float32, jnp.bfloat16
FP32 = lax.Precision.HIGHEST
VMEM = pl.BlockSpec(memory_space=pltpu.VMEM)
SMEM = pl.BlockSpec(memory_space=pltpu.SMEM)


def nt_dot(a, b, precision=None):
    return lax.dot_general(
        a, b, (((1,), (1,)), ((), ())), precision=precision, preferred_element_type=F32
    )


def tn_dot(a, b):
    return lax.dot_general(
        a, b, (((0,), (0,)), ((), ())), precision=FP32, preferred_element_type=F32
    )


def nn_dot(a, b):
    return lax.dot_general(
        a, b, (((1,), (0,)), ((), ())), precision=FP32, preferred_element_type=F32
    )


def call(kernel, outs, ins, scratch=(), cost=None):
    flat_ins, ins_tree = jax.tree.flatten(tuple(ins))
    flat_outs, outs_tree = jax.tree.flatten(tuple(outs))

    def body(*refs):
        middle, last = len(flat_ins), len(flat_ins) + len(flat_outs)
        kernel(
            *jax.tree.unflatten(ins_tree, refs[:middle]),
            *jax.tree.unflatten(outs_tree, refs[middle:last]),
            *refs[last:],
        )

    def space(x):
        return SMEM if x.dtype == jnp.int32 else VMEM

    results = pl.pallas_call(
        body,
        out_shape=flat_outs,
        in_specs=[space(x) for x in flat_ins],
        out_specs=[space(x) for x in flat_outs],
        scratch_shapes=list(scratch),
        compiler_params=pltpu.CompilerParams(vmem_limit_bytes=48 * 1024 * 1024),
        cost_estimate=cost,
    )(*flat_ins)
    return jax.tree.unflatten(outs_tree, results)


def lanes(j):
    return slice(j * BLOCK, (j + 1) * BLOCK)


def rows(j, count):
    return slice(j * count, (j + 1) * count)


def split(value):
    high = value.astype(BF16)
    return high, (value - high.astype(F32)).astype(BF16)


def sum_rows(refs, at):
    total = refs[0][at, :].astype(F32)
    for ref in refs[1:]:
        total += ref[at, :].astype(F32)
    return total


def eye(n):
    return lax.broadcasted_iota(jnp.int32, (n, n), 0) == lax.broadcasted_iota(jnp.int32, (n, n), 1)


def cast_kernel(v_ref, out_ref):
    frames = v_ref.shape[0]
    for j in range(v_ref.shape[1] // BLOCK):
        out_ref[rows(j, frames), :] = v_ref[:, lanes(j)].astype(BF16)


def turn_kernel(row_span, stretch, brow, bcol, blocks, index_ref, out_ref):
    for k in range(blocks.shape[0]):
        index_ref[0, k] = lax.rem(brow[k], row_span)
        index_ref[1, k] = lax.div(bcol[k], row_span) * stretch + lax.rem(bcol[k], stretch)
        out_ref[k] = blocks[k].T


def gram_kernel(v_ref, prior, out_ref):
    value = v_ref[...]
    out_ref[...] = nt_dot(value, jnp.concatenate([value, value * prior[...]], axis=0), FP32)


def fill(panel, ref, at, stretch):
    frames = panel.shape[1]
    for j in range(stretch):
        panel[at * stretch + j] = ref[rows(j, frames), :]


def whole_of(panel):
    return jnp.concatenate([panel[b] for b in range(panel.shape[0])], axis=1)


def forward_kernel(stretch, cols, index, search, blocks, gram, half, keep_ref, send_ref, acc, panel):
    frames = panel.shape[1]
    me = lax.axis_index("row")
    for flip, ref in enumerate(search):
        fill(panel, ref, lax.bitwise_xor(me, flip), stretch)
    acc[...] = jnp.zeros_like(acc)
    for k in range(blocks.shape[0]):
        acc[index[0, k]] += jnp.dot(panel[index[1, k]], blocks[k], preferred_element_type=F32)
    core = lax.rem(lax.axis_index("col"), 2)
    for x in range(cols // 2):
        for j in range(stretch):
            at = rows(x * stretch + j, frames)
            keep_ref[at, :] = acc[(2 * x + core) * stretch + j]
            send_ref[at, :] = acc[(2 * x + 1 - core) * stretch + j]
    at = rows(cols // 2 * stretch, frames)
    value = gram[...]
    if half:
        whole = whole_of(panel)
        inner = nt_dot(whole, jnp.concatenate([whole, jnp.zeros_like(whole)], axis=0))
        lane = lax.broadcasted_iota(jnp.int32, value.shape, 1)
        value = jnp.where(lane < frames, inner, value)
        send_ref[at.stop :, :] = half[0][...]
        keep_ref[at.stop :, :] = half[0][...]
    keep_ref[at, :] = value
    send_ref[at, :] = value


def pair_kernel(frames, keep, received, out_ref, first_refs):
    core = lax.rem(lax.axis_index("col"), 2)
    split_at = frames // 2
    data = out_ref.shape[0] - frames
    for j in range(data // frames):
        at = rows(j, frames)
        out_ref[at, :] = (keep[at, :] + received[at, :]).astype(BF16)
    at = pl.ds(pl.multiple_of(data + core * split_at, split_at), split_at)
    out_ref[data : data + split_at, :], out_ref[data + split_at :, :] = split(
        keep[at, :] + received[at, :]
    )
    if first_refs:
        at = pl.ds(pl.multiple_of(core * split_at, split_at), split_at)
        first_refs[0][at, :] = keep[data + frames :, :]
        at = pl.ds(pl.multiple_of((1 - core) * split_at, split_at), split_at)
        first_refs[0][at, :] = received[data + frames :, :]


def chips_kernel(frames, parts, before, out_ref):
    split_at = frames // 2
    data = out_ref.shape[0] - frames
    for j in range(data // frames):
        at = rows(j, frames)
        out_ref[at, :] = sum_rows(parts, at).astype(BF16)
    high, low = slice(data, data + split_at), slice(data + split_at, data + frames)
    out_ref[high, :], out_ref[low, :] = split(sum_rows(parts, high) + sum_rows(parts, low))


def backward_kernel(
    stretch, cols, last, index, own, received, blocks,
    far_refs, near_ref, keep_refs, keep_ref, norm_refs, acc, panel, gram,
):
    frames = panel.shape[1]
    split_at = frames // 2
    core = lax.rem(lax.axis_index("col"), 2)
    data = cols // 2 * stretch * frames
    for ref, side in ((own, core), (received, 1 - core)):
        for x in range(cols // 2):
            for j in range(stretch):
                panel[(2 * x + side) * stretch + j] = ref[rows(x * stretch + j, frames), :]
    fill_gram(gram, own, received, data, frames)
    acc[...] = jnp.zeros_like(acc)
    for k in range(blocks.shape[0]):
        acc[index[1, k]] += jnp.dot(panel[index[0, k]], blocks[k], preferred_element_type=F32)
    me = lax.axis_index("row")
    for far, (far_ref, kept_ref) in enumerate(zip(far_refs, keep_refs)):
        shard = lax.bitwise_xor(me, 2 * (far + 1))
        other = lax.bitwise_xor(shard, 1)
        for j in range(stretch):
            kept_ref[rows(j, frames), :] = acc[shard * stretch + j]
            far_ref[rows(j, frames), :] = acc[other * stretch + j].astype(BF16)
    other = lax.bitwise_xor(me, 1)
    for j in range(stretch):
        keep_ref[rows(j, frames), :] = acc[me * stretch + j]
        near_ref[rows(j, frames), :] = acc[other * stretch + j].astype(BF16)
    if last:
        norm_refs[0][...] = gram[:, :frames]
        return
    whole = whole_of(panel)
    total = gram[...] + nt_dot(whole, jnp.concatenate([jnp.zeros_like(whole), whole], axis=0))
    at = stretch * frames
    out_ref = far_refs[0]
    gram[...] = total
    out_ref[at : at + split_at, :], out_ref[at + split_at : at + frames, :] = split(
        gram[pl.ds(pl.multiple_of(core * split_at, split_at), split_at), :]
    )
    lane = lax.broadcasted_iota(jnp.int32, total.shape, 1)
    row = lax.broadcasted_iota(jnp.int32, total.shape, 0)
    on_diagonal = jnp.logical_or(lane == row, lane == row + frames)
    diagonal = jnp.sum(jnp.where(on_diagonal, total, 0.0), axis=0, keepdims=True)
    row = lax.broadcasted_iota(jnp.int32, (DIAG, 2 * frames), 0)
    out_ref[at + frames :, :] = jnp.where(row == 0, diagonal, 0.0).astype(BF16)


def rows_kernel(frames, sent, received, kept, later, out_refs, extra_refs):
    split_at = frames // 2
    data = kept[0].shape[0]
    for out_ref, kept_ref, received_ref in zip(out_refs, kept, received):
        for j in range(data // frames):
            at = rows(j, frames)
            out_ref[at, :] = (kept_ref[at, :] + received_ref[at, :].astype(F32)).astype(BF16)
    if later:
        extra_refs[0][...] = later[0][...]
    else:
        pair = (sent, received[0])
        high, low = slice(data, data + split_at), slice(data + split_at, data + frames)
        value = sum_rows(pair, high) + sum_rows(pair, low)
        block = jnp.concatenate(split(value), axis=0)
        tile = sum_rows(pair, slice(data + frames, data + frames + DIAG)).astype(BF16)
        extra_refs[0][...] = value
        extra_refs[1][...] = tile
        for out_ref in out_refs:
            out_ref[data : data + frames, :] = block
            out_ref[data + frames :, :] = tile


def fill_gram(gram, own, received, data, frames):
    split_at = frames // 2
    core = lax.rem(lax.axis_index("col"), 2)
    for ref, side in ((own, core), (received, 1 - core)):
        at = pl.ds(pl.multiple_of(side * split_at, split_at), split_at)
        gram[at, :] = ref[data : data + split_at, :].astype(F32) + ref[data + split_at :, :].astype(
            F32
        )


def second_gram_kernel(data, own, received, out_ref, gram):
    frames = out_ref.shape[0]
    fill_gram(gram, own, received, data, frames)
    whole = jnp.concatenate(
        [ref[rows(j, frames), :] for ref in (own, received) for j in range(data // frames)], axis=1
    )
    value = gram[:, frames:] + nt_dot(whole, whole)
    out_ref[...] = jnp.concatenate(split(value), axis=1)


def second_pair_kernel(own, received, gram_ref, out_ref):
    n = own.shape[0]
    both = own[...].astype(F32) + received[...].astype(F32)
    value = both[:, :n] + both[:, n:]
    gram_ref[...] = value
    out_ref[...] = jnp.concatenate(split(value), axis=1)


def near_kernel(keep, near, sum_ref, cast_ref):
    total = keep[...] + near[...].astype(F32)
    sum_ref[...] = total
    cast_ref[...] = total.astype(BF16)


def own_sum(keep, parts, j, frames):
    at = rows(j, frames)
    return keep[at, :] + sum_rows(parts, at)


def frame_shift(diagonal, frames):
    row = 1.25 * diagonal[:, frames:] / diagonal[:, :frames]
    return jnp.sum(jnp.where(eye(frames), row, 0.0), axis=1, keepdims=True), row


def image_kernel(
    pair_sum, far, gram, tile, v_ref, prior, image_ref, next_ref, cast_ref, half_ref, diag_ref
):
    frames = v_ref.shape[0]
    split_at = frames // 2
    data = cast_ref.shape[0]
    diagonal = tile[...].astype(F32) + sum_rows(far, slice(data + frames, data + frames + DIAG))
    diag_ref[...] = diagonal
    shift, _ = frame_shift(diagonal[0:1, :], frames)
    for j in range(data // frames):
        value = v_ref[:, lanes(j)]
        image = own_sum(pair_sum, far, j, frames) + prior[:, lanes(j)] * value
        following = image - shift * value
        image_ref[:, lanes(j)] = image
        next_ref[:, lanes(j)] = following
        cast_ref[rows(j, frames), :] = following.astype(BF16)
    half_ref[...] = (
        gram[...]
        + sum_rows(far, slice(data, data + split_at))
        + sum_rows(far, slice(data + split_at, data + frames))
    )


def remainder_kernel(v_ref, prior, before, out_ref):
    frames = v_ref.shape[0]
    stretch = v_ref.shape[1] // BLOCK
    for j in range(stretch):
        out_ref[rows(j, frames), :] = split(v_ref[:, lanes(j)])[1]
    terms = [part.astype(F32) for part in split(prior[...])]
    lines = [part[:, lanes(j)] for part in terms for j in range(stretch)]
    lines.append(jnp.zeros((DIAG - len(lines), BLOCK), F32))
    out_ref[stretch * frames :, :] = jnp.concatenate(lines, axis=0).astype(BF16)


def cross_kernel(frames, own, received, high, low, diag_ref, cast_ref):
    stretch = cast_ref.shape[0] // frames
    shift, _ = frame_shift(diag_ref[0:1, :], frames)
    tile = low[stretch * frames :, :].astype(F32)
    for j in range(stretch):
        at = rows(j, frames)
        weight = tile[j : j + 1, :] + tile[stretch + j : stretch + j + 1, :]
        value = sum_rows((high, low), at)
        cast_ref[at, :] = (sum_rows((own, received), at) + (weight - shift) * value).astype(BF16)


def eliminate(matrix, right, n):
    width = matrix.shape[1] + right.shape[1]
    work = jnp.concatenate([matrix, right], axis=1)
    work = [work[rows(i, TILE), :] for i in range(n // TILE)]
    at = lax.broadcasted_iota(jnp.int32, (TILE, width), 0)

    def column(k):
        return [jnp.broadcast_to(t[:, k : k + 1], (TILE, width)) for t in work]

    def step(tiles, spread, k, pivot):
        i, s = divmod(k, TILE)
        row = tiles[i][s : s + 1, :] * pivot
        done = [t - c * row for t, c in zip(tiles, spread)]
        done[i] = jnp.where(at == s, row, done[i])
        return done

    ahead = [column(k) for k in range(AHEAD)]
    for k in range(n):
        i, s = divmod(k, TILE)
        spread = ahead.pop(0)
        pivot = 1.0 / spread[i][s : s + 1, :]
        ahead = [step(later, spread, k, pivot) for later in ahead]
        work = step(work, spread, k, pivot)
        if k + AHEAD < n:
            ahead.append(column(k + AHEAD))
    return jnp.concatenate(work, axis=0)[:, n:]


def inverse_kernel(first, out_ref):
    n = first.shape[0]
    out_ref[...] = eliminate(first[:, n:], jnp.where(eye(n), 1.0, 0.0), n)


def solve_kernel(gram, parts, first, inverse_ref, norm_ref, diag_ref, out_ref):
    n = gram.shape[0]
    norm, energy = first[:, :n], first[:, n:]
    shift, shift_row = frame_shift(diag_ref[0:1, :], n)
    inverse = inverse_ref[...]
    next_rhs = energy - shift * norm
    cross = norm_ref[...] + next_rhs * shift_row
    alpha = nn_dot(inverse, norm)
    conj = nn_dot(inverse, cross.T)
    schur = gram[...] - nn_dot(cross, conj)
    for part in parts:
        both = part[...].astype(F32)
        schur += both[:, :n] + both[:, n:]
    gamma = eliminate(schur, next_rhs - nn_dot(cross, alpha), n)
    out_ref[:n, :] = alpha - nn_dot(conj, gamma)
    out_ref[n:, :] = gamma


def final_kernel(keep, far, near, v_ref, image_ref, next_ref, prior, coeffs_ref, x_ref, r_ref):
    n = v_ref.shape[0]
    coeffs = coeffs_ref[...]
    for j in range(keep.shape[0] // n):
        value = v_ref[:, lanes(j)]
        following = next_ref[:, lanes(j)]
        second_image = own_sum(keep, (near, *far), j, n) + prior[:, lanes(j)] * following
        x_ref[:, lanes(j)] = tn_dot(coeffs, jnp.concatenate([value, following], axis=0))
        r_ref[:, lanes(j)] = value - tn_dot(
            coeffs, jnp.concatenate([image_ref[:, lanes(j)], second_image], axis=0)
        )


def swapped(x, axis, flip):
    return lax.ppermute(x, axis, [(i, i ^ flip) for i in range(lax.axis_size(axis))])


def others(x, axis):
    return (x, *(swapped(x, axis, flip) for flip in range(2, lax.axis_size(axis), 2)))


def gather(x, axis):
    return tuple(part for own in others(x, axis) for part in (own, swapped(own, axis, 1)))


def shards(right_side, prior, blocks, block_row, block_col):
    frames, pix = right_side.shape
    stretch = pix // BLOCK
    n_rows, n_cols = lax.axis_size("row"), lax.axis_size("col")
    row_span, col_span = stretch * n_cols, stretch * n_rows
    prior = prior.reshape(1, pix)
    stored = blocks.shape[0]
    half_cols = n_cols // 2 * stretch * frames

    def shape(dims, dtype=F32):
        return jax.ShapeDtypeStruct(dims, dtype)

    own = shape((frames, pix))
    gram_type = shape((frames, 2 * frames))
    cast_type = shape((stretch * frames, BLOCK), BF16)
    aside = pl.CostEstimate(flops=2 * 10**9, bytes_accessed=8 * 10**6, transcendentals=0)

    pairs = n_rows // 2 - 1

    def forward(search, gram, half):
        size = half_cols + frames + (frames // 2 if half else 0)
        keep, send = call(
            lambda *refs: forward_kernel(stretch, n_cols, *refs),
            (shape((size, BLOCK)),) * 2,
            (index, search, turned, gram, half),
            [
                pltpu.VMEM((row_span, frames, BLOCK), F32),
                pltpu.VMEM((col_span, frames, BLOCK), BF16),
            ],
        )
        received = swapped(send, "col", 1)
        pair, first = call(
            lambda *refs: pair_kernel(frames, *refs),
            (shape((half_cols + frames, BLOCK), BF16), (gram_type,) if half else ()),
            (keep, received),
        )
        if half:
            aside_of_chips = call(inverse_kernel, (shape((frames, frames)),), first, cost=aside)
        elif n_rows == 4:
            (remainder,) = call(
                remainder_kernel,
                (shape((stretch * frames + DIAG, BLOCK), BF16),),
                (right_side, prior, pair),
            )
            aside_of_chips = [swapped(remainder, "row", 2)]
        else:
            aside_of_chips = []
        (foot,) = call(
            lambda *refs: chips_kernel(frames, *refs),
            (shape((half_cols + frames, BLOCK), BF16),),
            (others(pair, "col"), aside_of_chips),
        )
        return (foot, swapped(foot, "col", 1)), (*first, *aside_of_chips)

    def backward(foot, last):
        size = stretch * frames
        extra = 0 if last else frames + DIAG
        far, near, kept, keep, norm = call(
            lambda *refs: backward_kernel(stretch, n_cols, last, *refs),
            (
                tuple(shape((size + (0 if p else extra), BLOCK), BF16) for p in range(pairs)),
                shape((size, BLOCK), BF16),
                (shape((size, BLOCK)),) * pairs,
                shape((size, BLOCK)),
                (shape((frames, frames)),) if last else (),
            ),
            (index, *foot, blocks),
            [
                pltpu.VMEM((col_span, frames, BLOCK), F32),
                pltpu.VMEM((row_span, frames, BLOCK), BF16),
                pltpu.VMEM((frames, 2 * frames), F32),
            ],
        )
        received = tuple(swapped(x, "row", 1) for x in far)
        sums, gram = call(
            lambda *refs: rows_kernel(frames, *refs),
            (
                (shape((size + extra, BLOCK), BF16),) * pairs,
                (cast_type,)
                if last
                else (shape((frames // 2, 2 * frames)), shape((DIAG, 2 * frames), BF16)),
            ),
            (far[0], received, kept, (near,) if last else ()),
        )
        far = tuple(swapped(x, "row", 2 * (p + 1)) for p, x in enumerate(sums))
        near = swapped(gram[0] if last else near, "row", 1)
        if last:
            return (keep, far, near), norm
        return (keep, near, far, *gram), sums

    (cast,) = call(cast_kernel, (cast_type,), (right_side,))
    search = gather(cast, "row")
    index, turned = call(
        lambda *refs: turn_kernel(row_span, stretch, *refs),
        (shape((2, stored), jnp.int32), shape(blocks.shape, BF16)),
        (block_row, block_col, blocks),
        cost=aside,
    )
    (gram,) = call(gram_kernel, (gram_type,), (right_side, prior), cost=aside)
    foot, remainder = forward(search, gram, ())
    (keep, near, far, gram, tile), sums = backward(foot, False)
    pair_sum, pair_cast = call(
        near_kernel, (shape((stretch * frames, BLOCK)), cast_type), (keep, near)
    )
    image, following, cast, half, diagonal = call(
        image_kernel,
        (own, own, cast_type, shape((frames // 2, 2 * frames)), shape((DIAG, 2 * frames))),
        (pair_sum, far, gram, tile, right_side, prior),
    )
    if n_rows == 4:
        (cross,) = call(
            lambda *refs: cross_kernel(frames, *refs),
            (cast_type,),
            (
                sums[0],
                swapped(pair_cast, "row", 2),
                search[2],
                *remainder,
                diagonal,
            ),
        )
        search = (cast, swapped(cast, "row", 1), cross, swapped(cross, "row", 1))
    else:
        search = gather(cast, "row")
    (gram,) = call(gram_kernel, (gram_type,), (following, prior), cost=aside)
    foot, (first, inverse) = forward(search, gram, (half,))
    (second,) = call(
        lambda *refs: second_gram_kernel(half_cols, *refs),
        (shape((frames, 2 * frames), BF16),),
        foot,
        [pltpu.VMEM((frames, 2 * frames), F32)],
    )
    gram, second = call(
        second_pair_kernel,
        (shape((frames, frames)), shape((frames, 2 * frames), BF16)),
        (second, swapped(second, "row", 1)),
        cost=aside,
    )
    second = others(second, "row")[1:]
    parts, (norm,) = backward(foot, True)
    (coeffs,) = call(
        solve_kernel,
        (shape((2 * frames, frames)),),
        (gram, second, first, inverse, norm, diagonal),
        cost=aside,
    )
    return tuple(
        call(
            final_kernel,
            (own, own),
            (*parts, right_side, image, following, prior, coeffs),
        )
    )


def solution(mesh):
    return jax.shard_map(
        shards,
        mesh=mesh,
        in_specs=(
            P("groups", ("row", "col")),
            P(("row", "col")),
            P(("row", "col"), None, None),
            P(("row", "col")),
            P(("row", "col")),
        ),
        out_specs=(P("groups", ("row", "col")), P("groups", ("row", "col"))),
        check_vma=False,
    )
```
